128 devices in a mesh: gx: 4 (over x), gy: 4 (over z), gz: 8 (over y, core).
Axes of the slice: x: 4, y: 4, z: 4, core: 2. Of those that a mesh axis runs over, the one named last changes fastest.
Arguments:
- block: float32 [4, 128, 256, 512], P(None, 'gz', 'gy', 'gx'), may hold values from -40 to 40, as said below
- kappa: float32 [128, 256, 512], P('gz', 'gy', 'gx'), may hold values from 0.5 to 2
Outputs:
- ortho_block: float32 [4, 128, 256, 512], P(None, 'gz', 'gy', 'gx')
- triangle: float32 [20, 20], replicated
The draws below stay inside these ranges and needn't reach their ends.
Inputs may be any that keep to these rules, and one draw needn't show every extreme that they name: `block`: real values.
All inputs are finite; a program needn't handle non-finite values.
Results may differ from the reference program's by a relative error of at most 0.0003.
Values sent between devices are 32-bit elements; how exact they have to be, the bound alone decides.
No kernel may reach another device: no remote copies, remote signals or barrier semaphores. Data moves between devices by JAX's collectives and lax.ppermute only.
A program may use at most 128 MiB of HBM per device.

```python
import math
import jax
import jax.numpy as jnp
from jax import lax

COLS = 4
BASIS = 4
KRYLOV = 20
NX = 512
NY = 256
NZ = 128


def draw_block(key, part):
    key_noise, key_cols = jax.random.split(key, 2)
    zpos = (jnp.arange(NZ, dtype=jnp.float32)[:, None, None] + 0.5) / NZ
    ypos = (jnp.arange(NY, dtype=jnp.float32)[None, :, None] + 0.5) / NY
    xpos = (jnp.arange(NX, dtype=jnp.float32)[None, None, :] + 0.5) / NX
    ramp = (zpos + ypos + xpos) / 3.0
    cell_amp = 10.0 ** (ramp - 0.5)
    col_amp = 0.3 * 10.0 ** jax.random.uniform(key_cols, (COLS, 1, 1, 1), dtype=jnp.float32)
    raw = jnp.clip(jax.random.normal(key_noise, (COLS, NZ, NY, NX), dtype=jnp.float32), -4.0, 4.0)
    return (raw * cell_amp[None] * col_amp).astype(jnp.float32)


def shard_levels(key, dims, pieces, low, high):
    factor_of, own = 1.0, jax.random.fold_in(key, 6)
    for axis_at, blocks in pieces:
        heights = jnp.exp(jax.random.uniform(jax.random.fold_in(own, axis_at), (blocks,), jnp.float32, low / len(pieces), high / len(pieces)))
        factor_of = factor_of * jnp.repeat(heights, dims[axis_at] // blocks).reshape([-1 if axis == axis_at else 1 for axis in range(len(dims))])
    return factor_of


def setup_inputs(seed: int = 0) -> dict:
    keys = jax.random.split(jax.random.key(seed), 3)
    return {
        "block": draw_block(jax.random.fold_in(keys[2], 71), 0),
        "kappa": jnp.clip(jnp.exp(math.log(2.0) - 1.3862944 * jax.random.uniform(keys[1], (NZ, NY, NX), jnp.float32) ** shard_levels(keys[1], (NZ, NY, NX), ((0, 8), (1, 4), (2, 4)), -0.2, 0.2)), 0.5, 2.0),
    }


basis_shift = 6.0
basis_scale = 3.0

def upper_factor(matrix):
    count = matrix.shape[0]
    positions = jnp.arange(count, dtype=jnp.int32)
    rows = []
    for k in range(count):
        target = matrix[k]
        if k > 0:
            prior = jnp.stack(rows, 0)
            target = target - lax.optimization_barrier(jnp.sum(prior[:, k][:, None] * prior, 0))
        pivot = jnp.sqrt(target[k])
        row = jnp.where(positions == k, pivot, target / pivot)
        row = jnp.where(positions >= k, row, jnp.zeros_like(row))
        rows.append(row)
    return jnp.stack(rows, 0)

def upper_inverse(upper):
    count = upper.shape[0]
    positions = jnp.arange(count, dtype=jnp.int32)
    rows = [None] * count
    for i in range(count - 1, -1, -1):
        unit = (positions == i).astype(upper.dtype)
        total = unit
        for k in range(i + 1, count):
            total = total - upper[i, k] * rows[k]
        rows[i] = total / upper[i, i]
    return jnp.stack(rows, 0)

def apply_operator(field, kappa):
    padded = jnp.pad(field, ((0, 0), (1, 1), (1, 1), (1, 1)))
    kpad = jnp.pad(kappa, 1)
    centre = padded[:, 1:-1, 1:-1, 1:-1]
    kcentre = kpad[1:-1, 1:-1, 1:-1]
    offsets = [(2, 1, 1), (0, 1, 1), (1, 2, 1), (1, 0, 1), (1, 1, 2), (1, 1, 0)]
    nz, ny, nx = kappa.shape
    total = jnp.zeros_like(field)
    for oz, oy, ox in offsets:
        near = padded[:, oz:oz + nz, oy:oy + ny, ox:ox + nx]
        knear = kpad[oz:oz + nz, oy:oy + ny, ox:ox + nx]
        total = total + (0.5 * (kcentre + knear))[None] * (centre - near)
    return total

def reference(block, kappa):
    blocks = [block]
    current = block
    for step in range(BASIS):
        current = (apply_operator(current, kappa) - basis_shift * current) / basis_scale
        blocks.append(current)
    basis = jnp.concatenate(blocks, 0).reshape(KRYLOV, -1)
    gram = jnp.dot(basis, basis.T, precision=lax.Precision.HIGHEST)
    ncells = float(NX * NY * NZ)
    triangle = upper_factor(gram / ncells)
    inverse = upper_inverse(triangle[:COLS, :COLS])
    ortho_block = jnp.einsum('ij,izyx->jzyx', inverse, block, precision=lax.Precision.HIGHEST)
    return (ortho_block, triangle)
```

```python
import jax
import jax.numpy as jnp
from jax import lax
from jax.experimental import pallas as pl
from jax.experimental.pallas import tpu as pltpu
from jax.sharding import PartitionSpec as P

COLS = 4
BASIS = 4
KRYLOV = 20
MOMENTS = 2 * BASIS + 1
PAIRS = COLS * (COLS + 1) // 2
DEEP = BASIS

basis_shift = 6.0
basis_scale = 3.0

F32 = jnp.float32
VMEM = pl.BlockSpec(memory_space=pltpu.VMEM)
PARAMS = pltpu.CompilerParams(vmem_limit_bytes=48 * 1024 * 1024)


def lanes(rows):
    return lax.broadcasted_iota(jnp.int32, (rows, 128), 1)


def sublanes(rows):
    return lax.broadcasted_iota(jnp.int32, (rows, 128), 0)


def permute_lanes(value, index):
    return jnp.take_along_axis(value, index, axis=1, mode="promise_in_bounds")


def even_first(axis, first, second):
    return jnp.where(lax.axis_index(axis) % 2 == 0, first, second)


def sides(axis, first, second):
    at = lax.axis_index(axis)
    upper = jnp.where(at == lax.axis_size(axis) - 1, 0.0, even_first(axis, first, second))
    lower = jnp.where(at == 0, 0.0, even_first(axis, second, first))
    return upper, lower


def swap(first, second, axis):
    peers = lax.axis_size(axis)
    other = [(i, (i - 1 if i % 2 == 0 else i + 1) % peers) for i in range(peers)]
    second = lax.ppermute(second, axis, other)
    first = lax.ppermute(first, axis, [(i, i ^ 1) for i in range(peers)])
    return first, second


def pack_x_kernel(block, kappa, own, to_first, to_second):
    lane = lanes(64)
    offset, group = lane % 16, lane // 16
    keep = (offset < 4) | (offset >= 12)
    index = jnp.where(offset < 4, 124 + offset, jnp.where(offset >= 12, offset - 12, 0))

    def body(quad, carry):
        upper = jnp.zeros((64, 128), F32)
        lower = jnp.zeros((64, 128), F32)
        for part in range(4):
            z = quad * 4 + part
            strip = jnp.zeros((64, 128), F32)
            for g in range(COLS + 1):
                plane = block[g, z] if g < COLS else kappa[z]
                strip = jnp.where(keep & (group == g), permute_lanes(plane, index), strip)
            own[z] = strip
            here = offset // 4 == part
            upper = jnp.where(here, pltpu.roll(strip, 4 * part, 1), upper)
            lower = jnp.where(here, pltpu.roll(strip, (4 * part - 12) % 128, 1), lower)
        to_first[quad] = even_first("gx", upper, lower)
        to_second[quad] = even_first("gx", lower, upper)
        return carry

    lax.fori_loop(0, own.shape[0] // 4, body, 0)


def pack_x(block, kappa):
    nz, ny, nx = kappa.shape
    return pl.pallas_call(
        pack_x_kernel,
        out_shape=[
            jax.ShapeDtypeStruct((nz, ny, nx), F32),
            jax.ShapeDtypeStruct((nz // 4, ny, nx), F32),
            jax.ShapeDtypeStruct((nz // 4, ny, nx), F32),
        ],
        in_specs=[VMEM] * 2,
        out_specs=[VMEM] * 3,
        compiler_params=PARAMS,
        name="pack_x",
    )(block, kappa)


def pack_y_kernel(own, first, second, b_low, b_high, k_low, k_high, strip, to_first, to_second):
    offset = lanes(64) % 16
    half = sublanes(8) < 4

    def body(quad, carry):
        upper, lower = sides("gx", first[quad], second[quad])
        for part in range(4):
            z = quad * 4 + part
            beyond = jnp.where(
                offset < 8,
                pltpu.roll(upper, (4 - 4 * part) % 128, 1),
                pltpu.roll(lower, (8 - 4 * part) % 128, 1),
            )
            strip[z] = jnp.where((offset < 4) | (offset >= 12), own[z], beyond)
        return carry

    lax.fori_loop(0, strip.shape[0] // 4, body, 0)

    def pairs(duo, carry):
        z = duo * 2
        for a in range(COLS + 2):
            if a < COLS:
                low = [b_low[a, z + i] for i in range(2)]
                high = [b_high[a, z + i] for i in range(2)]
            elif a == COLS:
                low = [k_low[z + i] for i in range(2)]
                high = [k_high[z + i] for i in range(2)]
            else:
                low = [strip[z + i, 0:8] for i in range(2)]
                high = [strip[z + i, 56:64] for i in range(2)]
            upper = jnp.where(half, pltpu.roll(high[0], 4, 0), high[1])
            lower = jnp.where(half, low[0], pltpu.roll(low[1], 4, 0))
            to_first[a, duo] = even_first("gy", upper, lower)
            to_second[a, duo] = even_first("gy", lower, upper)
        return carry

    lax.fori_loop(0, strip.shape[0] // 2, pairs, 0)


def pack_y(block, kappa, own, first, second):
    nz, ny, nx = kappa.shape
    whole = lambda shape: pl.BlockSpec(shape, lambda i: (0,) * len(shape))
    edge4 = lambda at: pl.BlockSpec((COLS, nz, 8, nx), lambda i: (0, 0, at, 0))
    edge = lambda at: pl.BlockSpec((nz, 8, nx), lambda i: (0, at, 0))
    faces = (COLS + 2, nz // 2, 8, nx)
    return pl.pallas_call(
        pack_y_kernel,
        grid=(1,),
        out_shape=[
            jax.ShapeDtypeStruct((nz, ny, nx), F32),
            jax.ShapeDtypeStruct(faces, F32),
            jax.ShapeDtypeStruct(faces, F32),
        ],
        in_specs=[
            whole((nz, ny, nx)),
            whole((nz // 4, ny, nx)),
            whole((nz // 4, ny, nx)),
            edge4(0),
            edge4(ny // 8 - 1),
            edge(0),
            edge(ny // 8 - 1),
        ],
        out_specs=[whole((nz, ny, nx)), whole(faces), whole(faces)],
        compiler_params=PARAMS,
        name="pack_y",
    )(own, first, second, block, block, kappa, kappa)


def pack_z_kernel(first, second, b_low, b_high, k_low, k_high, s_low, s_high, rim, to_first, to_second):
    half = sublanes(8) < 4

    def pairs(duo, carry):
        for a in range(COLS + 2):
            upper, lower = sides("gy", first[a, duo], second[a, duo])
            rim[a, duo * 2] = jnp.where(half, upper, pltpu.roll(lower, 4, 0))
            rim[a, duo * 2 + 1] = jnp.where(half, pltpu.roll(upper, 4, 0), lower)
        return carry

    lax.fori_loop(0, rim.shape[1] // 2, pairs, 0)
    last = rim.shape[1] - DEEP
    ny = b_low.shape[2]

    def slabs(z, carry):
        for a in range(COLS + 2):
            if a < COLS:
                low, high = b_low[a, z], b_high[a, z]
            elif a == COLS:
                low, high = k_low[z], k_high[z]
            else:
                low, high = s_low[z], s_high[z]
            to_first[a, z, 0:ny] = even_first("gz", high, low)
            to_second[a, z, 0:ny] = even_first("gz", low, high)
            low, high = rim[a, z], rim[a, last + z]
            to_first[a, z, ny : ny + 8] = even_first("gz", high, low)
            to_second[a, z, ny : ny + 8] = even_first("gz", low, high)
        return carry

    lax.fori_loop(0, DEEP, slabs, 0)


def pack_z(block, kappa, strip, first, second):
    nz, ny, nx = kappa.shape
    whole = lambda shape: pl.BlockSpec(shape, lambda i: (0,) * len(shape))
    edge4 = lambda at: pl.BlockSpec((COLS, DEEP, ny, nx), lambda i: (0, at, 0, 0))
    edge = lambda at: pl.BlockSpec((DEEP, ny, nx), lambda i: (at, 0, 0))
    top = nz // DEEP - 1
    faces = (COLS + 2, nz // 2, 8, nx)
    rims = (COLS + 2, nz, 8, nx)
    slabs = (COLS + 2, DEEP, ny + 8, nx)
    return pl.pallas_call(
        pack_z_kernel,
        grid=(1,),
        out_shape=[jax.ShapeDtypeStruct(s, F32) for s in (rims, slabs, slabs)],
        in_specs=[whole(faces), whole(faces), edge4(0), edge4(top), edge(0), edge(top), edge(0), edge(top)],
        out_specs=[whole(rims), whole(slabs), whole(slabs)],
        compiler_params=PARAMS,
        name="pack_z",
    )(first, second, block, block, kappa, kappa, strip, strip)


NCELLROWS = 64
TILES = NCELLROWS // 8 + 1
ROWS = 8 * (TILES + 2)


def powers_kernel(block, kappa, strip, rim, first, second, out, field, side, kfield, kside, wts, swts, acc):
    nz = block.shape[1]
    ny = block.shape[2]
    depth = nz + 2 * DEEP
    lane8 = lanes(8)
    lane = lanes(ny + 8)
    klanes = 64 + lane % 16

    def lay(put, body, edge):
        put(8, ny, body)
        put(8 + ny, 8, edge)
        put(0, 8, edge)
        put(16 + ny, 8, body[0:8])

    def lay_all(ze, get):
        for a in range(COLS + 2):
            body, edge = get(a)
            if a < COLS:
                def put(row, count, value, a=a):
                    field[0, a, ze, row : row + count] = value
            elif a == COLS:
                def put(row, count, value):
                    kfield[ze, row : row + count] = value
            else:
                def put(row, count, value):
                    side[0, ze, row : row + count] = value
                    kside[ze, row : row + count] = permute_lanes(value, klanes[0:count])
            lay(put, body, edge)

    def own_slab(z, carry):
        def get(a):
            body = block[a, z] if a < COLS else kappa[z] if a == COLS else strip[z]
            return body, rim[a, z]

        lay_all(z + DEEP, get)
        return carry

    lax.fori_loop(0, nz, own_slab, 0)

    def far_slab(z, carry):
        def get_side(which):
            def get(a):
                values = sides("gz", first[a, z], second[a, z])[which]
                return values[0:ny], values[ny : ny + 8]

            return get

        lay_all(z, get_side(1))
        lay_all(z + DEEP + nz, get_side(0))
        return carry

    lax.fori_loop(0, DEEP, far_slab, 0)

    mid = slice(8, 16 + ny)
    up = slice(9, 17 + ny)
    down = slice(7, 15 + ny)
    kedge = jnp.where(lane == 127, 64 + 4, 64 + 11)

    def weights(ze, carry):
        for k_ref, w_ref, main in ((kfield, wts, True), (kside, swts, False)):
            k = k_ref[ze, mid]
            right = pltpu.roll(k, 127, 1)
            left = pltpu.roll(k, 1, 1)
            if main:
                beyond = permute_lanes(side[0, ze, mid], kedge)
                right = jnp.where(lane == 127, beyond, right)
                left = jnp.where(lane == 0, beyond, left)
            above = k_ref[ze, up]
            below = k_ref[ze, down]
            far = k_ref[jnp.minimum(ze + 1, depth - 1), mid]
            near = k_ref[jnp.maximum(ze - 1, 0), mid]
            total = 3.0 * k + 0.5 * (right + left + above + below + far + near)
            w_ref[0, ze, mid] = (total - basis_shift) / basis_scale

            def link(other):
                return jnp.where(jnp.minimum(k, other) > 0.0, (k + other) * (0.5 / basis_scale), 0.0)

            w_ref[1, ze, mid] = link(right)
            w_ref[2, ze, mid] = link(left)
            above = link(above)
            w_ref[3, ze, mid] = above
            w_ref[3, ze, 0:8] = above[ny : ny + 8]
            w_ref[4, ze, mid] = link(far)
        return carry

    lax.fori_loop(0, depth, weights, 0)
    acc[...] = jnp.zeros_like(acc)
    pairs = [(c, d) for c in range(COLS) for d in range(c, COLS)]

    for k in range(1, BASIS + 1):
        src, dst = (k - 1) % 2, k % 2
        final = k == BASIS

        def slab(ze, carry, inner, k=k, src=src, dst=dst, final=final):
            sums = {}
            for t in range(TILES):
                at = slice(8 + 8 * t, 16 + 8 * t)
                above = slice(9 + 8 * t, 17 + 8 * t)
                below = slice(7 + 8 * t, 15 + 8 * t)
                edge = side[src, ze, at]
                if not final:
                    new = swts[0, ze, at] * edge
                    new -= swts[1, ze, at] * pltpu.roll(edge, 127, 1)
                    new -= swts[2, ze, at] * pltpu.roll(edge, 1, 1)
                    new -= swts[3, ze, at] * side[src, ze, above]
                    new -= swts[3, ze, below] * side[src, ze, below]
                    new -= swts[4, ze, at] * side[src, ze + 1, at]
                    new -= swts[4, ze - 1, at] * side[src, ze - 1, at]
                    side[dst, ze, at] = new
                    if t == 0:
                        side[dst, ze, 8 + 8 * TILES : 16 + 8 * TILES] = new
                    if t == TILES - 1:
                        side[dst, ze, 0:8] = new
                if final and t == TILES - 1:
                    continue
                olds, news = [], []
                for c in range(COLS):
                    v = field[src, c, ze, at]
                    beyond = permute_lanes(edge, jnp.where(lane8 == 127, 16 * c + 4, 16 * c + 11))
                    right = jnp.where(lane8 == 127, beyond, pltpu.roll(v, 127, 1))
                    left = jnp.where(lane8 == 0, beyond, pltpu.roll(v, 1, 1))
                    new = wts[0, ze, at] * v
                    new -= wts[1, ze, at] * right
                    new -= wts[2, ze, at] * left
                    new -= wts[3, ze, at] * field[src, c, ze, above]
                    new -= wts[3, ze, below] * field[src, c, ze, below]
                    new -= wts[4, ze, at] * field[src, c, ze + 1, at]
                    new -= wts[4, ze - 1, at] * field[src, c, ze - 1, at]
                    if not final:
                        field[dst, c, ze, at] = new
                        if t == 0:
                            field[dst, c, ze, 8 + 8 * TILES : 16 + 8 * TILES] = new
                        if t == TILES - 1:
                            field[dst, c, ze, 0:8] = new
                    olds.append(v)
                    news.append(new)
                if inner and t < TILES - 1:
                    for p, (c, d) in enumerate(pairs):
                        if k == 1:
                            sums.setdefault(p, []).append(olds[c] * olds[d])
                        sums.setdefault((2 * k - 1) * PAIRS + p, []).append(olds[c] * news[d])
                        sums.setdefault(2 * k * PAIRS + p, []).append(news[c] * news[d])
            for m, terms in sums.items():
                total = terms[0]
                for term in terms[1:]:
                    total = total + term
                acc[m] += total
            return carry

        def outer(ze, carry, slab=slab):
            return slab(ze, carry, False)

        def inner(ze, carry, slab=slab):
            return slab(ze, carry, True)

        if k < DEEP:
            lax.fori_loop(k, DEEP, outer, 0)
            lax.fori_loop(DEEP + nz, depth - k, outer, 0)
        lax.fori_loop(DEEP, DEEP + nz, inner, 0)

    rows = jnp.sum(acc[...], axis=1)
    row = lax.dot_general(
        jnp.ones((8, 128), F32),
        rows,
        (((1,), (1,)), ((), ())),
        precision=lax.Precision.HIGHEST,
        preferred_element_type=F32,
    )
    out[...] = jnp.broadcast_to(row[0:1][None], out.shape)


def powers(block, kappa, strip, rim, first, second, peers):
    nz, ny, nx = kappa.shape
    depth = nz + 2 * DEEP
    slab = (depth, ROWS, nx)
    return pl.pallas_call(
        powers_kernel,
        out_shape=jax.ShapeDtypeStruct((peers, 1, 128), F32),
        in_specs=[VMEM] * 6,
        out_specs=VMEM,
        scratch_shapes=[
            pltpu.VMEM((2, COLS) + slab, F32),
            pltpu.VMEM((2,) + slab, F32),
            pltpu.VMEM(slab, F32),
            pltpu.VMEM(slab, F32),
            pltpu.VMEM((5,) + slab, F32),
            pltpu.VMEM((5,) + slab, F32),
            pltpu.VMEM((128, 8, 128), F32),
        ],
        compiler_params=PARAMS,
        name="powers",
    )(block, kappa, strip, rim, first, second)


def finish_kernel(ncells, parts, block, ortho, triangle, coef):
    @pl.when(pl.program_id(0) == 0)
    def _():
        row = jnp.sum(parts[...], axis=0) * (1.0 / ncells)
        row = jnp.broadcast_to(row, (24, 128))
        a, b = sublanes(24), lanes(24)
        c, d = a % 4, b % 4
        low, high = jnp.minimum(c, d), jnp.maximum(c, d)
        pair = low * 4 - (low * (low - 1)) // 2 + high - low
        inside = (a < KRYLOV) & (b < KRYLOV)
        index = jnp.where(inside, (a // 4 + b // 4) * PAIRS + pair, 127)
        matrix = permute_lanes(row, index)
        lane = lanes(1)
        uppers = []
        for k in range(KRYLOV):
            line = matrix[k : k + 1, :]
            pivot = line[:, k : k + 1]
            upper = jnp.where(lane >= k, line / jnp.sqrt(pivot), 0.0)
            uppers.append(upper)
            triangle[k : k + 1, :] = upper[:, 0:KRYLOV]
            if k + 1 < KRYLOV:
                matrix = matrix - matrix[:, k : k + 1] * (line / pivot)
        at = 0
        for i in range(COLS):
            for j in range(i, COLS):
                value = uppers[i][:, j : j + 1]
                value = 1.0 / value if i == j else value
                coef[at] = jnp.broadcast_to(value, (8, 128))
                at += 1

    u = {}
    at = 0
    for i in range(COLS):
        for j in range(i, COLS):
            u[i, j] = coef[at]
            at += 1

    def slab(z, carry):
        for t in range(ortho.shape[2] // 8):
            rows = slice(8 * t, 8 * t + 8)
            done = []
            for j in range(COLS):
                value = block[j, z, rows]
                for i in range(j):
                    value = value - u[i, j] * done[i]
                value = value * u[j, j]
                ortho[j, z, rows] = value
                done.append(value)
        return carry

    lax.fori_loop(0, ortho.shape[1], slab, 0)


def finish(parts, block, ncells):
    cols, nz, ny, nx = block.shape
    steps = 4
    piece = pl.BlockSpec((cols, nz // steps, ny, nx), lambda i: (0, i, 0, 0))
    return pl.pallas_call(
        lambda *refs: finish_kernel(ncells, *refs),
        grid=(steps,),
        out_shape=[
            jax.ShapeDtypeStruct(block.shape, F32),
            jax.ShapeDtypeStruct((KRYLOV, KRYLOV), F32),
        ],
        in_specs=[pl.BlockSpec(parts.shape, lambda i: (0, 0, 0)), piece],
        out_specs=[piece, pl.BlockSpec((KRYLOV, KRYLOV), lambda i: (0, 0))],
        scratch_shapes=[pltpu.VMEM((PAIRS, 8, 128), F32)],
        compiler_params=PARAMS,
        name="finish",
    )(parts, block)


def shards(block, kappa):
    axes = ("gx", "gy", "gz")
    peers = lax.axis_size(axes)
    ncells = float(kappa.size * peers)
    own, first, second = pack_x(block, kappa)
    first, second = swap(first, second, "gx")
    strip, first, second = pack_y(block, kappa, own, first, second)
    first, second = swap(first, second, "gy")
    rim, first, second = pack_z(block, kappa, strip, first, second)
    first, second = swap(first, second, "gz")
    moments = powers(block, kappa, strip, rim, first, second, peers)
    parts = lax.all_to_all(moments, axes, 0, 0, tiled=True)
    return tuple(finish(parts, block, ncells))


def solution(mesh):
    return jax.shard_map(
        shards,
        mesh=mesh,
        in_specs=(P(None, "gz", "gy", "gx"), P("gz", "gy", "gx")),
        out_specs=(P(None, "gz", "gy", "gx"), P()),
        check_vma=False,
    )
```

```python
import jax
import jax.numpy as jnp
from jax import lax
from jax.experimental import pallas as pl
from jax.experimental.pallas import tpu as pltpu
from jax.sharding import PartitionSpec as P

COLS = 4
BASIS = 4
KRYLOV = 20
MOMENTS = 2 * BASIS + 1
PAIRS = [(c, d) for c in range(COLS) for d in range(c, COLS)]
NPAIRS = len(PAIRS)
DEEP = BASIS
ARRAYS = COLS + 1
PITCH = 6 * DEEP
SLABS = 5

basis_shift = 6.0
basis_scale = 3.0

F32 = jnp.float32
VMEM = pl.BlockSpec(memory_space=pltpu.VMEM)
HBM = pl.BlockSpec(memory_space=pltpu.HBM)


def params(mib):
    return pltpu.CompilerParams(vmem_limit_bytes=mib * 1024 * 1024)


def cost(flops):
    return pl.CostEstimate(flops=flops, bytes_accessed=1 << 20, transcendentals=0)


def lanes(rows):
    return lax.broadcasted_iota(jnp.int32, (rows, 128), 1)


def sublanes(rows):
    return lax.broadcasted_iota(jnp.int32, (rows, 128), 0)


def permute_lanes(value, index):
    return jnp.take_along_axis(value, index, axis=1, mode="promise_in_bounds")


def even_first(axis, first, second):
    return jnp.where(lax.axis_index(axis) % 2 == 0, first, second)


def sides(axis, first, second):
    at = lax.axis_index(axis)
    upper = jnp.where(at == lax.axis_size(axis) - 1, 0.0, even_first(axis, first, second))
    lower = jnp.where(at == 0, 0.0, even_first(axis, second, first))
    return upper, lower


def swap(first, second, axis):
    peers = lax.axis_size(axis)
    other = [(i, (i - 1 if i % 2 == 0 else i + 1) % peers) for i in range(peers)]
    second = lax.ppermute(second, axis, other)
    first = lax.ppermute(first, axis, [(i, i ^ 1) for i in range(peers)])
    return first, second


def link(one, other, bounded):
    weight = (one + other) * (0.5 / basis_scale)
    if bounded:
        weight = jnp.where(jnp.minimum(one, other) > 0.0, weight, 0.0)
    return weight


def centre(k, others):
    total = 6.0 * k
    for other in others:
        total = total + other
    return total * (0.5 / basis_scale) - basis_shift / basis_scale


def rows_above(ref, index, t, tiles, value):
    if t == tiles - 1:
        return pltpu.roll(value, 7, 0)
    return ref[index + (slice(8 * t + 1, 8 * t + 9),)]


def rows_below(ref, index, t, value):
    if t == 0:
        return pltpu.roll(value, 1, 0)
    return ref[index + (slice(8 * t - 1, 8 * t + 7),)]


def tile(t):
    return slice(8 * t, 8 * t + 8)


class Sums:
    def __init__(self):
        self.held = {}

    def add(self, at, term):
        self.held[at] = self.held[at] + term if at in self.held else term

    def products(self, k, olds, news):
        for p, (c, d) in enumerate(PAIRS):
            if k == 1:
                self.add(p, olds[c] * olds[d])
            self.add((2 * k - 1) * NPAIRS + p, olds[c] * news[d])
            self.add(2 * k * NPAIRS + p, news[c] * news[d])

    def flush(self, acc):
        for at, total in self.held.items():
            acc[at] += total


def apply(v, above, below, far, near, w):
    new = w[0] * v
    new -= w[1] * pltpu.roll(v, 127, 1)
    new -= w[2] * pltpu.roll(v, 1, 1)
    new -= w[3] * above
    new -= w[4] * below
    new -= w[5] * far
    new -= w[6] * near
    return new


def tile_weights(w, q, wz, far, near, t):
    c0, right, left, above = (w[i, q, tile(t)] for i in range(4))
    below = rows_below(w, (3, q), t, above)
    return c0, right, left, above, below, wz[far, tile(t)], wz[near, tile(t)]


def pack_z_kernel(block, kappa, to_first, to_second, sems):
    nz = kappa.shape[0]
    high = nz - DEEP
    even = lax.axis_index("gz") % 2 == 0
    copies = []
    for i, (out, at) in enumerate(
        ((to_second, jnp.where(even, 0, high)), (to_first, jnp.where(even, high, 0)))
    ):
        copies.append(pltpu.make_async_copy(block.at[:, pl.ds(at, DEEP)], out.at[0:COLS], sems.at[2 * i]))
        copies.append(pltpu.make_async_copy(kappa.at[pl.ds(at, DEEP)], out.at[COLS], sems.at[2 * i + 1]))
    for copy in copies:
        copy.start()
    for copy in copies:
        copy.wait()


def pack_z(block, kappa):
    nz, ny, nx = kappa.shape
    face = jax.ShapeDtypeStruct((ARRAYS, DEEP, ny, nx), F32)
    return pl.pallas_call(
        pack_z_kernel,
        out_shape=[face, face],
        in_specs=[HBM, HBM],
        out_specs=[VMEM] * 2,
        scratch_shapes=[pltpu.SemaphoreType.DMA((4,))],
        compiler_params=params(8),
        name="pack_z",
    )(block, kappa)


def inner_kernel(block, kappa, acc, edge, p1, p2, p3, w, wz):
    nz, ny, _ = kappa.shape
    tiles = ny // 8
    half = sublanes(8) < 4
    acc[...] = jnp.zeros_like(acc)

    def weights(z, carry):
        for t in range(tiles):
            k = kappa[z, tile(t)]
            right, left = pltpu.roll(k, 127, 1), pltpu.roll(k, 1, 1)
            above = rows_above(kappa, (z,), t, tiles, k)
            below = rows_below(kappa, (z,), t, k)
            far = kappa[z + 1, tile(t)]
            near = kappa[jnp.maximum(z - 1, 0), tile(t)]
            w[0, z, tile(t)] = centre(k, (right, left, above, below, far, near))
            w[1, z, tile(t)] = link(k, right, False)
            w[2, z, tile(t)] = link(k, left, False)
            w[3, z, tile(t)] = link(k, above, False)
            wz[z, tile(t)] = link(k, far, False)
        return carry

    lax.fori_loop(0, nz - 1, weights, 0, unroll=3)
    fields = (block, p1, p2, p3, None)
    for k in range(1, BASIS + 1):
        src, dst = fields[k - 1], fields[k]

        def slab(z, carry, k=k, src=src, dst=dst):
            sums = Sums()

            def step(t):
                ws = tile_weights(w, z, wz, z, z - 1, t)
                olds, news = [], []
                for c in range(COLS):
                    v = src[c, z, tile(t)]
                    above = rows_above(src, (c, z), t, tiles, v)
                    below = rows_below(src, (c, z), t, v)
                    news.append(apply(v, above, below, src[c, z + 1, tile(t)], src[c, z - 1, tile(t)], ws))
                    olds.append(v)
                if dst is not None:
                    for c in range(COLS):
                        dst[c, z, tile(t)] = news[c]
                return olds, news

            first, last = step(0), step(tiles - 1)
            olds, news = (
                [jnp.where(half, b, a) for a, b in zip(first[i], last[i])] for i in range(2)
            )
            sums.products(k, olds, news)
            for t in range(1, tiles - 1):
                sums.products(k, *step(t))
            sums.flush(acc)
            return carry

        lax.fori_loop(k, nz - k, slab, 0, unroll=2)
        if dst is not None:
            for i in range(2):
                edge[k - 1, 0, i] = dst[:, k + i]
                edge[k - 1, 1, i] = dst[:, nz - 1 - k - i]


def inner(block, kappa):
    nz, ny, nx = kappa.shape
    return pl.pallas_call(
        inner_kernel,
        out_shape=[
            jax.ShapeDtypeStruct((MOMENTS * NPAIRS, 8, nx), F32),
            jax.ShapeDtypeStruct((BASIS - 1, 2, 2, COLS, ny, nx), F32),
        ],
        in_specs=[VMEM] * 2,
        out_specs=[VMEM] * 2,
        scratch_shapes=[pltpu.VMEM(block.shape, F32)] * 3
        + [pltpu.VMEM((4, nz, ny, nx), F32), pltpu.VMEM((nz, ny, nx), F32)],
        compiler_params=params(24),
        cost_estimate=cost(1 << 28),
        name="inner",
    )(block, kappa)


def pack_y_kernel(
    b_low, b_high, k_low, k_high, f_low, f_high, s_low, s_high, after, edges, to_first, to_second
):
    nz = k_low.shape[0]

    def own(z, carry):
        for a in range(ARRAYS):
            edges[a, z + DEEP, 0] = b_low[a, z] if a < COLS else k_low[z]
            edges[a, z + DEEP, 1] = b_high[a, z] if a < COLS else k_high[z]
        return carry

    lax.fori_loop(0, nz, own, 0, unroll=4)

    def far(i, carry):
        for a in range(ARRAYS):
            for at, (one, other) in enumerate(((f_low, s_low), (f_high, s_high))):
                upper, lower = sides("gz", one[a, i], other[a, i])
                edges[a, i, at] = lower
                edges[a, nz + DEEP + i, at] = upper
        return carry

    lax.fori_loop(0, DEEP, far, 0, unroll=2)
    half = sublanes(8) < 4

    def pairs(duo, carry):
        z = duo * 2
        for a in range(ARRAYS):
            upper = jnp.where(half, pltpu.roll(edges[a, z, 1], 4, 0), edges[a, z + 1, 1])
            lower = jnp.where(half, edges[a, z, 0], pltpu.roll(edges[a, z + 1, 0], 4, 0))
            to_first[a, duo] = even_first("gy", upper, lower)
            to_second[a, duo] = even_first("gy", lower, upper)
        return carry

    lax.fori_loop(0, to_first.shape[1], pairs, 0, unroll=4)


def pack_y(block, kappa, first, second, after):
    nz, ny, nx = kappa.shape
    depth = nz + 2 * DEEP
    last = ny // 8 - 1
    whole = lambda shape: pl.BlockSpec(shape, lambda i: (0,) * len(shape))
    b_edge = lambda at: pl.BlockSpec((COLS, nz, 8, nx), lambda i: (0, 0, at, 0))
    k_edge = lambda at: pl.BlockSpec((nz, 8, nx), lambda i: (0, at, 0))
    f_edge = lambda at: pl.BlockSpec((ARRAYS, DEEP, 8, nx), lambda i: (0, 0, at, 0))
    edges = (ARRAYS, depth, 2, 8, nx)
    face = (ARRAYS, depth // 2, 8, nx)
    return pl.pallas_call(
        pack_y_kernel,
        grid=(1,),
        out_shape=[jax.ShapeDtypeStruct(s, F32) for s in (edges, face, face)],
        in_specs=[f(at) for f in (b_edge, k_edge, f_edge, f_edge) for at in (0, last)]
        + [pl.BlockSpec(memory_space=pl.ANY)],
        out_specs=[whole(edges), whole(face), whole(face)],
        compiler_params=params(16),
        name="pack_y",
    )(block, block, kappa, kappa, first, first, second, second, after)


def outer_kernel(block, kappa, edge, first, second, acc, f0, f1, f2, f3, kz, w, wz):
    nz, ny, _ = kappa.shape
    tiles = ny // 8
    half = sublanes(8) < 4
    acc[...] = jnp.zeros_like(acc)

    def far(i, carry):
        for a in range(ARRAYS):
            upper, lower = sides("gz", first[a, i], second[a, i])
            if a < COLS:
                f0[0, a, i] = lower
                f0[1, a, DEEP - 1 - i] = upper
            else:
                kz[0, i] = lower
                kz[1, DEEP - 1 - i] = upper
        return carry

    lax.fori_loop(0, DEEP, far, 0)
    for i in range(2):
        for c in range(COLS):
            f0[0, c, DEEP + i] = block[c, i]
            f0[1, c, DEEP + i] = block[c, nz - 1 - i]
            for k, f in enumerate((f1, f2, f3)):
                for side in range(2):
                    f[side, c, DEEP + i] = edge[k, side, i, c]
    for i in range(DEEP + 1):
        kz[0, DEEP + i] = kappa[i]
        kz[1, DEEP + i] = kappa[nz - 1 - i]

    def weights(at, carry):
        side, e = at // 8, at % 8
        for t in range(tiles):
            k = kz[side, e, tile(t)]
            right, left = pltpu.roll(k, 127, 1), pltpu.roll(k, 1, 1)
            above = rows_above(kz, (side, e), t, tiles, k)
            below = rows_below(kz, (side, e), t, k)
            far = kz[side, e + 1, tile(t)]
            near = kz[side, jnp.maximum(e - 1, 0), tile(t)]
            w[0, at, tile(t)] = centre(k, (right, left, above, below, far, near))
            w[1, at, tile(t)] = link(k, right, False)
            w[2, at, tile(t)] = link(k, left, False)
            w[3, at, tile(t)] = link(k, above, False)
            wz[at, tile(t)] = link(k, far, True)
        return carry

    lax.fori_loop(0, 16, weights, 0, unroll=2)
    fields = (f0, f1, f2, f3, None)
    for k in range(1, BASIS + 1):
        src, dst = fields[k - 1], fields[k]

        def both(side, carry, k=k, src=src, dst=dst):
            for j in range(DEEP):
                own = j >= DEEP - k
                sums = Sums()

                def step(t):
                    at = side * 8 + j + k
                    ws = tile_weights(w, at, wz, at, at - 1, t)
                    olds, news = [], []
                    for c in range(COLS):
                        v = src[side, c, j + 1, tile(t)]
                        above = rows_above(src, (side, c, j + 1), t, tiles, v)
                        below = rows_below(src, (side, c, j + 1), t, v)
                        far, near = src[side, c, j + 2, tile(t)], src[side, c, j, tile(t)]
                        news.append(apply(v, above, below, far, near, ws))
                        olds.append(v)
                    if dst is not None:
                        for c in range(COLS):
                            dst[side, c, j, tile(t)] = news[c]
                    return olds, news

                first, last = step(0), step(tiles - 1)
                if own:
                    olds, news = (
                        [jnp.where(half, b, a) for a, b in zip(first[i], last[i])] for i in range(2)
                    )
                    sums.products(k, olds, news)
                for t in range(1, tiles - 1):
                    pair = step(t)
                    if own:
                        sums.products(k, *pair)
                sums.flush(acc)
            return carry

        lax.fori_loop(0, 2, both, 0)


def outer(block, kappa, edge, first, second):
    nz, ny, nx = kappa.shape
    return pl.pallas_call(
        outer_kernel,
        out_shape=jax.ShapeDtypeStruct((MOMENTS * NPAIRS, 8, nx), F32),
        in_specs=[VMEM] * 5,
        out_specs=VMEM,
        scratch_shapes=[pltpu.VMEM((2, COLS, DEEP + 2, ny, nx), F32)] * 4
        + [
            pltpu.VMEM((2, 2 * DEEP + 1, ny, nx), F32),
            pltpu.VMEM((4, 16, ny, nx), F32),
            pltpu.VMEM((16, ny, nx), F32),
        ],
        compiler_params=params(24),
        cost_estimate=cost(1 << 27),
        name="outer",
    )(block, kappa, edge, first, second)


def strip_of(planes):
    lane = lanes(8)
    offset, group = lane % PITCH, lane // PITCH
    index = jnp.where(offset < 8, 120 + offset, jnp.maximum(offset - 16, 0))
    strip = jnp.zeros((8, 128), F32)
    for g, plane in enumerate(planes):
        strip = jnp.where(group == g, permute_lanes(plane, index), strip)
    return strip


def strips_kernel(block, kappa, first, second, strip):
    nz, ny, _ = kappa.shape

    def rows(t, carry):
        at = pl.ds(pl.multiple_of(t * 8, 8), 8)
        for a in range(ARRAYS):
            ends = [sides("gz", first[a, i, at], second[a, i, at]) for i in range(DEEP)]

            def plane(z):
                if z < DEEP:
                    return ends[z][1]
                if z >= nz + DEEP:
                    return ends[z - nz - DEEP][0]
                return block[a, z - DEEP, at] if a < COLS else kappa[z - DEEP, at]

            for q in range(SLABS):
                strip[a, q, at] = strip_of([plane(z) for z in range(q, nz + 2 * DEEP, SLABS)])
        return carry

    lax.fori_loop(0, ny // 8, rows, 0)


def strips(block, kappa, first, second):
    nz, ny, nx = kappa.shape
    return pl.pallas_call(
        strips_kernel,
        out_shape=jax.ShapeDtypeStruct((ARRAYS, SLABS, ny, nx), F32),
        in_specs=[VMEM] * 4,
        out_specs=VMEM,
        compiler_params=params(16),
        cost_estimate=cost(1 << 25),
        name="strips",
    )(block, kappa, first, second)


def pack_x_kernel(first, second, strip, after, rim, side, to_first, to_second):
    half = sublanes(8) < 4
    depth, tiles = rim.shape[1], to_first.shape[1] // 8

    def duos(duo, carry):
        for a in range(ARRAYS):
            upper, lower = sides("gy", first[a, duo], second[a, duo])
            rim[a, duo * 2] = jnp.where(half, upper, pltpu.roll(lower, 4, 0))
            rim[a, duo * 2 + 1] = jnp.where(half, pltpu.roll(upper, 4, 0), lower)
        return carry

    lax.fori_loop(0, depth // 2, duos, 0, unroll=4)
    slot = lanes(8) % PITCH // DEEP

    def arrays(a, carry):
        for q in range(SLABS):
            side[a, q] = strip_of([rim[a, z] for z in range(q, depth, SLABS)])
        for t in range(tiles):
            upper = jnp.zeros((8, 128), F32)
            lower = jnp.zeros((8, 128), F32)
            for q in range(SLABS):
                value = strip[a, q, tile(t)] if t < tiles - 1 else side[a, q]
                upper = jnp.where(slot == q, pltpu.roll(value, (4 * q - 4) % 128, 1), upper)
                lower = jnp.where(slot == q, pltpu.roll(value, (4 * q - 16) % 128, 1), lower)
            to_first[a, tile(t)] = even_first("gx", upper, lower)
            to_second[a, tile(t)] = even_first("gx", lower, upper)
        return carry

    lax.fori_loop(0, ARRAYS, arrays, 0)


def pack_x(first, second, strip, after):
    _, _, ny, nx = strip.shape
    depth = first.shape[1] * 2
    face = (ARRAYS, ny + 8, nx)
    return pl.pallas_call(
        pack_x_kernel,
        out_shape=[
            jax.ShapeDtypeStruct(s, F32)
            for s in ((ARRAYS, depth, 8, nx), (ARRAYS, SLABS, 8, nx), face, face)
        ],
        in_specs=[VMEM] * 3 + [pl.BlockSpec(memory_space=pl.ANY)],
        out_specs=[VMEM] * 4,
        compiler_params=params(16),
        name="pack_x",
    )(first, second, strip, after)


def y_strip_kernel(edges, rim, acc, g0, g1, g2, g3, kr, w, wz):
    depth = rim.shape[1]
    half = sublanes(8) < 4
    acc[...] = jnp.zeros_like(acc)

    def fill(z, carry):
        for a in range(ARRAYS):
            parts = (edges[a, z, 1], rim[a, z], edges[a, z, 0])
            for t, part in enumerate(parts):
                if a < COLS:
                    g0[a, z, tile(t)] = part
                else:
                    kr[z, tile(t)] = part
        return carry

    lax.fori_loop(0, depth, fill, 0, unroll=4)

    def weights(z, carry):
        for t in range(3):
            k = kr[z, tile(t)]
            right, left = pltpu.roll(k, 127, 1), pltpu.roll(k, 1, 1)
            above = rows_above(kr, (z,), t, 3, k)
            below = rows_below(kr, (z,), t, k)
            far = kr[z + 1, tile(t)]
            near = kr[jnp.maximum(z - 1, 0), tile(t)]
            w[0, z, tile(t)] = centre(k, (right, left, above, below, far, near))
            w[1, z, tile(t)] = link(k, right, False)
            w[2, z, tile(t)] = link(k, left, False)
            w[3, z, tile(t)] = link(k, above, True)
            wz[z, tile(t)] = link(k, far, True)
        return carry

    lax.fori_loop(0, depth - 1, weights, 0, unroll=4)
    fields = (g0, g1, g2, g3, None)
    for k in range(1, BASIS + 1):
        src, dst = fields[k - 1], fields[k]

        def slab(z, own, k=k, src=src, dst=dst):
            sums = Sums()
            kept = []
            for t in range(3):
                if dst is None and t == 1:
                    continue
                ws = tile_weights(w, z, wz, z, z - 1, t)
                olds, news = [], []
                for c in range(COLS):
                    v = src[c, z, tile(t)]
                    above = rows_above(src, (c, z), t, 3, v)
                    below = rows_below(src, (c, z), t, v)
                    news.append(apply(v, above, below, src[c, z + 1, tile(t)], src[c, z - 1, tile(t)], ws))
                    olds.append(v)
                if dst is not None:
                    for c in range(COLS):
                        dst[c, z, tile(t)] = news[c]
                if t != 1:
                    kept.append((olds, news))
            if own:
                olds, news = (
                    [jnp.where(half, b, a) for a, b in zip(kept[0][i], kept[1][i])] for i in range(2)
                )
                sums.products(k, olds, news)
                sums.flush(acc)

        def far(i, carry, k=k, slab=slab):
            slab(k + i, False)
            slab(depth - DEEP + i, False)
            return carry

        def own(z, carry, slab=slab):
            slab(z, True)
            return carry

        if k < DEEP:
            lax.fori_loop(0, DEEP - k, far, 0)
        lax.fori_loop(DEEP, depth - DEEP, own, 0, unroll=4)


def y_strip(edges, rim):
    _, depth, _, nx = rim.shape
    return pl.pallas_call(
        y_strip_kernel,
        out_shape=jax.ShapeDtypeStruct((MOMENTS * NPAIRS, 8, nx), F32),
        in_specs=[VMEM] * 2,
        out_specs=VMEM,
        scratch_shapes=[pltpu.VMEM((COLS, depth, 24, nx), F32)] * 4
        + [
            pltpu.VMEM((depth, 24, nx), F32),
            pltpu.VMEM((4, depth, 24, nx), F32),
            pltpu.VMEM((depth, 24, nx), F32),
        ],
        compiler_params=params(16),
        cost_estimate=cost(1 << 27),
        name="y_strip",
    )(edges, rim)


def x_strip_kernel(strip, side, first, second, acc1, acc2, acc3, out, s0, s1, s2, s3, kr, w, wz, acc):
    tiles = first.shape[1] // 8
    offset = lanes(8) % PITCH

    def rows(t):
        return slice(8 + 8 * t, 16 + 8 * t)

    def lay(ref, index, t, value):
        ref[index + (rows(t),)] = value
        if t == 0:
            ref[index + (slice(8 + 8 * tiles, 16 + 8 * tiles),)] = value
        if t == tiles - 1:
            ref[index + (slice(0, 8),)] = value

    def next_slab(ref, index, q, at):
        if q < SLABS - 1:
            return ref[index + (q + 1, at)]
        return pltpu.roll(ref[index + (0, at)], 128 - PITCH, 1)

    def last_slab(ref, index, q, at):
        if q > 0:
            return ref[index + (q - 1, at)]
        return pltpu.roll(ref[index + (SLABS - 1, at)], PITCH, 1)

    def fill(a, put):
        for t in range(tiles):
            upper, lower = sides("gx", first[a, tile(t)], second[a, tile(t)])
            for q in range(SLABS):
                value = strip[a, q, tile(t)] if t < tiles - 1 else side[a, q]
                value = jnp.where(offset // 4 == 2, pltpu.roll(upper, (8 - 4 * q) % 128, 1), value)
                value = jnp.where(offset // 4 == 3, pltpu.roll(lower, (12 - 4 * q) % 128, 1), value)
                put(q, t, value)

    fill(COLS, lambda q, t, value: lay(kr, (q,), t, value))

    def fill_column(c, carry):
        fill(c, lambda q, t, value: lay(s0, (c, q), t, value))
        return carry

    lax.fori_loop(0, COLS, fill_column, 0)

    for q in range(SLABS):
        for t in range(tiles):
            k = kr[q, rows(t)]
            right, left = pltpu.roll(k, 127, 1), pltpu.roll(k, 1, 1)
            above = kr[q, 9 + 8 * t : 17 + 8 * t]
            below = kr[q, 7 + 8 * t : 15 + 8 * t]
            far, near = next_slab(kr, (), q, rows(t)), last_slab(kr, (), q, rows(t))
            w[0, q, rows(t)] = centre(k, (right, left, above, below, far, near))
            w[1, q, rows(t)] = link(k, right, True)
            w[2, q, rows(t)] = link(k, left, True)
            above = link(k, above, True)
            w[3, q, rows(t)] = above
            if t == tiles - 1:
                w[3, q, 0:8] = above
            wz[q + 1, rows(t)] = link(k, far, True)
            if q == 0:
                wz[0, rows(t)] = link(k, near, True)
    acc[...] = jnp.zeros_like(acc)
    fields = (s0, s1, s2, s3, None)
    for k in range(1, BASIS + 1):
        src, dst = fields[k - 1], fields[k]

        def slab(q):
            sums = Sums()
            for t in range(tiles if dst is not None else tiles - 1):
                at, above, below = rows(t), slice(9 + 8 * t, 17 + 8 * t), slice(7 + 8 * t, 15 + 8 * t)
                ws = [w[i, q, at] for i in range(4)] + [w[3, q, below], wz[q + 1, at], wz[q, at]]
                olds, news = [], []
                for c in range(COLS):
                    v = src[c, q, at]
                    far, near = next_slab(src, (c,), q, at), last_slab(src, (c,), q, at)
                    news.append(apply(v, src[c, q, above], src[c, q, below], far, near, ws))
                    olds.append(v)
                if dst is not None:
                    for c in range(COLS):
                        lay(dst, (c, q), t, news[c])
                if t < tiles - 1:
                    sums.products(k, olds, news)
            sums.flush(acc.at[0 if q < SLABS - 1 else 1])

        for q in range(SLABS):
            slab(q)

    lane1 = lax.broadcasted_iota(jnp.int32, (1, 128), 1)
    group, place = lane1 // PITCH, lane1 % PITCH // DEEP
    here = (place == 1) | (place == 4)
    total = jnp.zeros((acc.shape[1], 128), F32)
    for kept, sums in (
        ((lane1 >= DEEP) & (lane1 < 128 - DEEP), acc1[...] + acc2[...] + acc3[...]),
        (here & (group >= 1) & (group <= 3), acc[0]),
        (here & (group <= 3), acc[1]),
    ):
        total = total + jnp.where(kept, jnp.sum(sums, axis=1), 0.0)
    total = jnp.concatenate([total, jnp.zeros((128 - total.shape[0], 128), F32)], 0)
    row = lax.dot_general(
        jnp.ones((8, 128), F32),
        total,
        (((1,), (1,)), ((), ())),
        precision=lax.Precision.HIGHEST,
        preferred_element_type=F32,
    )
    out[...] = jnp.broadcast_to(row[0:1][None], out.shape)


def x_strip(strip, side, first, second, accs, peers):
    cols, slabs, ny, nx = strip.shape
    laid = (slabs, ny + 24, nx)
    return pl.pallas_call(
        x_strip_kernel,
        out_shape=jax.ShapeDtypeStruct((peers, 1, 128), F32),
        in_specs=[VMEM] * 7,
        out_specs=VMEM,
        scratch_shapes=[pltpu.VMEM((COLS,) + laid, F32)] * 4
        + [
            pltpu.VMEM(laid, F32),
            pltpu.VMEM((4,) + laid, F32),
            pltpu.VMEM((slabs + 1,) + laid[1:], F32),
            pltpu.VMEM((2, MOMENTS * NPAIRS, 8, nx), F32),
        ],
        compiler_params=params(16),
        name="x_strip",
    )(strip, side, first, second, *accs)


def finish_kernel(ncells, parts, block, ortho, triangle, coef):
    @pl.when(pl.program_id(0) == 0)
    def _():
        row = jnp.sum(parts[...], axis=0) * (1.0 / ncells)
        row = jnp.broadcast_to(row, (24, 128))
        a, b = sublanes(24), lanes(24)
        c, d = a % 4, b % 4
        low, high = jnp.minimum(c, d), jnp.maximum(c, d)
        pair = low * 4 - (low * (low - 1)) // 2 + high - low
        inside = (a < KRYLOV) & (b < KRYLOV)
        index = jnp.where(inside, (a // 4 + b // 4) * NPAIRS + pair, 127)
        matrix = permute_lanes(row, index)
        lane = lanes(1)
        uppers = []
        for k in range(KRYLOV):
            line = matrix[k : k + 1, :]
            pivot = line[:, k : k + 1]
            upper = jnp.where(lane >= k, line / jnp.sqrt(pivot), 0.0)
            uppers.append(upper)
            triangle[k : k + 1, :] = upper[:, 0:KRYLOV]
            if k + 1 < KRYLOV:
                matrix = matrix - matrix[:, k : k + 1] * (line / pivot)
        at = 0
        for i in range(COLS):
            for j in range(i, COLS):
                value = uppers[i][:, j : j + 1]
                value = 1.0 / value if i == j else value
                coef[at] = jnp.broadcast_to(value, (8, 128))
                at += 1

    u = {}
    at = 0
    for i in range(COLS):
        for j in range(i, COLS):
            u[i, j] = coef[at]
            at += 1

    def slab(z, carry):
        for t in range(ortho.shape[2] // 8):
            rows = slice(8 * t, 8 * t + 8)
            done = []
            for j in range(COLS):
                value = block[j, z, rows]
                for i in range(j):
                    value = value - u[i, j] * done[i]
                value = value * u[j, j]
                ortho[j, z, rows] = value
                done.append(value)
        return carry

    lax.fori_loop(0, ortho.shape[1], slab, 0)


def finish(parts, block, ncells):
    cols, nz, ny, nx = block.shape
    steps = 4
    piece = pl.BlockSpec((cols, nz // steps, ny, nx), lambda i: (0, i, 0, 0))
    return pl.pallas_call(
        lambda *refs: finish_kernel(ncells, *refs),
        grid=(steps,),
        out_shape=[
            jax.ShapeDtypeStruct(block.shape, F32),
            jax.ShapeDtypeStruct((KRYLOV, KRYLOV), F32),
        ],
        in_specs=[pl.BlockSpec(parts.shape, lambda i: (0, 0, 0)), piece],
        out_specs=[piece, pl.BlockSpec((KRYLOV, KRYLOV), lambda i: (0, 0))],
        scratch_shapes=[pltpu.VMEM((NPAIRS, 8, 128), F32)],
        compiler_params=params(16),
        name="finish",
    )(parts, block)


def shards(block, kappa):
    axes = ("gx", "gy", "gz")
    peers = lax.axis_size(axes)
    ncells = float(kappa.size * peers)
    first, second = swap(*pack_z(block, kappa), "gz")
    acc1, edge = inner(block, kappa)
    edges, y_first, y_second = pack_y(block, kappa, first, second, acc1)
    y_first, y_second = swap(y_first, y_second, "gy")
    strip = strips(block, kappa, first, second)
    acc2 = outer(block, kappa, edge, first, second)
    rim, side, x_first, x_second = pack_x(y_first, y_second, strip, acc2)
    x_first, x_second = swap(x_first, x_second, "gx")
    acc3 = y_strip(edges, rim)
    moments = x_strip(strip, side, x_first, x_second, (acc1, acc2, acc3), peers)
    parts = lax.all_to_all(moments, axes, 0, 0, tiled=True)
    return tuple(finish(parts, block, ncells))


def solution(mesh):
    return jax.shard_map(
        shards,
        mesh=mesh,
        in_specs=(P(None, "gz", "gy", "gx"), P("gz", "gy", "gx")),
        out_specs=(P(None, "gz", "gy", "gx"), P()),
        check_vma=False,
    )
```

```python
import jax
import jax.numpy as jnp
from jax import lax
from jax.experimental import pallas as pl
from jax.experimental.pallas import tpu as pltpu
from jax.sharding import PartitionSpec as P

COLS = 4
BASIS = 4
KRYLOV = 20
MOMENTS = 2 * BASIS + 1
PAIRS = [(c, d) for c in range(COLS) for d in range(c, COLS)]
NPAIRS = len(PAIRS)
DEEP = BASIS
ARRAYS = COLS + 1
PITCH = 4 * DEEP
SLABS = 3

basis_shift = 6.0
basis_scale = 3.0

F32 = jnp.float32
VMEM = pl.BlockSpec(memory_space=pltpu.VMEM)
HBM = pl.BlockSpec(memory_space=pltpu.HBM)


def params(mib):
    return pltpu.CompilerParams(vmem_limit_bytes=mib * 1024 * 1024)


def cost(flops):
    return pl.CostEstimate(flops=flops, bytes_accessed=1 << 20, transcendentals=0)


def lanes(rows):
    return lax.broadcasted_iota(jnp.int32, (rows, 128), 1)


def sublanes(rows):
    return lax.broadcasted_iota(jnp.int32, (rows, 128), 0)


def permute_lanes(value, index):
    return jnp.take_along_axis(value, index, axis=1, mode="promise_in_bounds")


def even_first(axis, first, second):
    return jnp.where(lax.axis_index(axis) % 2 == 0, first, second)


def sides(axis, first, second):
    at = lax.axis_index(axis)
    upper = jnp.where(at == lax.axis_size(axis) - 1, 0.0, even_first(axis, first, second))
    lower = jnp.where(at == 0, 0.0, even_first(axis, second, first))
    return upper, lower


def swap(first, second, axis):
    peers = lax.axis_size(axis)
    other = [(i, (i - 1 if i % 2 == 0 else i + 1) % peers) for i in range(peers)]
    second = lax.ppermute(second, axis, other)
    first = lax.ppermute(first, axis, [(i, i ^ 1) for i in range(peers)])
    return first, second


def pull(face, axis):
    peers = lax.axis_size(axis)
    return lax.ppermute(face, axis, [(i, (i - 1) % peers) for i in range(peers)])


def last_on(axis):
    return lax.axis_index(axis) == lax.axis_size(axis) - 1


def cut(there, value):
    return jnp.where(there, 0.0, value)


def link(one, other, bounded):
    weight = (one + other) * (0.5 / basis_scale)
    if bounded:
        weight = jnp.where(jnp.minimum(one, other) > 0.0, weight, 0.0)
    return weight


def centre(k, others):
    total = 6.0 * k
    for other in others:
        total = total + other
    return total * (0.5 / basis_scale) - basis_shift / basis_scale


def rows_above(ref, index, t, tiles, value):
    if t == tiles - 1:
        return pltpu.roll(value, 7, 0)
    return ref[index + (slice(8 * t + 1, 8 * t + 9),)]


def rows_below(ref, index, t, value):
    if t == 0:
        return pltpu.roll(value, 1, 0)
    return ref[index + (slice(8 * t - 1, 8 * t + 7),)]


def tile(t):
    return slice(8 * t, 8 * t + 8)


class Sums:
    def __init__(self):
        self.held = {}

    def add(self, at, term):
        self.held[at] = self.held[at] + term if at in self.held else term

    def products(self, k, olds, news):
        for p, (c, d) in enumerate(PAIRS):
            if k == 1:
                self.add(p, olds[c] * olds[d])
            self.add((2 * k - 1) * NPAIRS + p, olds[c] * news[d])
            self.add(2 * k * NPAIRS + p, news[c] * news[d])

    def flush(self, acc):
        for at, total in self.held.items():
            acc[at] += total


def apply(v, above, below, far, near, w):
    new = w[0] * v
    new -= w[1] * pltpu.roll(v, 127, 1)
    new -= w[2] * pltpu.roll(v, 1, 1)
    new -= w[3] * above
    new -= w[4] * below
    new -= w[5] * far
    new -= w[6] * near
    return new


def tile_weights(w, q, wz, far, near, t):
    c0, right, left, above = (w[i, q, tile(t)] for i in range(4))
    below = rows_below(w, (3, q), t, above)
    return c0, right, left, above, below, wz[far, tile(t)], wz[near, tile(t)]


def pack_z_kernel(block, kappa, to_first, to_second, sems):
    nz = kappa.shape[0]
    high = nz - DEEP
    even = lax.axis_index("gz") % 2 == 0
    copies = []
    for i, (out, at) in enumerate(
        ((to_second, jnp.where(even, 0, high)), (to_first, jnp.where(even, high, 0)))
    ):
        copies.append(pltpu.make_async_copy(block.at[:, pl.ds(at, DEEP)], out.at[0:COLS], sems.at[2 * i]))
        copies.append(pltpu.make_async_copy(kappa.at[pl.ds(at, DEEP)], out.at[COLS], sems.at[2 * i + 1]))
    for copy in copies:
        copy.start()
    for copy in copies:
        copy.wait()


def pack_z(block, kappa):
    nz, ny, nx = kappa.shape
    face = jax.ShapeDtypeStruct((ARRAYS, DEEP, ny, nx), F32)
    return pl.pallas_call(
        pack_z_kernel,
        out_shape=[face, face],
        in_specs=[HBM, HBM],
        out_specs=[VMEM] * 2,
        scratch_shapes=[pltpu.SemaphoreType.DMA((4,))],
        compiler_params=params(8),
        name="pack_z",
    )(block, kappa)


def inner_kernel(block, kappa, acc, edge, p1, p2, p3, w, wz):
    nz, ny, _ = kappa.shape
    tiles = ny // 8
    half = sublanes(8) < 4
    acc[...] = jnp.zeros_like(acc)

    def weights(z, carry):
        for t in range(tiles):
            k = kappa[z, tile(t)]
            right, left = pltpu.roll(k, 127, 1), pltpu.roll(k, 1, 1)
            above = rows_above(kappa, (z,), t, tiles, k)
            below = rows_below(kappa, (z,), t, k)
            far = kappa[z + 1, tile(t)]
            near = kappa[jnp.maximum(z - 1, 0), tile(t)]
            w[0, z, tile(t)] = centre(k, (right, left, above, below, far, near))
            w[1, z, tile(t)] = link(k, right, False)
            w[2, z, tile(t)] = link(k, left, False)
            w[3, z, tile(t)] = link(k, above, False)
            wz[z, tile(t)] = link(k, far, False)
        return carry

    lax.fori_loop(0, nz - 1, weights, 0, unroll=3)
    fields = (block, p1, p2, p3, None)
    for k in range(1, BASIS + 1):
        src, dst = fields[k - 1], fields[k]

        def slab(z, carry, k=k, src=src, dst=dst):
            sums = Sums()

            def step(t):
                ws = tile_weights(w, z, wz, z, z - 1, t)
                olds, news = [], []
                for c in range(COLS):
                    v = src[c, z, tile(t)]
                    above = rows_above(src, (c, z), t, tiles, v)
                    below = rows_below(src, (c, z), t, v)
                    news.append(apply(v, above, below, src[c, z + 1, tile(t)], src[c, z - 1, tile(t)], ws))
                    olds.append(v)
                if dst is not None:
                    for c in range(COLS):
                        dst[c, z, tile(t)] = news[c]
                return olds, news

            first, last = step(0), step(tiles - 1)
            olds, news = (
                [jnp.where(half, b, a) for a, b in zip(first[i], last[i])] for i in range(2)
            )
            sums.products(k, olds, news)
            for t in range(1, tiles - 1):
                sums.products(k, *step(t))
            sums.flush(acc)
            return carry

        lax.fori_loop(k, nz - k, slab, 0, unroll=2)
        if dst is not None:
            for i in range(2):
                edge[k - 1, 0, i] = dst[:, k + i]
                edge[k - 1, 1, i] = dst[:, nz - 1 - k - i]


def inner(block, kappa):
    nz, ny, nx = kappa.shape
    return pl.pallas_call(
        inner_kernel,
        out_shape=[
            jax.ShapeDtypeStruct((MOMENTS * NPAIRS, 8, nx), F32),
            jax.ShapeDtypeStruct((BASIS - 1, 2, 2, COLS, ny, nx), F32),
        ],
        in_specs=[VMEM] * 2,
        out_specs=[VMEM] * 2,
        scratch_shapes=[pltpu.VMEM(block.shape, F32)] * 3
        + [pltpu.VMEM((4, nz, ny, nx), F32), pltpu.VMEM((nz, ny, nx), F32)],
        compiler_params=params(24),
        cost_estimate=cost(1 << 28),
        name="inner",
    )(block, kappa)


def pack_y_kernel(
    b_low, b_high, k_low, k_high, f_low, f_high, s_low, s_high, after, edges, to_first, to_second
):
    nz = k_low.shape[0]

    def own(z, carry):
        for a in range(ARRAYS):
            edges[a, z + DEEP, 0] = b_low[a, z] if a < COLS else k_low[z]
            edges[a, z + DEEP, 1] = b_high[a, z] if a < COLS else k_high[z]
        return carry

    lax.fori_loop(0, nz, own, 0, unroll=4)

    def far(i, carry):
        for a in range(ARRAYS):
            for at, (one, other) in enumerate(((f_low, s_low), (f_high, s_high))):
                upper, lower = sides("gz", one[a, i], other[a, i])
                edges[a, i, at] = lower
                edges[a, nz + DEEP + i, at] = upper
        return carry

    lax.fori_loop(0, DEEP, far, 0, unroll=2)
    half = sublanes(8) < 4

    def pairs(duo, carry):
        z = duo * 2
        for a in range(ARRAYS):
            upper = jnp.where(half, pltpu.roll(edges[a, z, 1], 4, 0), edges[a, z + 1, 1])
            lower = jnp.where(half, edges[a, z, 0], pltpu.roll(edges[a, z + 1, 0], 4, 0))
            to_first[a, duo] = even_first("gy", upper, lower)
            to_second[a, duo] = even_first("gy", lower, upper)
        return carry

    lax.fori_loop(0, to_first.shape[1], pairs, 0, unroll=4)


def pack_y(block, kappa, first, second, after):
    nz, ny, nx = kappa.shape
    depth = nz + 2 * DEEP
    last = ny // 8 - 1
    whole = lambda shape: pl.BlockSpec(shape, lambda i: (0,) * len(shape))
    b_edge = lambda at: pl.BlockSpec((COLS, nz, 8, nx), lambda i: (0, 0, at, 0))
    k_edge = lambda at: pl.BlockSpec((nz, 8, nx), lambda i: (0, at, 0))
    f_edge = lambda at: pl.BlockSpec((ARRAYS, DEEP, 8, nx), lambda i: (0, 0, at, 0))
    edges = (ARRAYS, depth, 2, 8, nx)
    face = (ARRAYS, depth // 2, 8, nx)
    return pl.pallas_call(
        pack_y_kernel,
        grid=(1,),
        out_shape=[jax.ShapeDtypeStruct(s, F32) for s in (edges, face, face)],
        in_specs=[f(at) for f in (b_edge, k_edge, f_edge, f_edge) for at in (0, last)]
        + [pl.BlockSpec(memory_space=pl.ANY)],
        out_specs=[whole(edges), whole(face), whole(face)],
        compiler_params=params(16),
        name="pack_y",
    )(block, block, kappa, kappa, first, first, second, second, after)


def outer_kernel(block, kappa, edge, first, second, acc, f0, f1, f2, f3, kz, w, wz):
    nz, ny, _ = kappa.shape
    tiles = ny // 8
    half = sublanes(8) < 4
    acc[...] = jnp.zeros_like(acc)

    def far(i, carry):
        for a in range(ARRAYS):
            upper, lower = sides("gz", first[a, i], second[a, i])
            if a < COLS:
                f0[0, a, i] = lower
                f0[1, a, DEEP - 1 - i] = upper
            else:
                kz[0, i] = lower
                kz[1, DEEP - 1 - i] = upper
        return carry

    lax.fori_loop(0, DEEP, far, 0)
    for i in range(2):
        for c in range(COLS):
            f0[0, c, DEEP + i] = block[c, i]
            f0[1, c, DEEP + i] = block[c, nz - 1 - i]
            for k, f in enumerate((f1, f2, f3)):
                for side in range(2):
                    f[side, c, DEEP + i] = edge[k, side, i, c]
    for i in range(DEEP + 1):
        kz[0, DEEP + i] = kappa[i]
        kz[1, DEEP + i] = kappa[nz - 1 - i]

    def weights(at, carry):
        side, e = at // 8, at % 8
        for t in range(tiles):
            k = kz[side, e, tile(t)]
            right, left = pltpu.roll(k, 127, 1), pltpu.roll(k, 1, 1)
            above = rows_above(kz, (side, e), t, tiles, k)
            below = rows_below(kz, (side, e), t, k)
            far = kz[side, e + 1, tile(t)]
            near = kz[side, jnp.maximum(e - 1, 0), tile(t)]
            w[0, at, tile(t)] = centre(k, (right, left, above, below, far, near))
            w[1, at, tile(t)] = link(k, right, False)
            w[2, at, tile(t)] = link(k, left, False)
            w[3, at, tile(t)] = link(k, above, False)
            wz[at, tile(t)] = link(k, far, True)
        return carry

    lax.fori_loop(0, 16, weights, 0, unroll=2)
    fields = (f0, f1, f2, f3, None)
    for k in range(1, BASIS + 1):
        src, dst = fields[k - 1], fields[k]

        def both(side, carry, k=k, src=src, dst=dst):
            for j in range(DEEP):
                own = j >= DEEP - k
                sums = Sums()

                def step(t):
                    at = side * 8 + j + k
                    ws = tile_weights(w, at, wz, at, at - 1, t)
                    olds, news = [], []
                    for c in range(COLS):
                        v = src[side, c, j + 1, tile(t)]
                        above = rows_above(src, (side, c, j + 1), t, tiles, v)
                        below = rows_below(src, (side, c, j + 1), t, v)
                        far, near = src[side, c, j + 2, tile(t)], src[side, c, j, tile(t)]
                        news.append(apply(v, above, below, far, near, ws))
                        olds.append(v)
                    if dst is not None:
                        for c in range(COLS):
                            dst[side, c, j, tile(t)] = news[c]
                    return olds, news

                first, last = step(0), step(tiles - 1)
                if own:
                    olds, news = (
                        [jnp.where(half, b, a) for a, b in zip(first[i], last[i])] for i in range(2)
                    )
                    sums.products(k, olds, news)
                for t in range(1, tiles - 1):
                    pair = step(t)
                    if own:
                        sums.products(k, *pair)
                sums.flush(acc)
            return carry

        lax.fori_loop(0, 2, both, 0)


def outer(block, kappa, edge, first, second):
    nz, ny, nx = kappa.shape
    return pl.pallas_call(
        outer_kernel,
        out_shape=jax.ShapeDtypeStruct((MOMENTS * NPAIRS, 8, nx), F32),
        in_specs=[VMEM] * 5,
        out_specs=VMEM,
        scratch_shapes=[pltpu.VMEM((2, COLS, DEEP + 2, ny, nx), F32)] * 4
        + [
            pltpu.VMEM((2, 2 * DEEP + 1, ny, nx), F32),
            pltpu.VMEM((4, 16, ny, nx), F32),
            pltpu.VMEM((16, ny, nx), F32),
        ],
        compiler_params=params(24),
        cost_estimate=cost(1 << 27),
        name="outer",
    )(block, kappa, edge, first, second)


def strip_of(planes):
    lane = lanes(8)
    offset, group = lane % PITCH, lane // PITCH
    index = jnp.where(offset < 8, 120 + offset, offset - 8)
    strip = permute_lanes(planes[0], index)
    for g, plane in enumerate(planes[1:]):
        strip = jnp.where(group == g + 1, permute_lanes(plane, index), strip)
    return strip


def strips_kernel(block, kappa, first, second, strip):
    nz, ny, _ = kappa.shape

    def rows(t, carry):
        at = pl.ds(pl.multiple_of(t * 8, 8), 8)
        for a in range(ARRAYS):
            ends = [sides("gz", first[a, i, at], second[a, i, at]) for i in range(DEEP)]

            def plane(z):
                if z < DEEP:
                    return ends[z][1]
                if z >= nz + DEEP:
                    return ends[z - nz - DEEP][0]
                return block[a, z - DEEP, at] if a < COLS else kappa[z - DEEP, at]

            for q in range(SLABS):
                strip[a, q, at] = strip_of([plane(z) for z in range(q, nz + 2 * DEEP, SLABS)])
        return carry

    lax.fori_loop(0, ny // 8, rows, 0)


def strips(block, kappa, first, second):
    nz, ny, nx = kappa.shape
    return pl.pallas_call(
        strips_kernel,
        out_shape=jax.ShapeDtypeStruct((ARRAYS, SLABS, ny, nx), F32),
        in_specs=[VMEM] * 4,
        out_specs=VMEM,
        compiler_params=params(16),
        cost_estimate=cost(1 << 25),
        name="strips",
    )(block, kappa, first, second)


HALVES = [(a, q) for a in range(ARRAYS) for q in range(SLABS)]


def pack_x_kernel(first, second, strip, after, rim, side, face):
    depth = rim.shape[1]
    ny = strip.shape[2]
    half = sublanes(8) < 4
    low = lanes(8) % PITCH < 8

    def duos(duo, carry):
        for a in range(ARRAYS):
            upper, lower = sides("gy", first[a, duo], second[a, duo])
            rim[a, duo * 2] = jnp.where(half, upper, pltpu.roll(lower, 4, 0))
            rim[a, duo * 2 + 1] = jnp.where(half, pltpu.roll(upper, 4, 0), lower)
        return carry

    lax.fori_loop(0, depth // 2, duos, 0, unroll=4)
    for a, q in HALVES:
        side[a, q] = strip_of([rim[a, z] for z in range(q, depth, SLABS)])

    def pack(at, get):
        for n in range(0, len(HALVES), 2):
            value = pltpu.roll(get(*HALVES[n]), 120, 1)
            if n + 1 < len(HALVES):
                value = jnp.where(low, value, get(*HALVES[n + 1]))
            face[n // 2, at] = value

    def rows(t, carry):
        at = pl.ds(pl.multiple_of(t * 8, 8), 8)
        pack(at, lambda a, q: strip[a, q, at])
        return carry

    lax.fori_loop(0, ny // 8, rows, 0, unroll=4)
    pack(slice(ny, ny + 8), lambda a, q: side[a, q])


def pack_x(first, second, strip, after):
    _, _, ny, nx = strip.shape
    face = ((len(HALVES) + 1) // 2, ny + 8, nx)
    rim = (ARRAYS, 2 * first.shape[1], 8, nx)
    return pl.pallas_call(
        pack_x_kernel,
        out_shape=[jax.ShapeDtypeStruct(s, F32) for s in (rim, (ARRAYS, SLABS, 8, nx), face)],
        in_specs=[VMEM] * 3 + [pl.BlockSpec(memory_space=pl.ANY)],
        out_specs=[VMEM] * 3,
        compiler_params=params(16),
        name="pack_x",
    )(first, second, strip, after)


def y_strip_kernel(edges, rim, acc, g0, g1, g2, g3, kr, w, wz):
    depth = rim.shape[1]
    half = sublanes(8) < 4
    acc[...] = jnp.zeros_like(acc)

    def fill(z, carry):
        for a in range(ARRAYS):
            parts = (edges[a, z, 1], rim[a, z], edges[a, z, 0])
            for t, part in enumerate(parts):
                if a < COLS:
                    g0[a, z, tile(t)] = part
                else:
                    kr[z, tile(t)] = part
        return carry

    lax.fori_loop(0, depth, fill, 0, unroll=4)

    def weights(z, carry):
        for t in range(3):
            k = kr[z, tile(t)]
            right, left = pltpu.roll(k, 127, 1), pltpu.roll(k, 1, 1)
            above = rows_above(kr, (z,), t, 3, k)
            below = rows_below(kr, (z,), t, k)
            far = kr[z + 1, tile(t)]
            near = kr[jnp.maximum(z - 1, 0), tile(t)]
            w[0, z, tile(t)] = centre(k, (right, left, above, below, far, near))
            w[1, z, tile(t)] = link(k, right, False)
            w[2, z, tile(t)] = link(k, left, False)
            w[3, z, tile(t)] = link(k, above, True)
            wz[z, tile(t)] = link(k, far, True)
        return carry

    lax.fori_loop(0, depth - 1, weights, 0, unroll=4)
    fields = (g0, g1, g2, g3, None)
    for k in range(1, BASIS + 1):
        src, dst = fields[k - 1], fields[k]

        def slab(z, own, k=k, src=src, dst=dst):
            sums = Sums()
            kept = []
            for t in range(3):
                if dst is None and t == 1:
                    continue
                ws = tile_weights(w, z, wz, z, z - 1, t)
                olds, news = [], []
                for c in range(COLS):
                    v = src[c, z, tile(t)]
                    above = rows_above(src, (c, z), t, 3, v)
                    below = rows_below(src, (c, z), t, v)
                    news.append(apply(v, above, below, src[c, z + 1, tile(t)], src[c, z - 1, tile(t)], ws))
                    olds.append(v)
                if dst is not None:
                    for c in range(COLS):
                        dst[c, z, tile(t)] = news[c]
                if t != 1:
                    kept.append((olds, news))
            if own:
                olds, news = (
                    [jnp.where(half, b, a) for a, b in zip(kept[0][i], kept[1][i])] for i in range(2)
                )
                sums.products(k, olds, news)
                sums.flush(acc)

        def far(i, carry, k=k, slab=slab):
            slab(k + i, False)
            slab(depth - DEEP + i, False)
            return carry

        def own(z, carry, slab=slab):
            slab(z, True)
            return carry

        if k < DEEP:
            lax.fori_loop(0, DEEP - k, far, 0)
        lax.fori_loop(DEEP, depth - DEEP, own, 0, unroll=4)


def y_strip(edges, rim):
    _, depth, _, nx = rim.shape
    return pl.pallas_call(
        y_strip_kernel,
        out_shape=jax.ShapeDtypeStruct((MOMENTS * NPAIRS, 8, nx), F32),
        in_specs=[VMEM] * 2,
        out_specs=VMEM,
        scratch_shapes=[pltpu.VMEM((COLS, depth, 24, nx), F32)] * 4
        + [
            pltpu.VMEM((depth, 24, nx), F32),
            pltpu.VMEM((4, depth, 24, nx), F32),
            pltpu.VMEM((depth, 24, nx), F32),
        ],
        compiler_params=params(16),
        cost_estimate=cost(1 << 27),
        name="y_strip",
    )(edges, rim)


def x_strip_kernel(strip, side, face, acc1, acc2, acc3, out, s0, s1, s2, s3, kr, w, wz, acc):
    tiles = face.shape[1] // 8
    offset = lanes(8) % PITCH
    right_seam, left_seam = (last_on("gx") & (offset == at) for at in (7, 8))

    def rows(t):
        return slice(8 + 8 * t, 16 + 8 * t)

    def lay(ref, index, t, value):
        ref[index + (rows(t),)] = value
        if t == 0:
            ref[index + (slice(8 + 8 * tiles, 16 + 8 * tiles),)] = value
        if t == tiles - 1:
            ref[index + (slice(0, 8),)] = value

    def next_slab(ref, index, q, at):
        if q < SLABS - 1:
            return ref[index + (q + 1, at)]
        return pltpu.roll(ref[index + (0, at)], 128 - PITCH, 1)

    def last_slab(ref, index, q, at):
        if q > 0:
            return ref[index + (q - 1, at)]
        return pltpu.roll(ref[index + (SLABS - 1, at)], PITCH, 1)

    for n, (a, q) in enumerate(HALVES):
        for t in range(tiles):
            value = strip[a, q, tile(t)] if t < tiles - 1 else side[a, q]
            beyond = face[n // 2, tile(t)]
            beyond = pltpu.roll(beyond, 8, 1) if n % 2 == 0 else beyond
            value = jnp.where(offset < 8, value, beyond)
            if a < COLS:
                lay(s0, (a, q), t, value)
            else:
                lay(kr, (q,), t, value)

    for q in range(SLABS):
        for t in range(tiles):
            k = kr[q, rows(t)]
            right, left = cut(right_seam, pltpu.roll(k, 127, 1)), cut(left_seam, pltpu.roll(k, 1, 1))
            above = kr[q, 9 + 8 * t : 17 + 8 * t]
            below = kr[q, 7 + 8 * t : 15 + 8 * t]
            far, near = next_slab(kr, (), q, rows(t)), last_slab(kr, (), q, rows(t))
            w[0, q, rows(t)] = centre(k, (right, left, above, below, far, near))
            w[1, q, rows(t)] = link(k, right, True)
            w[2, q, rows(t)] = link(k, left, True)
            above = link(k, above, True)
            w[3, q, rows(t)] = above
            if t == tiles - 1:
                w[3, q, 0:8] = above
            wz[q + 1, rows(t)] = link(k, far, True)
            if q == 0:
                wz[0, rows(t)] = link(k, near, True)
    acc[...] = jnp.zeros_like(acc)
    fields = (s0, s1, s2, s3, None)
    for k in range(1, BASIS + 1):
        src, dst = fields[k - 1], fields[k]

        def slab(q):
            sums = Sums()
            for t in range(tiles if dst is not None else tiles - 1):
                at, above, below = rows(t), slice(9 + 8 * t, 17 + 8 * t), slice(7 + 8 * t, 15 + 8 * t)
                ws = [w[i, q, at] for i in range(4)] + [w[3, q, below], wz[q + 1, at], wz[q, at]]
                olds, news = [], []
                for c in range(COLS):
                    v = src[c, q, at]
                    far, near = next_slab(src, (c,), q, at), last_slab(src, (c,), q, at)
                    news.append(apply(v, src[c, q, above], src[c, q, below], far, near, ws))
                    olds.append(v)
                if dst is not None:
                    for c in range(COLS):
                        lay(dst, (c, q), t, news[c])
                if t < tiles - 1:
                    sums.products(k, olds, news)
            sums.flush(acc.at[q])

        for q in range(SLABS):
            slab(q)

    lane1 = lax.broadcasted_iota(jnp.int32, (1, 128), 1)
    z = lane1 // PITCH * SLABS
    here = (lane1 % PITCH >= DEEP) & (lane1 % PITCH < PITCH - DEEP)
    groups = 128 // PITCH
    total = jnp.where(
        (lane1 >= DEEP) & (lane1 < 128 - DEEP), jnp.sum(acc1[...] + acc2[...] + acc3[...], axis=1), 0.0
    )
    for q in range(SLABS):
        kept = here & (z + q >= DEEP) & (z + q < groups * SLABS - DEEP)
        total = total + jnp.where(kept, jnp.sum(acc[q], axis=1), 0.0)
    total = jnp.concatenate([total, jnp.zeros((128 - total.shape[0], 128), F32)], 0)
    row = lax.dot_general(
        jnp.ones((8, 128), F32),
        total,
        (((1,), (1,)), ((), ())),
        precision=lax.Precision.HIGHEST,
        preferred_element_type=F32,
    )
    out[...] = jnp.broadcast_to(row[0:1][None], out.shape)


def x_strip(strip, side, face, accs, peers):
    _, slabs, ny, nx = strip.shape
    laid = (slabs, ny + 24, nx)
    return pl.pallas_call(
        x_strip_kernel,
        out_shape=jax.ShapeDtypeStruct((peers, 1, 128), F32),
        in_specs=[VMEM] * 6,
        out_specs=VMEM,
        scratch_shapes=[pltpu.VMEM((COLS,) + laid, F32)] * 4
        + [
            pltpu.VMEM(laid, F32),
            pltpu.VMEM((4,) + laid, F32),
            pltpu.VMEM((slabs + 1,) + laid[1:], F32),
            pltpu.VMEM((slabs, MOMENTS * NPAIRS, 8, nx), F32),
        ],
        compiler_params=params(16),
        name="x_strip",
    )(strip, side, face, *accs)


def factor(row, triangle, coef):
    lane, sub = lanes(8), sublanes(8)
    blocks = (KRYLOV + 7) // 8
    columns = []
    for b in range(KRYLOV):
        parts = []
        for i in range(blocks):
            a = sub + 8 * i
            low, high = jnp.minimum(a % COLS, b % COLS), jnp.maximum(a % COLS, b % COLS)
            pair = low * COLS - (low * (low - 1)) // 2 + high - low
            index = jnp.where(a < KRYLOV, (a // COLS + b // COLS) * NPAIRS + pair, 127)
            parts.append(permute_lanes(row, index))
        columns.append(parts)
    at = 0
    for k in range(KRYLOV):
        i, j = k // 8, k % 8

        def entry(b):
            return jnp.broadcast_to(columns[b][i][j : j + 1], (8, 128))

        pivot = entry(k)
        inverse = 1.0 / pivot
        root = jnp.sqrt(pivot)
        scale = 1.0 / root
        line = jnp.where(lane == k, root, 0.0)
        if k < COLS:
            coef[at] = scale
            at += 1
        for b in range(k + 1, KRYLOV):
            value = entry(b)
            line = jnp.where(lane == b, value * scale, line)
            if b < COLS:
                coef[at] = value * scale
                at += 1
            value = value * inverse
            for n in range((k + 1) // 8, blocks):
                columns[b][n] = columns[b][n] - columns[k][n] * value
        triangle[k : k + 1, :] = line[0:1, 0:KRYLOV]


def finish_kernel(ncells, parts, block, ortho, triangle, coef):
    step = pl.program_id(0)

    @pl.when(step == 0)
    def _():
        row = jnp.sum(parts[...], axis=0) * (1.0 / ncells)
        factor(jnp.broadcast_to(row, (8, 128)), triangle, coef)

    u = {}
    for i in range(COLS):
        for j in range(i, COLS):
            u[i, j] = coef[len(u)]
    slabs = ortho.shape[1]

    def slab(z, carry):
        for t in range(ortho.shape[2] // 8):
            done = []
            for j in range(COLS):
                value = block[j, step * slabs + z, tile(t)]
                for i in range(j):
                    value = value - u[i, j] * done[i]
                value = value * u[j, j]
                ortho[j, z, tile(t)] = value
                done.append(value)
        return carry

    lax.fori_loop(0, slabs, slab, 0, unroll=2)


def finish(parts, block, ncells):
    cols, nz, ny, nx = block.shape
    steps = 4
    piece = pl.BlockSpec((cols, nz // steps, ny, nx), lambda i: (0, i, 0, 0))
    return pl.pallas_call(
        lambda *refs: finish_kernel(ncells, *refs),
        grid=(steps,),
        out_shape=[
            jax.ShapeDtypeStruct(block.shape, F32),
            jax.ShapeDtypeStruct((KRYLOV, KRYLOV), F32),
        ],
        in_specs=[pl.BlockSpec(parts.shape, lambda i: (0, 0, 0)), VMEM],
        out_specs=[piece, pl.BlockSpec((KRYLOV, KRYLOV), lambda i: (0, 0))],
        scratch_shapes=[pltpu.VMEM((NPAIRS, 8, 128), F32)],
        compiler_params=params(16),
        name="finish",
    )(parts, block)


def shards(block, kappa):
    axes = ("gx", "gy", "gz")
    peers = lax.axis_size(axes)
    ncells = float(kappa.size * peers)
    far = [pltpu.with_memory_space_constraint(value, pltpu.HBM) for value in (block, kappa)]
    first, second = swap(*pack_z(*far), "gz")
    acc1, edge = inner(block, kappa)
    edges, y_first, y_second = pack_y(block, kappa, first, second, acc1)
    y_first, y_second = swap(y_first, y_second, "gy")
    strip = strips(block, kappa, first, second)
    acc2 = outer(block, kappa, edge, first, second)
    rim, side, face = pack_x(y_first, y_second, strip, acc2)
    face = pull(face, "gx")
    acc3 = y_strip(edges, rim)
    moments = x_strip(strip, side, face, (acc1, acc2, acc3), peers)
    parts = lax.all_to_all(moments, axes, 0, 0, tiled=True)
    return tuple(finish(parts, block, ncells))


def solution(mesh):
    return jax.shard_map(
        shards,
        mesh=mesh,
        in_specs=(P(None, "gz", "gy", "gx"), P("gz", "gy", "gx")),
        out_specs=(P(None, "gz", "gy", "gx"), P()),
        check_vma=False,
    )
```

```python
import jax
import jax.numpy as jnp
from jax import lax
from jax.experimental import pallas as pl
from jax.experimental.pallas import tpu as pltpu
from jax.sharding import PartitionSpec as P

COLS = 4
BASIS = 4
KRYLOV = 20
MOMENTS = 2 * BASIS + 1
PAIRS = [(c, d) for c in range(COLS) for d in range(c, COLS)]
NPAIRS = len(PAIRS)
DEEP = BASIS
ARRAYS = COLS + 1
PITCH = 4 * DEEP
SLABS = 3

basis_shift = 6.0
basis_scale = 3.0

F32 = jnp.float32
VMEM = pl.BlockSpec(memory_space=pltpu.VMEM)
HBM = pl.BlockSpec(memory_space=pltpu.HBM)


def params(mib):
    return pltpu.CompilerParams(vmem_limit_bytes=mib * 1024 * 1024)


def cost(flops):
    return pl.CostEstimate(flops=flops, bytes_accessed=1 << 20, transcendentals=0)


def lanes(rows):
    return lax.broadcasted_iota(jnp.int32, (rows, 128), 1)


def sublanes(rows):
    return lax.broadcasted_iota(jnp.int32, (rows, 128), 0)


def permute_lanes(value, index):
    return jnp.take_along_axis(value, index, axis=1, mode="promise_in_bounds")


def even_first(axis, first, second):
    return jnp.where(lax.axis_index(axis) % 2 == 0, first, second)


def sides(axis, first, second):
    at = lax.axis_index(axis)
    upper = jnp.where(at == lax.axis_size(axis) - 1, 0.0, even_first(axis, first, second))
    lower = jnp.where(at == 0, 0.0, even_first(axis, second, first))
    return upper, lower


def swap(first, second, axis):
    peers = lax.axis_size(axis)
    other = [(i, (i - 1 if i % 2 == 0 else i + 1) % peers) for i in range(peers)]
    second = lax.ppermute(second, axis, other)
    first = lax.ppermute(first, axis, [(i, i ^ 1) for i in range(peers)])
    return first, second


def upward():
    return lax.axis_index("gz") % 2 == 0


def pull(face, axis):
    peers, layers = lax.axis_size(axis), lax.axis_size("gz")
    pairs = []
    for i in range(peers):
        for z in range(layers):
            to = (i - 1 if z % 2 == 0 else i + 1) % peers
            pairs.append((i * layers + z, to * layers + z))
    return lax.ppermute(face, (axis, "gz"), pairs)


def at_seam(axis):
    at = lax.axis_index(axis)
    return at == jnp.where(upward(), lax.axis_size(axis) - 1, 0)


def cut(there, value):
    return jnp.where(there, 0.0, value)


def link(one, other, bounded):
    weight = (one + other) * (0.5 / basis_scale)
    if bounded:
        weight = jnp.where(jnp.minimum(one, other) > 0.0, weight, 0.0)
    return weight


def centre(k, others):
    total = 6.0 * k
    for other in others:
        total = total + other
    return total * (0.5 / basis_scale) - basis_shift / basis_scale


def rows_above(ref, index, t, tiles, value):
    if t == tiles - 1:
        return pltpu.roll(value, 7, 0)
    return ref[index + (slice(8 * t + 1, 8 * t + 9),)]


def rows_below(ref, index, t, value):
    if t == 0:
        return pltpu.roll(value, 1, 0)
    return ref[index + (slice(8 * t - 1, 8 * t + 7),)]


def tile(t):
    return slice(8 * t, 8 * t + 8)


class Sums:
    def __init__(self):
        self.held = {}

    def add(self, at, term):
        self.held[at] = self.held[at] + term if at in self.held else term

    def products(self, k, olds, news):
        for p, (c, d) in enumerate(PAIRS):
            if k == 1:
                self.add(p, olds[c] * olds[d])
            self.add((2 * k - 1) * NPAIRS + p, olds[c] * news[d])
            self.add(2 * k * NPAIRS + p, news[c] * news[d])

    def flush(self, acc):
        for at, total in self.held.items():
            acc[at] += total


def apply(v, above, below, far, near, w):
    new = w[0] * v
    new -= w[1] * pltpu.roll(v, 127, 1)
    new -= w[2] * pltpu.roll(v, 1, 1)
    new -= w[3] * above
    new -= w[4] * below
    new -= w[5] * far
    new -= w[6] * near
    return new


def tile_weights(w, q, wz, far, near, t):
    c0, right, left, above = (w[i, q, tile(t)] for i in range(4))
    below = rows_below(w, (3, q), t, above)
    return c0, right, left, above, below, wz[far, tile(t)], wz[near, tile(t)]


def pack_z_kernel(block, kappa, to_first, to_second, sems):
    nz = kappa.shape[0]
    high = nz - DEEP
    even = lax.axis_index("gz") % 2 == 0
    copies = []
    for i, (out, at) in enumerate(
        ((to_second, jnp.where(even, 0, high)), (to_first, jnp.where(even, high, 0)))
    ):
        copies.append(pltpu.make_async_copy(block.at[:, pl.ds(at, DEEP)], out.at[0:COLS], sems.at[2 * i]))
        copies.append(pltpu.make_async_copy(kappa.at[pl.ds(at, DEEP)], out.at[COLS], sems.at[2 * i + 1]))
    for copy in copies:
        copy.start()
    for copy in copies:
        copy.wait()


def pack_z(block, kappa):
    nz, ny, nx = kappa.shape
    face = jax.ShapeDtypeStruct((ARRAYS, DEEP, ny, nx), F32)
    return pl.pallas_call(
        pack_z_kernel,
        out_shape=[face, face],
        in_specs=[HBM, HBM],
        out_specs=[VMEM] * 2,
        scratch_shapes=[pltpu.SemaphoreType.DMA((4,))],
        compiler_params=params(8),
        name="pack_z",
    )(block, kappa)


def inner_kernel(block, kappa, acc, edge, p1, p2, p3, w, wz):
    nz, ny, _ = kappa.shape
    tiles = ny // 8
    half = sublanes(8) < 4
    acc[...] = jnp.zeros_like(acc)

    def weights(z, carry):
        for t in range(tiles):
            k = kappa[z, tile(t)]
            right, left = pltpu.roll(k, 127, 1), pltpu.roll(k, 1, 1)
            above = rows_above(kappa, (z,), t, tiles, k)
            below = rows_below(kappa, (z,), t, k)
            far = kappa[z + 1, tile(t)]
            near = kappa[jnp.maximum(z - 1, 0), tile(t)]
            w[0, z, tile(t)] = centre(k, (right, left, above, below, far, near))
            w[1, z, tile(t)] = link(k, right, False)
            w[2, z, tile(t)] = link(k, left, False)
            w[3, z, tile(t)] = link(k, above, False)
            wz[z, tile(t)] = link(k, far, False)
        return carry

    lax.fori_loop(0, nz - 1, weights, 0, unroll=3)
    fields = (block, p1, p2, p3, None)
    for k in range(1, BASIS + 1):
        src, dst = fields[k - 1], fields[k]

        def slab(z, carry, k=k, src=src, dst=dst):
            sums = Sums()

            def step(t):
                ws = tile_weights(w, z, wz, z, z - 1, t)
                olds, news = [], []
                for c in range(COLS):
                    v = src[c, z, tile(t)]
                    above = rows_above(src, (c, z), t, tiles, v)
                    below = rows_below(src, (c, z), t, v)
                    news.append(apply(v, above, below, src[c, z + 1, tile(t)], src[c, z - 1, tile(t)], ws))
                    olds.append(v)
                if dst is not None:
                    for c in range(COLS):
                        dst[c, z, tile(t)] = news[c]
                return olds, news

            first, last = step(0), step(tiles - 1)
            olds, news = (
                [jnp.where(half, b, a) for a, b in zip(first[i], last[i])] for i in range(2)
            )
            sums.products(k, olds, news)
            for t in range(1, tiles - 1):
                sums.products(k, *step(t))
            sums.flush(acc)
            return carry

        lax.fori_loop(k, nz - k, slab, 0, unroll=2)
        if dst is not None:
            for i in range(2):
                edge[k - 1, 0, i] = dst[:, k + i]
                edge[k - 1, 1, i] = dst[:, nz - 1 - k - i]


def inner(block, kappa):
    nz, ny, nx = kappa.shape
    return pl.pallas_call(
        inner_kernel,
        out_shape=[
            jax.ShapeDtypeStruct((MOMENTS * NPAIRS, 8, nx), F32),
            jax.ShapeDtypeStruct((BASIS - 1, 2, 2, COLS, ny, nx), F32),
        ],
        in_specs=[VMEM] * 2,
        out_specs=[VMEM] * 2,
        scratch_shapes=[pltpu.VMEM(block.shape, F32)] * 3
        + [pltpu.VMEM((4, nz, ny, nx), F32), pltpu.VMEM((nz, ny, nx), F32)],
        compiler_params=params(24),
        cost_estimate=cost(1 << 28),
        name="inner",
    )(block, kappa)


def pack_y_kernel(b_low, b_high, k_low, k_high, f_low, f_high, s_low, s_high, after, kept, face):
    nz = k_low.shape[0]

    def lay(a, z, low, high):
        face[a, z] = jnp.where(upward(), low, high)
        kept[a, z] = jnp.where(upward(), high, low)

    def own(z, carry):
        for a in range(ARRAYS):
            if a < COLS:
                lay(a, z + DEEP, b_low[a, z], b_high[a, z])
            else:
                lay(a, z + DEEP, k_low[z], k_high[z])
        return carry

    lax.fori_loop(0, nz, own, 0, unroll=4)

    def far(i, carry):
        for a in range(ARRAYS):
            low = sides("gz", f_low[a, i], s_low[a, i])
            high = sides("gz", f_high[a, i], s_high[a, i])
            lay(a, nz + DEEP + i, low[0], high[0])
            lay(a, i, low[1], high[1])
        return carry

    lax.fori_loop(0, DEEP, far, 0, unroll=2)


def pack_y(block, kappa, first, second, after):
    nz, ny, nx = kappa.shape
    last = ny // 8 - 1
    whole = lambda shape: pl.BlockSpec(shape, lambda i: (0,) * len(shape))
    b_edge = lambda at: pl.BlockSpec((COLS, nz, 8, nx), lambda i: (0, 0, at, 0))
    k_edge = lambda at: pl.BlockSpec((nz, 8, nx), lambda i: (0, at, 0))
    f_edge = lambda at: pl.BlockSpec((ARRAYS, DEEP, 8, nx), lambda i: (0, 0, at, 0))
    face = (ARRAYS, nz + 2 * DEEP, 8, nx)
    return pl.pallas_call(
        pack_y_kernel,
        grid=(1,),
        out_shape=[jax.ShapeDtypeStruct(face, F32)] * 2,
        in_specs=[f(at) for f in (b_edge, k_edge, f_edge, f_edge) for at in (0, last)]
        + [pl.BlockSpec(memory_space=pl.ANY)],
        out_specs=[whole(face)] * 2,
        compiler_params=params(16),
        name="pack_y",
    )(block, block, kappa, kappa, first, first, second, second, after)


def outer_kernel(block, kappa, edge, first, second, acc, f0, f1, f2, f3, kz, w, wz):
    nz, ny, _ = kappa.shape
    tiles = ny // 8
    half = sublanes(8) < 4
    acc[...] = jnp.zeros_like(acc)

    def far(i, carry):
        for a in range(ARRAYS):
            upper, lower = sides("gz", first[a, i], second[a, i])
            if a < COLS:
                f0[0, a, i] = lower
                f0[1, a, DEEP - 1 - i] = upper
            else:
                kz[0, i] = lower
                kz[1, DEEP - 1 - i] = upper
        return carry

    lax.fori_loop(0, DEEP, far, 0)
    for i in range(2):
        for c in range(COLS):
            f0[0, c, DEEP + i] = block[c, i]
            f0[1, c, DEEP + i] = block[c, nz - 1 - i]
            for k, f in enumerate((f1, f2, f3)):
                for side in range(2):
                    f[side, c, DEEP + i] = edge[k, side, i, c]
    for i in range(DEEP + 1):
        kz[0, DEEP + i] = kappa[i]
        kz[1, DEEP + i] = kappa[nz - 1 - i]

    def weights(at, carry):
        side, e = at // 8, at % 8
        for t in range(tiles):
            k = kz[side, e, tile(t)]
            right, left = pltpu.roll(k, 127, 1), pltpu.roll(k, 1, 1)
            above = rows_above(kz, (side, e), t, tiles, k)
            below = rows_below(kz, (side, e), t, k)
            far = kz[side, e + 1, tile(t)]
            near = kz[side, jnp.maximum(e - 1, 0), tile(t)]
            w[0, at, tile(t)] = centre(k, (right, left, above, below, far, near))
            w[1, at, tile(t)] = link(k, right, False)
            w[2, at, tile(t)] = link(k, left, False)
            w[3, at, tile(t)] = link(k, above, False)
            wz[at, tile(t)] = link(k, far, True)
        return carry

    lax.fori_loop(0, 16, weights, 0, unroll=2)
    fields = (f0, f1, f2, f3, None)
    for k in range(1, BASIS + 1):
        src, dst = fields[k - 1], fields[k]

        def both(side, carry, k=k, src=src, dst=dst):
            for j in range(DEEP):
                own = j >= DEEP - k
                sums = Sums()

                def step(t):
                    at = side * 8 + j + k
                    ws = tile_weights(w, at, wz, at, at - 1, t)
                    olds, news = [], []
                    for c in range(COLS):
                        v = src[side, c, j + 1, tile(t)]
                        above = rows_above(src, (side, c, j + 1), t, tiles, v)
                        below = rows_below(src, (side, c, j + 1), t, v)
                        far, near = src[side, c, j + 2, tile(t)], src[side, c, j, tile(t)]
                        news.append(apply(v, above, below, far, near, ws))
                        olds.append(v)
                    if dst is not None:
                        for c in range(COLS):
                            dst[side, c, j, tile(t)] = news[c]
                    return olds, news

                first, last = step(0), step(tiles - 1)
                if own:
                    olds, news = (
                        [jnp.where(half, b, a) for a, b in zip(first[i], last[i])] for i in range(2)
                    )
                    sums.products(k, olds, news)
                for t in range(1, tiles - 1):
                    pair = step(t)
                    if own:
                        sums.products(k, *pair)
                sums.flush(acc)
            return carry

        lax.fori_loop(0, 2, both, 0)


def outer(block, kappa, edge, first, second):
    nz, ny, nx = kappa.shape
    return pl.pallas_call(
        outer_kernel,
        out_shape=jax.ShapeDtypeStruct((MOMENTS * NPAIRS, 8, nx), F32),
        in_specs=[VMEM] * 5,
        out_specs=VMEM,
        scratch_shapes=[pltpu.VMEM((2, COLS, DEEP + 2, ny, nx), F32)] * 4
        + [
            pltpu.VMEM((2, 2 * DEEP + 1, ny, nx), F32),
            pltpu.VMEM((4, 16, ny, nx), F32),
            pltpu.VMEM((16, ny, nx), F32),
        ],
        compiler_params=params(24),
        cost_estimate=cost(1 << 27),
        name="outer",
    )(block, kappa, edge, first, second)


def strip_of(planes):
    lane = lanes(8)
    offset, group = lane % PITCH, lane // PITCH
    index = jnp.where(offset < 8, 120 + offset, offset - 8)
    strip = permute_lanes(planes[0], index)
    for g, plane in enumerate(planes[1:]):
        strip = jnp.where(group == g + 1, permute_lanes(plane, index), strip)
    return strip


def strips_kernel(block, kappa, first, second, strip):
    nz, ny, _ = kappa.shape

    def rows(t, carry):
        at = pl.ds(pl.multiple_of(t * 8, 8), 8)
        for a in range(ARRAYS):
            ends = [sides("gz", first[a, i, at], second[a, i, at]) for i in range(DEEP)]

            def plane(z):
                if z < DEEP:
                    return ends[z][1]
                if z >= nz + DEEP:
                    return ends[z - nz - DEEP][0]
                return block[a, z - DEEP, at] if a < COLS else kappa[z - DEEP, at]

            for q in range(SLABS):
                strip[a, q, at] = strip_of([plane(z) for z in range(q, nz + 2 * DEEP, SLABS)])
        return carry

    lax.fori_loop(0, ny // 8, rows, 0)


def strips(block, kappa, first, second):
    nz, ny, nx = kappa.shape
    return pl.pallas_call(
        strips_kernel,
        out_shape=jax.ShapeDtypeStruct((ARRAYS, SLABS, ny, nx), F32),
        in_specs=[VMEM] * 4,
        out_specs=VMEM,
        compiler_params=params(16),
        cost_estimate=cost(1 << 25),
        name="strips",
    )(block, kappa, first, second)


HALVES = [(a, q) for a in range(ARRAYS) for q in range(SLABS)]


def pack_x_kernel(rim, strip, after, side, face):
    depth = rim.shape[1]
    ny = strip.shape[2]
    low = lanes(8) % PITCH < 8
    for a, q in HALVES:
        side[a, q] = strip_of([rim[a, z] for z in range(q, depth, SLABS)])

    def pack(at, get):
        for n in range(0, len(HALVES), 2):
            value = get(*HALVES[n])
            value = jnp.where(upward(), pltpu.roll(value, 120, 1), value)
            if n + 1 < len(HALVES):
                other = get(*HALVES[n + 1])
                value = jnp.where(low, value, jnp.where(upward(), other, pltpu.roll(other, 8, 1)))
            face[n // 2, at] = value

    def rows(t, carry):
        at = pl.ds(pl.multiple_of(t * 8, 8), 8)
        pack(at, lambda a, q: strip[a, q, at])
        return carry

    lax.fori_loop(0, ny // 8, rows, 0, unroll=4)
    pack(slice(ny, ny + 8), lambda a, q: side[a, q])


def pack_x(rim, strip, after):
    _, _, ny, nx = strip.shape
    face = ((len(HALVES) + 1) // 2, ny + 8, nx)
    return pl.pallas_call(
        pack_x_kernel,
        out_shape=[jax.ShapeDtypeStruct(s, F32) for s in ((ARRAYS, SLABS, 8, nx), face)],
        in_specs=[VMEM] * 2 + [pl.BlockSpec(memory_space=pl.ANY)],
        out_specs=[VMEM] * 2,
        compiler_params=params(16),
        name="pack_x",
    )(rim, strip, after)


def y_strip_kernel(kept, rim, acc, g0, g1, g2, g3, kr, w, wz):
    depth = rim.shape[1]
    half = sublanes(8) < 4
    seam = [at_seam("gy") & (sublanes(8) == 7), at_seam("gy") & (sublanes(8) == 0)]
    acc[...] = jnp.zeros_like(acc)

    def fill(z, carry):
        for a in range(ARRAYS):
            below = jnp.where(upward(), kept[a, z], rim[a, z])
            above = jnp.where(upward(), rim[a, z], kept[a, z])
            for t, part in enumerate((below, above)):
                if a < COLS:
                    g0[a, z, tile(t)] = part
                else:
                    kr[z, tile(t)] = part
        return carry

    lax.fori_loop(0, depth, fill, 0, unroll=4)

    def weights(z, carry):
        for t in range(2):
            k = kr[z, tile(t)]
            right, left = pltpu.roll(k, 127, 1), pltpu.roll(k, 1, 1)
            above = rows_above(kr, (z,), t, 2, k)
            below = rows_below(kr, (z,), t, k)
            above = cut(seam[0], above) if t == 0 else above
            below = cut(seam[1], below) if t == 1 else below
            far = kr[z + 1, tile(t)]
            near = kr[jnp.maximum(z - 1, 0), tile(t)]
            w[0, z, tile(t)] = centre(k, (right, left, above, below, far, near))
            w[1, z, tile(t)] = link(k, right, False)
            w[2, z, tile(t)] = link(k, left, False)
            w[3, z, tile(t)] = link(k, above, True)
            wz[z, tile(t)] = link(k, far, True)
        return carry

    lax.fori_loop(0, depth - 1, weights, 0, unroll=4)
    fields = (g0, g1, g2, g3, None)
    for k in range(1, BASIS + 1):
        src, dst = fields[k - 1], fields[k]

        def slab(z, own, k=k, src=src, dst=dst):
            sums = Sums()
            kept = []
            for t in range(2):
                ws = tile_weights(w, z, wz, z, z - 1, t)
                olds, news = [], []
                for c in range(COLS):
                    v = src[c, z, tile(t)]
                    above = rows_above(src, (c, z), t, 2, v)
                    below = rows_below(src, (c, z), t, v)
                    news.append(apply(v, above, below, src[c, z + 1, tile(t)], src[c, z - 1, tile(t)], ws))
                    olds.append(v)
                if dst is not None:
                    for c in range(COLS):
                        dst[c, z, tile(t)] = news[c]
                kept.append((olds, news))
            if own:
                olds, news = (
                    [jnp.where(half, b, a) for a, b in zip(kept[0][i], kept[1][i])] for i in range(2)
                )
                sums.products(k, olds, news)
                sums.flush(acc)

        def far(i, carry, k=k, slab=slab):
            slab(k + i, False)
            slab(depth - DEEP + i, False)
            return carry

        def own(z, carry, slab=slab):
            slab(z, True)
            return carry

        if k < DEEP:
            lax.fori_loop(0, DEEP - k, far, 0, unroll=True)
        lax.fori_loop(DEEP, depth - DEEP, own, 0, unroll=4)


def y_strip(kept, rim):
    _, depth, _, nx = rim.shape
    return pl.pallas_call(
        y_strip_kernel,
        out_shape=jax.ShapeDtypeStruct((MOMENTS * NPAIRS, 8, nx), F32),
        in_specs=[VMEM] * 2,
        out_specs=VMEM,
        scratch_shapes=[pltpu.VMEM((COLS, depth, 16, nx), F32)] * 4
        + [
            pltpu.VMEM((depth, 16, nx), F32),
            pltpu.VMEM((4, depth, 16, nx), F32),
            pltpu.VMEM((depth, 16, nx), F32),
        ],
        compiler_params=params(16),
        cost_estimate=cost(1 << 27),
        name="y_strip",
    )(kept, rim)


def x_strip_kernel(strip, side, face, acc1, acc2, acc3, out, s0, s1, s2, s3, kr, w, wz, acc):
    tiles = face.shape[1] // 8
    offset = lanes(8) % PITCH
    half = sublanes(8) < 4
    right_seam, left_seam = (at_seam("gx") & (offset == at) for at in (7, 8))
    above_seam, below_seam = (at_seam("gy") & (sublanes(8) == at) for at in (7, 0))
    shift = jnp.where(upward(), 0, 1)

    def next_slab(ref, index, q, at):
        if q < SLABS - 1:
            return ref[index + (q + 1, at)]
        return pltpu.roll(ref[index + (0, at)], 128 - PITCH, 1)

    def last_slab(ref, index, q, at):
        if q > 0:
            return ref[index + (q - 1, at)]
        return pltpu.roll(ref[index + (SLABS - 1, at)], PITCH, 1)

    for n, (a, q) in enumerate(HALVES):
        for t in range(tiles):
            own = strip[a, q, tile(t)] if t < tiles - 1 else side[a, q]
            beyond = face[n // 2, tile(t)]
            if n % 2 == 0:
                beyond = jnp.where(upward(), pltpu.roll(beyond, 8, 1), beyond)
            else:
                beyond = jnp.where(upward(), beyond, pltpu.roll(beyond, 120, 1))
            value = jnp.where((offset < 8) == upward(), own, beyond)
            at = t + shift if t < tiles - 1 else (tiles - 1) * (1 - shift)
            at = pl.ds(pl.multiple_of(at * 8, 8), 8)
            if a < COLS:
                s0[a, q, at] = value
            else:
                kr[q, at] = value

    for q in range(SLABS):
        for t in range(tiles):
            k = kr[q, tile(t)]
            right, left = cut(right_seam, pltpu.roll(k, 127, 1)), cut(left_seam, pltpu.roll(k, 1, 1))
            above = rows_above(kr, (q,), t, tiles, k)
            below = rows_below(kr, (q,), t, k)
            if t == 0 or t == tiles - 2:
                above = cut(above_seam & (upward() == (t > 0)), above)
            if t == 1 or t == tiles - 1:
                below = cut(below_seam & (upward() == (t > 1)), below)
            far, near = next_slab(kr, (), q, tile(t)), last_slab(kr, (), q, tile(t))
            w[0, q, tile(t)] = centre(k, (right, left, above, below, far, near))
            w[1, q, tile(t)] = link(k, right, True)
            w[2, q, tile(t)] = link(k, left, True)
            w[3, q, tile(t)] = link(k, above, True)
            wz[q + 1, tile(t)] = link(k, far, True)
            if q == 0:
                wz[0, tile(t)] = link(k, near, True)
    acc[...] = jnp.zeros_like(acc)
    fields = (s0, s1, s2, s3, None)
    for k in range(1, BASIS + 1):
        src, dst = fields[k - 1], fields[k]

        def slab(q):
            sums = Sums()

            def step(t):
                ws = tile_weights(w, q, wz, q + 1, q, t)
                olds, news = [], []
                for c in range(COLS):
                    v = src[c, q, tile(t)]
                    above = rows_above(src, (c, q), t, tiles, v)
                    below = rows_below(src, (c, q), t, v)
                    far, near = next_slab(src, (c,), q, tile(t)), last_slab(src, (c,), q, tile(t))
                    news.append(apply(v, above, below, far, near, ws))
                    olds.append(v)
                if dst is not None:
                    for c in range(COLS):
                        dst[c, q, tile(t)] = news[c]
                return olds, news

            first, last = step(0), step(tiles - 1)
            olds, news = (
                [jnp.where(half, b, a) for a, b in zip(first[i], last[i])] for i in range(2)
            )
            sums.products(k, olds, news)
            for t in range(1, tiles - 1):
                sums.products(k, *step(t))
            sums.flush(acc.at[q])

        for q in range(SLABS):
            slab(q)

    lane1 = lax.broadcasted_iota(jnp.int32, (1, 128), 1)
    z = lane1 // PITCH * SLABS
    here = (lane1 % PITCH >= DEEP) & (lane1 % PITCH < PITCH - DEEP)
    groups = 128 // PITCH
    total = jnp.where(
        (lane1 >= DEEP) & (lane1 < 128 - DEEP), jnp.sum(acc1[...] + acc2[...] + acc3[...], axis=1), 0.0
    )
    for q in range(SLABS):
        kept = here & (z + q >= DEEP) & (z + q < groups * SLABS - DEEP)
        total = total + jnp.where(kept, jnp.sum(acc[q], axis=1), 0.0)
    total = jnp.concatenate([total, jnp.zeros((128 - total.shape[0], 128), F32)], 0)
    row = lax.dot_general(
        jnp.ones((8, 128), F32),
        total,
        (((1,), (1,)), ((), ())),
        precision=lax.Precision.HIGHEST,
        preferred_element_type=F32,
    )
    out[...] = jnp.broadcast_to(row[0:1][None], out.shape)


def x_strip(strip, side, face, accs, peers):
    _, slabs, ny, nx = strip.shape
    laid = (slabs, ny + 8, nx)
    return pl.pallas_call(
        x_strip_kernel,
        out_shape=jax.ShapeDtypeStruct((peers, 1, 128), F32),
        in_specs=[VMEM] * 6,
        out_specs=VMEM,
        scratch_shapes=[pltpu.VMEM((COLS,) + laid, F32)] * 4
        + [
            pltpu.VMEM(laid, F32),
            pltpu.VMEM((4,) + laid, F32),
            pltpu.VMEM((slabs + 1,) + laid[1:], F32),
            pltpu.VMEM((slabs, MOMENTS * NPAIRS, 8, nx), F32),
        ],
        compiler_params=params(16),
        name="x_strip",
    )(strip, side, face, *accs)


def factor(row, triangle, coef):
    lane, sub = lanes(8), sublanes(8)
    blocks = (KRYLOV + 7) // 8
    columns = []
    for b in range(KRYLOV):
        parts = []
        for i in range(blocks):
            a = sub + 8 * i
            low, high = jnp.minimum(a % COLS, b % COLS), jnp.maximum(a % COLS, b % COLS)
            pair = low * COLS - (low * (low - 1)) // 2 + high - low
            index = jnp.where(a < KRYLOV, (a // COLS + b // COLS) * NPAIRS + pair, 127)
            parts.append(permute_lanes(row, index))
        columns.append(parts)
    at = 0
    for k in range(KRYLOV):
        i, j = k // 8, k % 8

        def entry(b):
            return jnp.broadcast_to(columns[b][i][j : j + 1], (8, 128))

        pivot = entry(k)
        inverse = 1.0 / pivot
        root = jnp.sqrt(pivot)
        scale = 1.0 / root
        line = jnp.where(lane == k, root, 0.0)
        if k < COLS:
            coef[at] = scale
            at += 1
        for b in range(k + 1, KRYLOV):
            value = entry(b)
            line = jnp.where(lane == b, value * scale, line)
            if b < COLS:
                coef[at] = value * scale
                at += 1
            value = value * inverse
            for n in range((k + 1) // 8, blocks):
                columns[b][n] = columns[b][n] - columns[k][n] * value
        triangle[k : k + 1, :] = line[0:1, 0:KRYLOV]


def finish_kernel(ncells, parts, block, ortho, triangle, coef):
    step = pl.program_id(0)

    @pl.when(step == 0)
    def _():
        row = jnp.sum(parts[...], axis=0) * (1.0 / ncells)
        factor(jnp.broadcast_to(row, (8, 128)), triangle, coef)

    u = {}
    for i in range(COLS):
        for j in range(i, COLS):
            u[i, j] = coef[len(u)]
    slabs = ortho.shape[1]

    def slab(z, carry):
        for t in range(ortho.shape[2] // 8):
            done = []
            for j in range(COLS):
                value = block[j, step * slabs + z, tile(t)]
                for i in range(j):
                    value = value - u[i, j] * done[i]
                value = value * u[j, j]
                ortho[j, z, tile(t)] = value
                done.append(value)
        return carry

    lax.fori_loop(0, slabs, slab, 0, unroll=2)


def finish(parts, block, ncells):
    cols, nz, ny, nx = block.shape
    steps = 4
    piece = pl.BlockSpec((cols, nz // steps, ny, nx), lambda i: (0, i, 0, 0))
    return pl.pallas_call(
        lambda *refs: finish_kernel(ncells, *refs),
        grid=(steps,),
        out_shape=[
            jax.ShapeDtypeStruct(block.shape, F32),
            jax.ShapeDtypeStruct((KRYLOV, KRYLOV), F32),
        ],
        in_specs=[pl.BlockSpec(parts.shape, lambda i: (0, 0, 0)), VMEM],
        out_specs=[piece, pl.BlockSpec((KRYLOV, KRYLOV), lambda i: (0, 0))],
        scratch_shapes=[pltpu.VMEM((NPAIRS, 8, 128), F32)],
        compiler_params=params(16),
        name="finish",
    )(parts, block)


def shards(block, kappa):
    axes = ("gx", "gy", "gz")
    peers = lax.axis_size(axes)
    ncells = float(kappa.size * peers)
    far = [pltpu.with_memory_space_constraint(value, pltpu.HBM) for value in (block, kappa)]
    first, second = swap(*pack_z(*far), "gz")
    acc1, edge = inner(block, kappa)
    kept, face = pack_y(block, kappa, first, second, acc1)
    rim = pull(face, "gy")
    strip = strips(block, kappa, first, second)
    acc2 = outer(block, kappa, edge, first, second)
    side, face = pack_x(rim, strip, acc2)
    face = pull(face, "gx")
    acc3 = y_strip(kept, rim)
    moments = x_strip(strip, side, face, (acc1, acc2, acc3), peers)
    parts = lax.all_to_all(moments, axes, 0, 0, tiled=True)
    return tuple(finish(parts, block, ncells))


def solution(mesh):
    return jax.shard_map(
        shards,
        mesh=mesh,
        in_specs=(P(None, "gz", "gy", "gx"), P("gz", "gy", "gx")),
        out_specs=(P(None, "gz", "gy", "gx"), P()),
        check_vma=False,
    )
```

```python
import jax
import jax.numpy as jnp
import numpy as np
from jax import lax
from jax.experimental import pallas as pl
from jax.experimental.pallas import tpu as pltpu
from jax.sharding import PartitionSpec as P

COLS = 4
BASIS = 4
KRYLOV = 20
MOMENTS = 2 * BASIS + 1
PAIRS = [(c, d) for c in range(COLS) for d in range(c, COLS)]
NPAIRS = len(PAIRS)
DEEP = BASIS
ARRAYS = COLS + 1
PITCH = 4 * DEEP
SLABS = 3

basis_shift = 6.0
basis_scale = 3.0

F32 = jnp.float32
VMEM = pl.BlockSpec(memory_space=pltpu.VMEM)
HBM = pl.BlockSpec(memory_space=pltpu.HBM)


def params(mib):
    return pltpu.CompilerParams(vmem_limit_bytes=mib * 1024 * 1024)


def cost(flops):
    return pl.CostEstimate(flops=flops, bytes_accessed=1 << 20, transcendentals=0)


def lanes(rows):
    return lax.broadcasted_iota(jnp.int32, (rows, 128), 1)


def sublanes(rows):
    return lax.broadcasted_iota(jnp.int32, (rows, 128), 0)


def permute_lanes(value, index):
    return jnp.take_along_axis(value, index, axis=1, mode="promise_in_bounds")


def even_first(axis, first, second):
    return jnp.where(lax.axis_index(axis) % 2 == 0, first, second)


def sides(axis, first, second):
    at = lax.axis_index(axis)
    upper = jnp.where(at == lax.axis_size(axis) - 1, 0.0, even_first(axis, first, second))
    lower = jnp.where(at == 0, 0.0, even_first(axis, second, first))
    return upper, lower


def swap(first, second, axis):
    peers = lax.axis_size(axis)
    other = [(i, (i - 1 if i % 2 == 0 else i + 1) % peers) for i in range(peers)]
    second = lax.ppermute(second, axis, other)
    first = lax.ppermute(first, axis, [(i, i ^ 1) for i in range(peers)])
    return first, second


def upward():
    return lax.axis_index("gz") % 2 == 0


def pull(face, *axes):
    sizes = [lax.axis_size(axis) for axis in axes] + [lax.axis_size("gz")]
    pairs = []
    for at in np.ndindex(*sizes):
        step = -1 if at[-1] % 2 == 0 else 1
        to = [(i + step) % size for i, size in zip(at[:-1], sizes)] + [at[-1]]
        pairs.append(tuple(int(np.ravel_multi_index(place, sizes)) for place in (at, to)))
    return lax.ppermute(face, (*axes, "gz"), pairs)


def at_seam(axis):
    at = lax.axis_index(axis)
    return at == jnp.where(upward(), lax.axis_size(axis) - 1, 0)


def cut(there, value):
    return jnp.where(there, 0.0, value)


def link(one, other, bounded):
    weight = (one + other) * (0.5 / basis_scale)
    if bounded:
        weight = jnp.where(jnp.minimum(one, other) > 0.0, weight, 0.0)
    return weight


def centre(k, others):
    total = 6.0 * k
    for other in others:
        total = total + other
    return total * (0.5 / basis_scale) - basis_shift / basis_scale


def rows_above(ref, index, t, tiles, value):
    if t == tiles - 1:
        return pltpu.roll(value, 7, 0)
    return ref[index + (slice(8 * t + 1, 8 * t + 9),)]


def rows_below(ref, index, t, value):
    if t == 0:
        return pltpu.roll(value, 1, 0)
    return ref[index + (slice(8 * t - 1, 8 * t + 7),)]


def tile(t):
    return slice(8 * t, 8 * t + 8)


class Sums:
    def __init__(self):
        self.held = {}

    def add(self, at, term):
        self.held[at] = self.held[at] + term if at in self.held else term

    def products(self, k, olds, news):
        for p, (c, d) in enumerate(PAIRS):
            if k == 1:
                self.add(p, olds[c] * olds[d])
            self.add((2 * k - 1) * NPAIRS + p, olds[c] * news[d])
            self.add(2 * k * NPAIRS + p, news[c] * news[d])

    def flush(self, acc):
        for at, total in self.held.items():
            acc[at] += total


def apply(v, above, below, far, near, w):
    new = w[0] * v
    new -= w[1] * pltpu.roll(v, 127, 1)
    new -= w[2] * pltpu.roll(v, 1, 1)
    new -= w[3] * above
    new -= w[4] * below
    new -= w[5] * far
    new -= w[6] * near
    return new


def tile_weights(w, q, wz, far, near, t):
    c0, right, left, above = (w[i, q, tile(t)] for i in range(4))
    below = rows_below(w, (3, q), t, above)
    return c0, right, left, above, below, wz[far, tile(t)], wz[near, tile(t)]


def pack_z_kernel(block, kappa, to_first, to_second, sems):
    nz = kappa.shape[0]
    high = nz - DEEP
    even = lax.axis_index("gz") % 2 == 0
    copies = []
    for i, (out, at) in enumerate(
        ((to_second, jnp.where(even, 0, high)), (to_first, jnp.where(even, high, 0)))
    ):
        copies.append(pltpu.make_async_copy(block.at[:, pl.ds(at, DEEP)], out.at[0:COLS], sems.at[2 * i]))
        copies.append(pltpu.make_async_copy(kappa.at[pl.ds(at, DEEP)], out.at[COLS], sems.at[2 * i + 1]))
    for copy in copies:
        copy.start()
    for copy in copies:
        copy.wait()


def pack_z(block, kappa):
    nz, ny, nx = kappa.shape
    face = jax.ShapeDtypeStruct((ARRAYS, DEEP, ny, nx), F32)
    return pl.pallas_call(
        pack_z_kernel,
        out_shape=[face, face],
        in_specs=[HBM, HBM],
        out_specs=[VMEM] * 2,
        scratch_shapes=[pltpu.SemaphoreType.DMA((4,))],
        compiler_params=params(8),
        name="pack_z",
    )(block, kappa)


def inner_kernel(block, kappa, acc, edge, p1, p2, p3, w, wz):
    nz, ny, _ = kappa.shape
    tiles = ny // 8
    half = sublanes(8) < 4
    acc[...] = jnp.zeros_like(acc)

    def weights(z, carry):
        for t in range(tiles):
            k = kappa[z, tile(t)]
            right, left = pltpu.roll(k, 127, 1), pltpu.roll(k, 1, 1)
            above = rows_above(kappa, (z,), t, tiles, k)
            below = rows_below(kappa, (z,), t, k)
            far = kappa[z + 1, tile(t)]
            near = kappa[jnp.maximum(z - 1, 0), tile(t)]
            w[0, z, tile(t)] = centre(k, (right, left, above, below, far, near))
            w[1, z, tile(t)] = link(k, right, False)
            w[2, z, tile(t)] = link(k, left, False)
            w[3, z, tile(t)] = link(k, above, False)
            wz[z, tile(t)] = link(k, far, False)
        return carry

    lax.fori_loop(0, nz - 1, weights, 0, unroll=5)
    fields = (block, p1, p2, p3, None)
    for k in range(1, BASIS + 1):
        src, dst = fields[k - 1], fields[k]

        def slab(z, carry, k=k, src=src, dst=dst):
            sums = Sums()

            def step(t):
                ws = tile_weights(w, z, wz, z, z - 1, t)
                olds, news = [], []
                for c in range(COLS):
                    v = src[c, z, tile(t)]
                    above = rows_above(src, (c, z), t, tiles, v)
                    below = rows_below(src, (c, z), t, v)
                    news.append(apply(v, above, below, src[c, z + 1, tile(t)], src[c, z - 1, tile(t)], ws))
                    olds.append(v)
                if dst is not None:
                    for c in range(COLS):
                        dst[c, z, tile(t)] = news[c]
                return olds, news

            first, last = step(0), step(tiles - 1)
            olds, news = (
                [jnp.where(half, b, a) for a, b in zip(first[i], last[i])] for i in range(2)
            )
            sums.products(k, olds, news)
            for t in range(1, tiles - 1):
                sums.products(k, *step(t))
            sums.flush(acc)
            return carry

        lax.fori_loop(k, nz - k, slab, 0, unroll=(nz - 2 * k + 1) // 2)
        if dst is not None:
            for i in range(2):
                edge[k - 1, 0, i] = dst[:, k + i]
                edge[k - 1, 1, i] = dst[:, nz - 1 - k - i]


def inner(block, kappa):
    nz, ny, nx = kappa.shape
    return pl.pallas_call(
        inner_kernel,
        out_shape=[
            jax.ShapeDtypeStruct((MOMENTS * NPAIRS, 8, nx), F32),
            jax.ShapeDtypeStruct((BASIS - 1, 2, 2, COLS, ny, nx), F32),
        ],
        in_specs=[VMEM] * 2,
        out_specs=[VMEM] * 2,
        scratch_shapes=[pltpu.VMEM(block.shape, F32)] * 3
        + [pltpu.VMEM((4, nz, ny, nx), F32), pltpu.VMEM((nz, ny, nx), F32)],
        compiler_params=params(24),
        cost_estimate=cost(1 << 28),
        name="inner",
    )(block, kappa)


def strip_of(planes):
    lane = lanes(8)
    offset, group = lane % PITCH, lane // PITCH
    index = jnp.where(offset < 8, 120 + offset, offset - 8)
    strip = None
    for g, plane in enumerate(planes):
        if plane is not None:
            value = permute_lanes(plane, index)
            strip = value if strip is None else jnp.where(group == g, value, strip)
    return strip


def pack_halves(one, other):
    value = jnp.where(upward(), pltpu.roll(one, 120, 1), one)
    if other is None:
        return value
    low = lanes(8) % PITCH < 8
    return jnp.where(low, value, jnp.where(upward(), other, pltpu.roll(other, 8, 1)))


HALVES = [(a, q) for a in range(ARRAYS) for q in range(SLABS)]
DUOS = [HALVES[n : n + 2] for n in range(0, len(HALVES), 2)]
FAR = 2 * DEEP


def pack_duo(duo, get):
    return pack_halves(get(*duo[0]), get(*duo[1]) if len(duo) > 1 else None)


def faces_kernel(block, kappa, strip, x_face, y_face, y_kept):
    nz, ny, _ = kappa.shape

    def rows(t, carry):
        at = pl.ds(pl.multiple_of(t * 8, 8), 8)

        def plane(a, z):
            if z < 0 or z >= nz:
                return None
            return block[a, z, at] if a < COLS else kappa[z, at]

        held = {}
        for a, q in HALVES:
            held[a, q] = strip_of([plane(a, z - DEEP) for z in range(q, nz + FAR, SLABS)])
            strip[a, q, at] = held[a, q]
        for n, duo in enumerate(DUOS):
            x_face[n, at] = pack_duo(duo, lambda a, q: held[a, q])
        return carry

    lax.fori_loop(0, ny // 8, rows, 0, unroll=2)

    def slabs(z, carry):
        for a in range(ARRAYS):
            low, high = (block[a, z, at] if a < COLS else kappa[z, at] for at in (slice(0, 8), slice(ny - 8, ny)))
            y_face[a, z] = jnp.where(upward(), low, high)
            y_kept[a, z] = jnp.where(upward(), high, low)
        return carry

    lax.fori_loop(0, nz, slabs, 0, unroll=4)


def faces(block, kappa):
    nz, ny, nx = kappa.shape
    shapes = ((ARRAYS, SLABS, ny, nx), (len(DUOS), ny, nx), (ARRAYS, nz, 8, nx), (ARRAYS, nz, 8, nx))
    return pl.pallas_call(
        faces_kernel,
        out_shape=[jax.ShapeDtypeStruct(shape, F32) for shape in shapes],
        in_specs=[VMEM] * 2,
        out_specs=[VMEM] * 4,
        compiler_params=params(16),
        cost_estimate=cost(1 << 24),
        name="faces",
    )(block, kappa)


def far_y_kernel(f_low, f_high, s_low, s_high, after, face, kept):
    def slabs(i, carry):
        for a in range(ARRAYS):
            low = sides("gz", f_low[a, i], s_low[a, i])
            high = sides("gz", f_high[a, i], s_high[a, i])
            for at, which in ((i, 1), (DEEP + i, 0)):
                face[a, at] = jnp.where(upward(), low[which], high[which])
                kept[a, at] = jnp.where(upward(), high[which], low[which])
        return carry

    lax.fori_loop(0, DEEP, slabs, 0, unroll=2)


def far_y(first, second, after):
    _, _, ny, nx = first.shape
    last = ny // 8 - 1
    whole = lambda shape: pl.BlockSpec(shape, lambda i: (0,) * len(shape))
    edge = lambda at: pl.BlockSpec((ARRAYS, DEEP, 8, nx), lambda i: (0, 0, at, 0))
    shape = (ARRAYS, FAR, 8, nx)
    return pl.pallas_call(
        far_y_kernel,
        grid=(1,),
        out_shape=[jax.ShapeDtypeStruct(shape, F32)] * 2,
        in_specs=[edge(0), edge(last), edge(0), edge(last), pl.BlockSpec(memory_space=pl.ANY)],
        out_specs=[whole(shape)] * 2,
        compiler_params=params(16),
        name="far_y",
    )(first, first, second, second, after)


def far_strips_kernel(first, second, after, strip):
    def rows(t, carry):
        at = pl.ds(pl.multiple_of(t * 8, 8), 8)
        for a in range(ARRAYS):
            uppers, lowers = zip(*[sides("gz", first[a, i, at], second[a, i, at]) for i in range(DEEP)])
            strip[a, at] = strip_of(lowers + uppers)
        return carry

    lax.fori_loop(0, strip.shape[1] // 8, rows, 0, unroll=2)


def far_strips(first, second, after):
    _, _, ny, nx = first.shape
    return pl.pallas_call(
        far_strips_kernel,
        out_shape=jax.ShapeDtypeStruct((ARRAYS, ny, nx), F32),
        in_specs=[VMEM] * 2 + [pl.BlockSpec(memory_space=pl.ANY)],
        out_specs=VMEM,
        compiler_params=params(16),
        cost_estimate=cost(1 << 23),
        name="far_strips",
    )(first, second, after)


def far_pairs():
    return [(n, n + 1 if n + 1 < ARRAYS else None) for n in range(0, ARRAYS, 2)]


def pack_x_kernel(own_face, rim, far_strip, side, face, corner):
    nz = rim.shape[1]
    tiles = far_strip.shape[1] // 8

    def plane(a, z):
        return rim[a, z] if 0 <= z < nz else None

    def far_tile(a, t):
        return None if a is None else far_strip[a, tile(t)]

    for n in range(len(DUOS)):
        for t in range(tiles):
            face[n * tiles + t] = own_face[n, tile(t)]
    at = len(DUOS) * tiles
    for n, (one, other) in enumerate(far_pairs()):
        packed = [pack_halves(far_tile(one, t), far_tile(other, t)) for t in range(tiles)]
        for t in range(tiles):
            face[at + n * tiles + t] = packed[t]
        corner[n] = jnp.where(upward(), packed[0], packed[tiles - 1])
    at += len(far_pairs()) * tiles
    for a, q in HALVES:
        side[a, q] = strip_of([plane(a, z - DEEP) for z in range(q, nz + FAR, SLABS)])
    for n, duo in enumerate(DUOS):
        face[at + n] = pack_duo(duo, lambda a, q: side[a, q])


def pack_x(own_face, rim, far_strip):
    _, ny, nx = far_strip.shape
    count = (len(DUOS) + len(far_pairs())) * ny // 8 + len(DUOS)
    shapes = ((ARRAYS, SLABS, 8, nx), (count, 8, nx), (len(far_pairs()), 8, nx))
    return pl.pallas_call(
        pack_x_kernel,
        out_shape=[jax.ShapeDtypeStruct(shape, F32) for shape in shapes],
        in_specs=[VMEM] * 3,
        out_specs=[VMEM] * 3,
        compiler_params=params(16),
        name="pack_x",
    )(own_face, rim, far_strip)


def outer_kernel(block, kappa, edge, first, second, after, acc, f0, f1, f2, f3, kz, w, wz):
    nz, ny, _ = kappa.shape
    tiles = ny // 8
    half = sublanes(8) < 4
    acc[...] = jnp.zeros_like(acc)

    def far(i, carry):
        for a in range(ARRAYS):
            upper, lower = sides("gz", first[a, i], second[a, i])
            if a < COLS:
                f0[0, a, i] = lower
                f0[1, a, DEEP - 1 - i] = upper
            else:
                kz[0, i] = lower
                kz[1, DEEP - 1 - i] = upper
        return carry

    lax.fori_loop(0, DEEP, far, 0)
    for i in range(2):
        for c in range(COLS):
            f0[0, c, DEEP + i] = block[c, i]
            f0[1, c, DEEP + i] = block[c, nz - 1 - i]
            for k, f in enumerate((f1, f2, f3)):
                for side in range(2):
                    f[side, c, DEEP + i] = edge[k, side, i, c]
    for i in range(DEEP + 1):
        kz[0, DEEP + i] = kappa[i]
        kz[1, DEEP + i] = kappa[nz - 1 - i]

    def weights(at, carry):
        side, e = at // 8, at % 8
        for t in range(tiles):
            k = kz[side, e, tile(t)]
            right, left = pltpu.roll(k, 127, 1), pltpu.roll(k, 1, 1)
            above = rows_above(kz, (side, e), t, tiles, k)
            below = rows_below(kz, (side, e), t, k)
            far = kz[side, e + 1, tile(t)]
            near = kz[side, jnp.maximum(e - 1, 0), tile(t)]
            w[0, at, tile(t)] = centre(k, (right, left, above, below, far, near))
            w[1, at, tile(t)] = link(k, right, False)
            w[2, at, tile(t)] = link(k, left, False)
            w[3, at, tile(t)] = link(k, above, False)
            wz[at, tile(t)] = link(k, far, True)
        return carry

    lax.fori_loop(0, 16, weights, 0, unroll=4)
    fields = (f0, f1, f2, f3, None)
    for k in range(1, BASIS + 1):
        src, dst = fields[k - 1], fields[k]

        def both(side, carry, k=k, src=src, dst=dst):
            for j in range(DEEP):
                own = j >= DEEP - k
                sums = Sums()

                def step(t):
                    at = side * 8 + j + k
                    ws = tile_weights(w, at, wz, at, at - 1, t)
                    olds, news = [], []
                    for c in range(COLS):
                        v = src[side, c, j + 1, tile(t)]
                        above = rows_above(src, (side, c, j + 1), t, tiles, v)
                        below = rows_below(src, (side, c, j + 1), t, v)
                        far, near = src[side, c, j + 2, tile(t)], src[side, c, j, tile(t)]
                        news.append(apply(v, above, below, far, near, ws))
                        olds.append(v)
                    if dst is not None:
                        for c in range(COLS):
                            dst[side, c, j, tile(t)] = news[c]
                    return olds, news

                first, last = step(0), step(tiles - 1)
                if own:
                    olds, news = (
                        [jnp.where(half, b, a) for a, b in zip(first[i], last[i])] for i in range(2)
                    )
                    sums.products(k, olds, news)
                for t in range(1, tiles - 1):
                    pair = step(t)
                    if own:
                        sums.products(k, *pair)
                sums.flush(acc)
            return carry

        lax.fori_loop(0, 2, both, 0)


def outer(block, kappa, edge, first, second, after):
    nz, ny, nx = kappa.shape
    return pl.pallas_call(
        outer_kernel,
        out_shape=jax.ShapeDtypeStruct((MOMENTS * NPAIRS, 8, nx), F32),
        in_specs=[VMEM] * 5 + [pl.BlockSpec(memory_space=pl.ANY)],
        out_specs=VMEM,
        scratch_shapes=[pltpu.VMEM((2, COLS, DEEP + 2, ny, nx), F32)] * 4
        + [
            pltpu.VMEM((2, 2 * DEEP + 1, ny, nx), F32),
            pltpu.VMEM((4, 16, ny, nx), F32),
            pltpu.VMEM((16, ny, nx), F32),
        ],
        compiler_params=params(24),
        cost_estimate=cost(1 << 27),
        name="outer",
    )(block, kappa, edge, first, second, after)


def y_strip_kernel(kept, far_kept, rim, far_rim, acc, g0, g1, g2, g3, kr, w, wz):
    nz = rim.shape[1]
    depth = nz + FAR
    half = sublanes(8) < 4
    seam = [at_seam("gy") & (sublanes(8) == 7), at_seam("gy") & (sublanes(8) == 0)]
    acc[...] = jnp.zeros_like(acc)

    def lay(z, kept, rim, at):
        for a in range(ARRAYS):
            below = jnp.where(upward(), kept[a, at], rim[a, at])
            above = jnp.where(upward(), rim[a, at], kept[a, at])
            for t, part in enumerate((below, above)):
                if a < COLS:
                    g0[a, z, tile(t)] = part
                else:
                    kr[z, tile(t)] = part

    def fill(z, carry):
        lay(z + DEEP, kept, rim, z)
        return carry

    def fill_far(i, carry):
        lay(i, far_kept, far_rim, i)
        lay(nz + DEEP + i, far_kept, far_rim, DEEP + i)
        return carry

    lax.fori_loop(0, nz, fill, 0, unroll=4)
    lax.fori_loop(0, DEEP, fill_far, 0, unroll=2)

    def weights(z, carry):
        for t in range(2):
            k = kr[z, tile(t)]
            right, left = pltpu.roll(k, 127, 1), pltpu.roll(k, 1, 1)
            above = rows_above(kr, (z,), t, 2, k)
            below = rows_below(kr, (z,), t, k)
            above = cut(seam[0], above) if t == 0 else above
            below = cut(seam[1], below) if t == 1 else below
            far = kr[z + 1, tile(t)]
            near = kr[jnp.maximum(z - 1, 0), tile(t)]
            w[0, z, tile(t)] = centre(k, (right, left, above, below, far, near))
            w[1, z, tile(t)] = link(k, right, False)
            w[2, z, tile(t)] = link(k, left, False)
            w[3, z, tile(t)] = link(k, above, True)
            wz[z, tile(t)] = link(k, far, True)
        return carry

    lax.fori_loop(0, depth - 1, weights, 0, unroll=4)
    fields = (g0, g1, g2, g3, None)
    for k in range(1, BASIS + 1):
        src, dst = fields[k - 1], fields[k]

        def slab(z, own, k=k, src=src, dst=dst):
            sums = Sums()
            kept = []
            for t in range(2):
                ws = tile_weights(w, z, wz, z, z - 1, t)
                olds, news = [], []
                for c in range(COLS):
                    v = src[c, z, tile(t)]
                    above = rows_above(src, (c, z), t, 2, v)
                    below = rows_below(src, (c, z), t, v)
                    news.append(apply(v, above, below, src[c, z + 1, tile(t)], src[c, z - 1, tile(t)], ws))
                    olds.append(v)
                if dst is not None:
                    for c in range(COLS):
                        dst[c, z, tile(t)] = news[c]
                kept.append((olds, news))
            if own:
                olds, news = (
                    [jnp.where(half, b, a) for a, b in zip(kept[0][i], kept[1][i])] for i in range(2)
                )
                sums.products(k, olds, news)
                sums.flush(acc)

        def far(i, carry, k=k, slab=slab):
            slab(k + i, False)
            slab(depth - DEEP + i, False)
            return carry

        def own(z, carry, slab=slab):
            slab(z, True)
            return carry

        if k < DEEP:
            lax.fori_loop(0, DEEP - k, far, 0, unroll=True)
        lax.fori_loop(DEEP, depth - DEEP, own, 0, unroll=16)


def y_strip(kept, far_kept, rim, far_rim):
    _, nz, _, nx = rim.shape
    depth = nz + FAR
    return pl.pallas_call(
        y_strip_kernel,
        out_shape=jax.ShapeDtypeStruct((MOMENTS * NPAIRS, 8, nx), F32),
        in_specs=[VMEM] * 4,
        out_specs=VMEM,
        scratch_shapes=[pltpu.VMEM((COLS, depth, 16, nx), F32)] * 4
        + [
            pltpu.VMEM((depth, 16, nx), F32),
            pltpu.VMEM((4, depth, 16, nx), F32),
            pltpu.VMEM((depth, 16, nx), F32),
        ],
        compiler_params=params(16),
        cost_estimate=cost(1 << 27),
        name="y_strip",
    )(kept, far_kept, rim, far_rim)


def x_strip_kernel(strip, side, far_strip, far_rim, face, corner, acc1, acc2, acc3, out, s0, s1, s2, s3, kr, w, wz, acc):
    tiles = strip.shape[2] // 8 + 1
    lane = lanes(8)
    offset = lane % PITCH
    half = sublanes(8) < 4
    right_seam, left_seam = (at_seam("gx") & (offset == at) for at in (7, 8))
    above_seam, below_seam = (at_seam("gy") & (sublanes(8) == at) for at in (7, 0))
    shift = jnp.where(upward(), 0, 1)

    def next_slab(ref, index, q, at):
        if q < SLABS - 1:
            return ref[index + (q + 1, at)]
        return pltpu.roll(ref[index + (0, at)], 128 - PITCH, 1)

    def last_slab(ref, index, q, at):
        if q > 0:
            return ref[index + (q - 1, at)]
        return pltpu.roll(ref[index + (SLABS - 1, at)], PITCH, 1)

    own_side = (offset < 8) == upward()
    depth = 128 // PITCH * SLABS
    far_at = len(DUOS) * (tiles - 1)
    rim_at = far_at + len(far_pairs()) * (tiles - 1)
    far_side = [strip_of([far_rim[a, i] for i in range(FAR)]) for a in range(ARRAYS)]
    for n, (a, q) in enumerate(HALVES):
        z = lane // PITCH * SLABS + q
        far = (z < DEEP) | (z >= depth - DEEP)
        index = jnp.where(z < DEEP, z, jnp.where(far, z - (depth - FAR), 0)) * PITCH
        for t in range(tiles):
            own = strip[a, q, tile(t)] if t < tiles - 1 else side[a, q]
            beyond = face[n // 2 * (tiles - 1) + t] if t < tiles - 1 else face[rim_at + n // 2]
            if n % 2 == 0:
                beyond = jnp.where(upward(), pltpu.roll(beyond, 8, 1), beyond)
            else:
                beyond = jnp.where(upward(), beyond, pltpu.roll(beyond, 120, 1))
            far_own = far_strip[a, tile(t)] if t < tiles - 1 else far_side[a]
            far_beyond = face[far_at + a // 2 * (tiles - 1) + t] if t < tiles - 1 else corner[a // 2]
            far_own = permute_lanes(far_own, index + offset)
            far_beyond = permute_lanes(far_beyond, index + offset % 8 + 8 * (a % 2))
            value = jnp.where(own_side, jnp.where(far, far_own, own), jnp.where(far, far_beyond, beyond))
            at = t + shift if t < tiles - 1 else (tiles - 1) * (1 - shift)
            at = pl.ds(pl.multiple_of(at * 8, 8), 8)
            if a < COLS:
                s0[a, q, at] = value
            else:
                kr[q, at] = value

    for q in range(SLABS):
        for t in range(tiles):
            k = kr[q, tile(t)]
            right, left = cut(right_seam, pltpu.roll(k, 127, 1)), cut(left_seam, pltpu.roll(k, 1, 1))
            above = rows_above(kr, (q,), t, tiles, k)
            below = rows_below(kr, (q,), t, k)
            if t == 0 or t == tiles - 2:
                above = cut(above_seam & (upward() == (t > 0)), above)
            if t == 1 or t == tiles - 1:
                below = cut(below_seam & (upward() == (t > 1)), below)
            far, near = next_slab(kr, (), q, tile(t)), last_slab(kr, (), q, tile(t))
            w[0, q, tile(t)] = centre(k, (right, left, above, below, far, near))
            w[1, q, tile(t)] = link(k, right, True)
            w[2, q, tile(t)] = link(k, left, True)
            w[3, q, tile(t)] = link(k, above, True)
            wz[q + 1, tile(t)] = link(k, far, True)
            if q == 0:
                wz[0, tile(t)] = link(k, near, True)
    acc[...] = jnp.zeros_like(acc)
    fields = (s0, s1, s2, s3, None)
    for k in range(1, BASIS + 1):
        src, dst = fields[k - 1], fields[k]

        def slab(q):
            sums = Sums()

            def step(t):
                ws = tile_weights(w, q, wz, q + 1, q, t)
                olds, news = [], []
                for c in range(COLS):
                    v = src[c, q, tile(t)]
                    above = rows_above(src, (c, q), t, tiles, v)
                    below = rows_below(src, (c, q), t, v)
                    far, near = next_slab(src, (c,), q, tile(t)), last_slab(src, (c,), q, tile(t))
                    news.append(apply(v, above, below, far, near, ws))
                    olds.append(v)
                if dst is not None:
                    for c in range(COLS):
                        dst[c, q, tile(t)] = news[c]
                return olds, news

            first, last = step(0), step(tiles - 1)
            olds, news = (
                [jnp.where(half, b, a) for a, b in zip(first[i], last[i])] for i in range(2)
            )
            sums.products(k, olds, news)
            for t in range(1, tiles - 1):
                sums.products(k, *step(t))
            sums.flush(acc.at[q])

        for q in range(SLABS):
            slab(q)

    lane1 = lax.broadcasted_iota(jnp.int32, (1, 128), 1)
    z = lane1 // PITCH * SLABS
    here = (lane1 % PITCH >= DEEP) & (lane1 % PITCH < PITCH - DEEP)
    groups = 128 // PITCH
    total = jnp.where(
        (lane1 >= DEEP) & (lane1 < 128 - DEEP), jnp.sum(acc1[...] + acc2[...] + acc3[...], axis=1), 0.0
    )
    for q in range(SLABS):
        kept = here & (z + q >= DEEP) & (z + q < groups * SLABS - DEEP)
        total = total + jnp.where(kept, jnp.sum(acc[q], axis=1), 0.0)
    total = jnp.concatenate([total, jnp.zeros((128 - total.shape[0], 128), F32)], 0)
    row = lax.dot_general(
        jnp.ones((8, 128), F32),
        total,
        (((1,), (1,)), ((), ())),
        precision=lax.Precision.HIGHEST,
        preferred_element_type=F32,
    )
    out[...] = jnp.broadcast_to(row[0:1][None], out.shape)


def x_strip(strip, side, far_strip, far_rim, face, corner, accs, peers):
    _, slabs, ny, nx = strip.shape
    laid = (slabs, ny + 8, nx)
    return pl.pallas_call(
        x_strip_kernel,
        out_shape=jax.ShapeDtypeStruct((peers, 1, 128), F32),
        in_specs=[VMEM] * 9,
        out_specs=VMEM,
        scratch_shapes=[pltpu.VMEM((COLS,) + laid, F32)] * 4
        + [
            pltpu.VMEM(laid, F32),
            pltpu.VMEM((4,) + laid, F32),
            pltpu.VMEM((slabs + 1,) + laid[1:], F32),
            pltpu.VMEM((slabs, MOMENTS * NPAIRS, 8, nx), F32),
        ],
        compiler_params=params(16),
        name="x_strip",
    )(strip, side, far_strip, far_rim, face, corner, *accs)


def factor(row, triangle, coef):
    lane, sub = lanes(8), sublanes(8)
    blocks = (KRYLOV + 7) // 8
    columns = []
    for b in range(KRYLOV):
        parts = []
        for i in range(blocks):
            a = sub + 8 * i
            low, high = jnp.minimum(a % COLS, b % COLS), jnp.maximum(a % COLS, b % COLS)
            pair = low * COLS - (low * (low - 1)) // 2 + high - low
            index = jnp.where(a < KRYLOV, (a // COLS + b // COLS) * NPAIRS + pair, 127)
            parts.append(permute_lanes(row, index))
        columns.append(parts)
    at = 0
    for k in range(KRYLOV):
        i, j = k // 8, k % 8

        def entry(b):
            return jnp.broadcast_to(columns[b][i][j : j + 1], (8, 128))

        pivot = entry(k)
        inverse = 1.0 / pivot
        root = jnp.sqrt(pivot)
        scale = 1.0 / root
        line = jnp.where(lane == k, root, 0.0)
        if k < COLS:
            coef[at] = scale
            at += 1
        for b in range(k + 1, KRYLOV):
            value = entry(b)
            line = jnp.where(lane == b, value * scale, line)
            if b < COLS:
                coef[at] = value * scale
                at += 1
            value = value * inverse
            for n in range((k + 1) // 8, blocks):
                columns[b][n] = columns[b][n] - columns[k][n] * value
        triangle[k : k + 1, :] = line[0:1, 0:KRYLOV]


def finish_kernel(ncells, parts, block, ortho, triangle, coef):
    step = pl.program_id(0)

    @pl.when(step == 0)
    def _():
        row = jnp.sum(parts[...], axis=0) * (1.0 / ncells)
        factor(jnp.broadcast_to(row, (8, 128)), triangle, coef)

    u = {}
    for i in range(COLS):
        for j in range(i, COLS):
            u[i, j] = coef[len(u)]
    slabs = ortho.shape[1]

    def slab(z, carry):
        for t in range(ortho.shape[2] // 8):
            done = []
            for j in range(COLS):
                value = block[j, step * slabs + z, tile(t)]
                for i in range(j):
                    value = value - u[i, j] * done[i]
                value = value * u[j, j]
                ortho[j, z, tile(t)] = value
                done.append(value)
        return carry

    lax.fori_loop(0, slabs, slab, 0, unroll=2)


def finish(parts, block, ncells):
    cols, nz, ny, nx = block.shape
    steps = 4
    piece = pl.BlockSpec((cols, nz // steps, ny, nx), lambda i: (0, i, 0, 0))
    return pl.pallas_call(
        lambda *refs: finish_kernel(ncells, *refs),
        grid=(steps,),
        out_shape=[
            jax.ShapeDtypeStruct(block.shape, F32),
            jax.ShapeDtypeStruct((KRYLOV, KRYLOV), F32),
        ],
        in_specs=[pl.BlockSpec(parts.shape, lambda i: (0, 0, 0)), VMEM],
        out_specs=[piece, pl.BlockSpec((KRYLOV, KRYLOV), lambda i: (0, 0))],
        scratch_shapes=[pltpu.VMEM((NPAIRS, 8, 128), F32)],
        compiler_params=params(16),
        name="finish",
    )(parts, block)


def shards(block, kappa):
    axes = ("gx", "gy", "gz")
    peers = lax.axis_size(axes)
    ncells = float(kappa.size * peers)
    far = [pltpu.with_memory_space_constraint(value, pltpu.HBM) for value in (block, kappa)]
    first, second = swap(*pack_z(*far), "gz")
    strip, x_face, y_face, y_kept = faces(block, kappa)
    rim = pull(y_face, "gy")
    acc1, edge = inner(block, kappa)
    far_face, far_kept = far_y(first, second, acc1)
    far_rim = pull(far_face, "gy")
    far_strip = far_strips(first, second, far_kept)
    side, x_face, corner = pack_x(x_face, rim, far_strip)
    x_face, corner = pull(x_face, "gx"), pull(corner, "gx", "gy")
    acc2 = outer(block, kappa, edge, first, second, side)
    acc3 = y_strip(y_kept, far_kept, rim, far_rim)
    accs = (acc1, acc2, acc3)
    moments = x_strip(strip, side, far_strip, far_rim, x_face, corner, accs, peers)
    parts = lax.all_to_all(moments, axes, 0, 0, tiled=True)
    return tuple(finish(parts, block, ncells))


def solution(mesh):
    return jax.shard_map(
        shards,
        mesh=mesh,
        in_specs=(P(None, "gz", "gy", "gx"), P("gz", "gy", "gx")),
        out_specs=(P(None, "gz", "gy", "gx"), P()),
        check_vma=False,
    )
```

```python
import jax
import jax.numpy as jnp
import numpy as np
from jax import lax
from jax.experimental import pallas as pl
from jax.experimental.pallas import tpu as pltpu
from jax.sharding import PartitionSpec as P

COLS = 4
BASIS = 4
KRYLOV = 20
MOMENTS = 2 * BASIS + 1
PAIRS = [(c, d) for c in range(COLS) for d in range(c, COLS)]
NPAIRS = len(PAIRS)
DEEP = BASIS
ARRAYS = COLS + 1
PITCH = 4 * DEEP
SLABS = 3

basis_shift = 6.0
basis_scale = 3.0

F32 = jnp.float32
VMEM = pl.BlockSpec(memory_space=pltpu.VMEM)
HBM = pl.BlockSpec(memory_space=pltpu.HBM)


def params(mib):
    return pltpu.CompilerParams(vmem_limit_bytes=mib * 1024 * 1024)


def cost(flops):
    return pl.CostEstimate(flops=flops, bytes_accessed=1 << 20, transcendentals=0)


def lanes(rows):
    return lax.broadcasted_iota(jnp.int32, (rows, 128), 1)


def sublanes(rows):
    return lax.broadcasted_iota(jnp.int32, (rows, 128), 0)


def permute_lanes(value, index):
    return jnp.take_along_axis(value, index, axis=1, mode="promise_in_bounds")


def even_first(axis, first, second):
    return jnp.where(lax.axis_index(axis) % 2 == 0, first, second)


def sides(axis, first, second):
    at = lax.axis_index(axis)
    upper = jnp.where(at == lax.axis_size(axis) - 1, 0.0, even_first(axis, first, second))
    lower = jnp.where(at == 0, 0.0, even_first(axis, second, first))
    return upper, lower


def swap(first, second, axis):
    peers = lax.axis_size(axis)
    other = [(i, (i - 1 if i % 2 == 0 else i + 1) % peers) for i in range(peers)]
    second = lax.ppermute(second, axis, other)
    first = lax.ppermute(first, axis, [(i, i ^ 1) for i in range(peers)])
    return first, second


def upward():
    return lax.axis_index("gz") % 2 == 0


def pull(face, *axes):
    sizes = [lax.axis_size(axis) for axis in axes] + [lax.axis_size("gz")]
    pairs = []
    for at in np.ndindex(*sizes):
        step = -1 if at[-1] % 2 == 0 else 1
        to = [(i + step) % size for i, size in zip(at[:-1], sizes)] + [at[-1]]
        pairs.append(tuple(int(np.ravel_multi_index(place, sizes)) for place in (at, to)))
    return lax.ppermute(face, (*axes, "gz"), pairs)


def at_seam(axis):
    at = lax.axis_index(axis)
    return at == jnp.where(upward(), lax.axis_size(axis) - 1, 0)


def cut(there, value):
    return jnp.where(there, 0.0, value)


def link(one, other, bounded):
    weight = (one + other) * (0.5 / basis_scale)
    if bounded:
        weight = jnp.where(jnp.minimum(one, other) > 0.0, weight, 0.0)
    return weight


def centre(k, others):
    total = 6.0 * k
    for other in others:
        total = total + other
    return total * (0.5 / basis_scale) - basis_shift / basis_scale


def rows_above(ref, index, t, tiles, value):
    if t == tiles - 1:
        return pltpu.roll(value, 7, 0)
    return ref[index + (slice(8 * t + 1, 8 * t + 9),)]


def rows_below(ref, index, t, value):
    if t == 0:
        return pltpu.roll(value, 1, 0)
    return ref[index + (slice(8 * t - 1, 8 * t + 7),)]


def tile(t):
    return slice(8 * t, 8 * t + 8)


class Sums:
    def __init__(self):
        self.held = {}

    def add(self, at, term):
        self.held[at] = self.held[at] + term if at in self.held else term

    def products(self, k, olds, news):
        for p, (c, d) in enumerate(PAIRS):
            if k == 1:
                self.add(p, olds[c] * olds[d])
            self.add((2 * k - 1) * NPAIRS + p, olds[c] * news[d])
            self.add(2 * k * NPAIRS + p, news[c] * news[d])

    def flush(self, acc):
        for at, total in self.held.items():
            acc[at] += total


def apply(v, above, below, far, near, w):
    new = w[0] * v
    new -= w[1] * pltpu.roll(v, 127, 1)
    new -= w[2] * pltpu.roll(v, 1, 1)
    new -= w[3] * above
    new -= w[4] * below
    new -= w[5] * far
    new -= w[6] * near
    return new


def tile_weights(w, q, wz, far, near, t):
    c0, right, left, above = (w[i, q, tile(t)] for i in range(4))
    below = rows_below(w, (3, q), t, above)
    return c0, right, left, above, below, wz[far, tile(t)], wz[near, tile(t)]


def pack_z_kernel(block, kappa, to_first, to_second, sems):
    nz = kappa.shape[0]
    high = nz - DEEP
    even = lax.axis_index("gz") % 2 == 0
    copies = []
    for i, (out, at) in enumerate(
        ((to_second, jnp.where(even, 0, high)), (to_first, jnp.where(even, high, 0)))
    ):
        copies.append(pltpu.make_async_copy(block.at[:, pl.ds(at, DEEP)], out.at[0:COLS], sems.at[2 * i]))
        copies.append(pltpu.make_async_copy(kappa.at[pl.ds(at, DEEP)], out.at[COLS], sems.at[2 * i + 1]))
    for copy in copies:
        copy.start()
    for copy in copies:
        copy.wait()


def pack_z(block, kappa):
    nz, ny, nx = kappa.shape
    face = jax.ShapeDtypeStruct((ARRAYS, DEEP, ny, nx), F32)
    return pl.pallas_call(
        pack_z_kernel,
        out_shape=[face, face],
        in_specs=[HBM, HBM],
        out_specs=[VMEM] * 2,
        scratch_shapes=[pltpu.SemaphoreType.DMA((4,))],
        compiler_params=params(8),
        name="pack_z",
    )(block, kappa)


def inner_kernel(block, kappa, acc, edge, p1, p2, p3, w, wz):
    nz, ny, _ = kappa.shape
    tiles = ny // 8
    half = sublanes(8) < 4
    acc[...] = jnp.zeros_like(acc)

    def weights(z, carry):
        for t in range(tiles):
            k = kappa[z, tile(t)]
            right, left = pltpu.roll(k, 127, 1), pltpu.roll(k, 1, 1)
            above = rows_above(kappa, (z,), t, tiles, k)
            below = rows_below(kappa, (z,), t, k)
            far = kappa[z + 1, tile(t)]
            near = kappa[jnp.maximum(z - 1, 0), tile(t)]
            w[0, z, tile(t)] = centre(k, (right, left, above, below, far, near))
            w[1, z, tile(t)] = link(k, right, False)
            w[2, z, tile(t)] = link(k, left, False)
            w[3, z, tile(t)] = link(k, above, False)
            wz[z, tile(t)] = link(k, far, False)
        return carry

    lax.fori_loop(0, nz - 1, weights, 0, unroll=5)
    fields = (block, p1, p2, p3, None)
    for k in range(1, BASIS + 1):
        src, dst = fields[k - 1], fields[k]

        def slab(z, carry, k=k, src=src, dst=dst):
            sums = Sums()

            def step(t):
                ws = tile_weights(w, z, wz, z, z - 1, t)
                olds, news = [], []
                for c in range(COLS):
                    v = src[c, z, tile(t)]
                    above = rows_above(src, (c, z), t, tiles, v)
                    below = rows_below(src, (c, z), t, v)
                    news.append(apply(v, above, below, src[c, z + 1, tile(t)], src[c, z - 1, tile(t)], ws))
                    olds.append(v)
                if dst is not None:
                    for c in range(COLS):
                        dst[c, z, tile(t)] = news[c]
                return olds, news

            first, last = step(0), step(tiles - 1)
            olds, news = (
                [jnp.where(half, b, a) for a, b in zip(first[i], last[i])] for i in range(2)
            )
            sums.products(k, olds, news)
            for t in range(1, tiles - 1):
                sums.products(k, *step(t))
            sums.flush(acc)
            return carry

        lax.fori_loop(k, nz - k, slab, 0, unroll=(nz - 2 * k + 1) // 2)
        if dst is not None:
            for i in range(2):
                edge[k - 1, 0, i] = dst[:, k + i]
                edge[k - 1, 1, i] = dst[:, nz - 1 - k - i]


def inner(block, kappa):
    nz, ny, nx = kappa.shape
    return pl.pallas_call(
        inner_kernel,
        out_shape=[
            jax.ShapeDtypeStruct((MOMENTS * NPAIRS, 8, nx), F32),
            jax.ShapeDtypeStruct((BASIS - 1, 2, 2, COLS, ny, nx), F32),
        ],
        in_specs=[VMEM] * 2,
        out_specs=[VMEM] * 2,
        scratch_shapes=[pltpu.VMEM(block.shape, F32)] * 3
        + [pltpu.VMEM((4, nz, ny, nx), F32), pltpu.VMEM((nz, ny, nx), F32)],
        compiler_params=params(24),
        cost_estimate=cost(1 << 28),
        name="inner",
    )(block, kappa)


def strip_of(planes):
    lane = lanes(8)
    offset, group = lane % PITCH, lane // PITCH
    index = jnp.where(offset < 8, 120 + offset, offset - 8)
    strip = None
    for g, plane in enumerate(planes):
        if plane is not None:
            value = permute_lanes(plane, index)
            strip = value if strip is None else jnp.where(group == g, value, strip)
    return strip


def pack_halves(one, other):
    value = jnp.where(upward(), pltpu.roll(one, 120, 1), one)
    if other is None:
        return value
    low = lanes(8) % PITCH < 8
    return jnp.where(low, value, jnp.where(upward(), other, pltpu.roll(other, 8, 1)))


HALVES = [(a, q) for a in range(ARRAYS) for q in range(SLABS)]
DUOS = [HALVES[n : n + 2] for n in range(0, len(HALVES), 2)]
FAR = 2 * DEEP


def pack_duo(duo, get):
    return pack_halves(get(*duo[0]), get(*duo[1]) if len(duo) > 1 else None)


def faces_kernel(block, kappa, strip, x_face, y_face, y_kept):
    nz, ny, _ = kappa.shape

    def rows(t, carry):
        at = pl.ds(pl.multiple_of(t * 8, 8), 8)

        def plane(a, z):
            if z < 0 or z >= nz:
                return None
            return block[a, z, at] if a < COLS else kappa[z, at]

        held = {}
        for a, q in HALVES:
            held[a, q] = strip_of([plane(a, z - DEEP) for z in range(q, nz + FAR, SLABS)])
            strip[a, q, at] = held[a, q]
        for n, duo in enumerate(DUOS):
            x_face[n, at] = pack_duo(duo, lambda a, q: held[a, q])
        return carry

    lax.fori_loop(0, ny // 8, rows, 0, unroll=2)

    def slabs(z, carry):
        for a in range(ARRAYS):
            low, high = (block[a, z, at] if a < COLS else kappa[z, at] for at in (slice(0, 8), slice(ny - 8, ny)))
            y_face[a, z] = jnp.where(upward(), low, high)
            y_kept[a, z] = jnp.where(upward(), high, low)
        return carry

    lax.fori_loop(0, nz, slabs, 0, unroll=4)


def faces(block, kappa):
    nz, ny, nx = kappa.shape
    shapes = ((ARRAYS, SLABS, ny, nx), (len(DUOS), ny, nx), (ARRAYS, nz, 8, nx), (ARRAYS, nz, 8, nx))
    return pl.pallas_call(
        faces_kernel,
        out_shape=[jax.ShapeDtypeStruct(shape, F32) for shape in shapes],
        in_specs=[VMEM] * 2,
        out_specs=[VMEM] * 4,
        compiler_params=params(16),
        cost_estimate=cost(1 << 24),
        name="faces",
    )(block, kappa)


def far_y_kernel(f_low, f_high, s_low, s_high, after, face, kept):
    def slabs(i, carry):
        for a in range(ARRAYS):
            low = sides("gz", f_low[a, i], s_low[a, i])
            high = sides("gz", f_high[a, i], s_high[a, i])
            for at, which in ((i, 1), (DEEP + i, 0)):
                face[a, at] = jnp.where(upward(), low[which], high[which])
                kept[a, at] = jnp.where(upward(), high[which], low[which])
        return carry

    lax.fori_loop(0, DEEP, slabs, 0, unroll=2)


def far_y(first, second, after):
    _, _, ny, nx = first.shape
    last = ny // 8 - 1
    whole = lambda shape: pl.BlockSpec(shape, lambda i: (0,) * len(shape))
    edge = lambda at: pl.BlockSpec((ARRAYS, DEEP, 8, nx), lambda i: (0, 0, at, 0))
    shape = (ARRAYS, FAR, 8, nx)
    return pl.pallas_call(
        far_y_kernel,
        grid=(1,),
        out_shape=[jax.ShapeDtypeStruct(shape, F32)] * 2,
        in_specs=[edge(0), edge(last), edge(0), edge(last), pl.BlockSpec(memory_space=pl.ANY)],
        out_specs=[whole(shape)] * 2,
        compiler_params=params(16),
        name="far_y",
    )(first, first, second, second, after)


def far_strips_kernel(first, second, after, strip):
    def rows(t, carry):
        at = pl.ds(pl.multiple_of(t * 8, 8), 8)
        for a in range(ARRAYS):
            uppers, lowers = zip(*[sides("gz", first[a, i, at], second[a, i, at]) for i in range(DEEP)])
            strip[a, at] = strip_of(lowers + uppers)
        return carry

    lax.fori_loop(0, strip.shape[1] // 8, rows, 0, unroll=2)


def far_strips(first, second, after):
    _, _, ny, nx = first.shape
    return pl.pallas_call(
        far_strips_kernel,
        out_shape=jax.ShapeDtypeStruct((ARRAYS, ny, nx), F32),
        in_specs=[VMEM] * 2 + [pl.BlockSpec(memory_space=pl.ANY)],
        out_specs=VMEM,
        compiler_params=params(16),
        cost_estimate=cost(1 << 23),
        name="far_strips",
    )(first, second, after)


def far_pairs():
    return [(n, n + 1 if n + 1 < ARRAYS else None) for n in range(0, ARRAYS, 2)]


def pack_x_kernel(own_face, rim, far_strip, side, face, corner):
    nz = rim.shape[1]
    tiles = far_strip.shape[1] // 8

    def plane(a, z):
        return rim[a, z] if 0 <= z < nz else None

    def far_tile(a, t):
        return None if a is None else far_strip[a, tile(t)]

    for n in range(len(DUOS)):
        for t in range(tiles):
            face[n * tiles + t] = own_face[n, tile(t)]
    at = len(DUOS) * tiles
    for n, (one, other) in enumerate(far_pairs()):
        packed = [pack_halves(far_tile(one, t), far_tile(other, t)) for t in range(tiles)]
        for t in range(tiles):
            face[at + n * tiles + t] = packed[t]
        corner[n] = jnp.where(upward(), packed[0], packed[tiles - 1])
    at += len(far_pairs()) * tiles
    for a, q in HALVES:
        side[a, q] = strip_of([plane(a, z - DEEP) for z in range(q, nz + FAR, SLABS)])
    for n, duo in enumerate(DUOS):
        face[at + n] = pack_duo(duo, lambda a, q: side[a, q])


def pack_x(own_face, rim, far_strip):
    _, ny, nx = far_strip.shape
    count = (len(DUOS) + len(far_pairs())) * ny // 8 + len(DUOS)
    shapes = ((ARRAYS, SLABS, 8, nx), (count, 8, nx), (len(far_pairs()), 8, nx))
    return pl.pallas_call(
        pack_x_kernel,
        out_shape=[jax.ShapeDtypeStruct(shape, F32) for shape in shapes],
        in_specs=[VMEM] * 3,
        out_specs=[VMEM] * 3,
        compiler_params=params(16),
        name="pack_x",
    )(own_face, rim, far_strip)


def outer_kernel(block, kappa, edge, first, second, after, acc, f0, f1, f2, f3, kz, w, wz):
    nz, ny, _ = kappa.shape
    tiles = ny // 8
    half = sublanes(8) < 4
    acc[...] = jnp.zeros_like(acc)

    def far(i, carry):
        for a in range(ARRAYS):
            upper, lower = sides("gz", first[a, i], second[a, i])
            if a < COLS:
                f0[0, a, i] = lower
                f0[1, a, DEEP - 1 - i] = upper
            else:
                kz[0, i] = lower
                kz[1, DEEP - 1 - i] = upper
        return carry

    lax.fori_loop(0, DEEP, far, 0)
    for i in range(2):
        for c in range(COLS):
            f0[0, c, DEEP + i] = block[c, i]
            f0[1, c, DEEP + i] = block[c, nz - 1 - i]
            for k, f in enumerate((f1, f2, f3)):
                for side in range(2):
                    f[side, c, DEEP + i] = edge[k, side, i, c]
    for i in range(DEEP + 1):
        kz[0, DEEP + i] = kappa[i]
        kz[1, DEEP + i] = kappa[nz - 1 - i]

    def weights(at, carry):
        side, e = at // 8, at % 8
        for t in range(tiles):
            k = kz[side, e, tile(t)]
            right, left = pltpu.roll(k, 127, 1), pltpu.roll(k, 1, 1)
            above = rows_above(kz, (side, e), t, tiles, k)
            below = rows_below(kz, (side, e), t, k)
            far = kz[side, e + 1, tile(t)]
            near = kz[side, jnp.maximum(e - 1, 0), tile(t)]
            w[0, at, tile(t)] = centre(k, (right, left, above, below, far, near))
            w[1, at, tile(t)] = link(k, right, False)
            w[2, at, tile(t)] = link(k, left, False)
            w[3, at, tile(t)] = link(k, above, False)
            wz[at, tile(t)] = link(k, far, True)
        return carry

    lax.fori_loop(0, 16, weights, 0, unroll=4)
    fields = (f0, f1, f2, f3, None)
    for k in range(1, BASIS + 1):
        src, dst = fields[k - 1], fields[k]

        def both(side, carry, k=k, src=src, dst=dst):
            for j in range(DEEP):
                own = j >= DEEP - k
                sums = Sums()

                def step(t):
                    at = side * 8 + j + k
                    ws = tile_weights(w, at, wz, at, at - 1, t)
                    olds, news = [], []
                    for c in range(COLS):
                        v = src[side, c, j + 1, tile(t)]
                        above = rows_above(src, (side, c, j + 1), t, tiles, v)
                        below = rows_below(src, (side, c, j + 1), t, v)
                        far, near = src[side, c, j + 2, tile(t)], src[side, c, j, tile(t)]
                        news.append(apply(v, above, below, far, near, ws))
                        olds.append(v)
                    if dst is not None:
                        for c in range(COLS):
                            dst[side, c, j, tile(t)] = news[c]
                    return olds, news

                first, last = step(0), step(tiles - 1)
                if own:
                    olds, news = (
                        [jnp.where(half, b, a) for a, b in zip(first[i], last[i])] for i in range(2)
                    )
                    sums.products(k, olds, news)
                for t in range(1, tiles - 1):
                    pair = step(t)
                    if own:
                        sums.products(k, *pair)
                sums.flush(acc)
            return carry

        lax.fori_loop(0, 2, both, 0)


def outer(block, kappa, edge, first, second, after):
    nz, ny, nx = kappa.shape
    return pl.pallas_call(
        outer_kernel,
        out_shape=jax.ShapeDtypeStruct((MOMENTS * NPAIRS, 8, nx), F32),
        in_specs=[VMEM] * 5 + [pl.BlockSpec(memory_space=pl.ANY)],
        out_specs=VMEM,
        scratch_shapes=[pltpu.VMEM((2, COLS, DEEP + 2, ny, nx), F32)] * 4
        + [
            pltpu.VMEM((2, 2 * DEEP + 1, ny, nx), F32),
            pltpu.VMEM((4, 16, ny, nx), F32),
            pltpu.VMEM((16, ny, nx), F32),
        ],
        compiler_params=params(24),
        cost_estimate=cost(1 << 27),
        name="outer",
    )(block, kappa, edge, first, second, after)


def y_strip_kernel(kept, far_kept, rim, far_rim, acc, g0, g1, g2, g3, kr, w, wz):
    nz = rim.shape[1]
    depth = nz + FAR
    half = sublanes(8) < 4
    seam = [at_seam("gy") & (sublanes(8) == 7), at_seam("gy") & (sublanes(8) == 0)]
    acc[...] = jnp.zeros_like(acc)

    def lay(z, kept, rim, at):
        for a in range(ARRAYS):
            below = jnp.where(upward(), kept[a, at], rim[a, at])
            above = jnp.where(upward(), rim[a, at], kept[a, at])
            for t, part in enumerate((below, above)):
                if a < COLS:
                    g0[a, z, tile(t)] = part
                else:
                    kr[z, tile(t)] = part

    def fill(z, carry):
        lay(z + DEEP, kept, rim, z)
        return carry

    def fill_far(i, carry):
        lay(i, far_kept, far_rim, i)
        lay(nz + DEEP + i, far_kept, far_rim, DEEP + i)
        return carry

    lax.fori_loop(0, nz, fill, 0, unroll=4)
    lax.fori_loop(0, DEEP, fill_far, 0, unroll=2)

    def weights(z, carry):
        for t in range(2):
            k = kr[z, tile(t)]
            right, left = pltpu.roll(k, 127, 1), pltpu.roll(k, 1, 1)
            above = rows_above(kr, (z,), t, 2, k)
            below = rows_below(kr, (z,), t, k)
            above = cut(seam[0], above) if t == 0 else above
            below = cut(seam[1], below) if t == 1 else below
            far = kr[z + 1, tile(t)]
            near = kr[jnp.maximum(z - 1, 0), tile(t)]
            w[0, z, tile(t)] = centre(k, (right, left, above, below, far, near))
            w[1, z, tile(t)] = link(k, right, False)
            w[2, z, tile(t)] = link(k, left, False)
            w[3, z, tile(t)] = link(k, above, True)
            wz[z, tile(t)] = link(k, far, True)
        return carry

    lax.fori_loop(0, depth - 1, weights, 0, unroll=4)
    fields = (g0, g1, g2, g3, None)
    for k in range(1, BASIS + 1):
        src, dst = fields[k - 1], fields[k]

        def slab(z, own, k=k, src=src, dst=dst):
            sums = Sums()
            kept = []
            for t in range(2):
                ws = tile_weights(w, z, wz, z, z - 1, t)
                olds, news = [], []
                for c in range(COLS):
                    v = src[c, z, tile(t)]
                    above = rows_above(src, (c, z), t, 2, v)
                    below = rows_below(src, (c, z), t, v)
                    news.append(apply(v, above, below, src[c, z + 1, tile(t)], src[c, z - 1, tile(t)], ws))
                    olds.append(v)
                if dst is not None:
                    for c in range(COLS):
                        dst[c, z, tile(t)] = news[c]
                kept.append((olds, news))
            if own:
                olds, news = (
                    [jnp.where(half, b, a) for a, b in zip(kept[0][i], kept[1][i])] for i in range(2)
                )
                sums.products(k, olds, news)
                sums.flush(acc)

        def far(i, carry, k=k, slab=slab):
            slab(k + i, False)
            slab(depth - DEEP + i, False)
            return carry

        def own(z, carry, slab=slab):
            slab(z, True)
            return carry

        if k < DEEP:
            lax.fori_loop(0, DEEP - k, far, 0, unroll=True)
        lax.fori_loop(DEEP, depth - DEEP, own, 0, unroll=16)


def y_strip(kept, far_kept, rim, far_rim):
    _, nz, _, nx = rim.shape
    depth = nz + FAR
    return pl.pallas_call(
        y_strip_kernel,
        out_shape=jax.ShapeDtypeStruct((MOMENTS * NPAIRS, 8, nx), F32),
        in_specs=[VMEM] * 4,
        out_specs=VMEM,
        scratch_shapes=[pltpu.VMEM((COLS, depth, 16, nx), F32)] * 4
        + [
            pltpu.VMEM((depth, 16, nx), F32),
            pltpu.VMEM((4, depth, 16, nx), F32),
            pltpu.VMEM((depth, 16, nx), F32),
        ],
        compiler_params=params(16),
        cost_estimate=cost(1 << 30),
        name="y_strip",
    )(kept, far_kept, rim, far_rim)


def x_strip_kernel(strip, side, far_strip, far_rim, face, corner, acc1, acc2, acc3, out, s0, s1, s2, s3, kr, w, wz, acc):
    tiles = strip.shape[2] // 8 + 1
    lane = lanes(8)
    offset = lane % PITCH
    half = sublanes(8) < 4
    right_seam, left_seam = (at_seam("gx") & (offset == at) for at in (7, 8))
    above_seam, below_seam = (at_seam("gy") & (sublanes(8) == at) for at in (7, 0))
    shift = jnp.where(upward(), 0, 1)

    def next_slab(ref, index, q, at):
        if q < SLABS - 1:
            return ref[index + (q + 1, at)]
        return pltpu.roll(ref[index + (0, at)], 128 - PITCH, 1)

    def last_slab(ref, index, q, at):
        if q > 0:
            return ref[index + (q - 1, at)]
        return pltpu.roll(ref[index + (SLABS - 1, at)], PITCH, 1)

    own_side = (offset < 8) == upward()
    depth = 128 // PITCH * SLABS
    far_at = len(DUOS) * (tiles - 1)
    rim_at = far_at + len(far_pairs()) * (tiles - 1)
    far_side = [strip_of([far_rim[a, i] for i in range(FAR)]) for a in range(ARRAYS)]
    for n, (a, q) in enumerate(HALVES):
        z = lane // PITCH * SLABS + q
        far = (z < DEEP) | (z >= depth - DEEP)
        index = jnp.where(z < DEEP, z, jnp.where(far, z - (depth - FAR), 0)) * PITCH
        for t in range(tiles):
            own = strip[a, q, tile(t)] if t < tiles - 1 else side[a, q]
            beyond = face[n // 2 * (tiles - 1) + t] if t < tiles - 1 else face[rim_at + n // 2]
            if n % 2 == 0:
                beyond = jnp.where(upward(), pltpu.roll(beyond, 8, 1), beyond)
            else:
                beyond = jnp.where(upward(), beyond, pltpu.roll(beyond, 120, 1))
            far_own = far_strip[a, tile(t)] if t < tiles - 1 else far_side[a]
            far_beyond = face[far_at + a // 2 * (tiles - 1) + t] if t < tiles - 1 else corner[a // 2]
            far_own = permute_lanes(far_own, index + offset)
            far_beyond = permute_lanes(far_beyond, index + offset % 8 + 8 * (a % 2))
            value = jnp.where(own_side, jnp.where(far, far_own, own), jnp.where(far, far_beyond, beyond))
            at = t + shift if t < tiles - 1 else (tiles - 1) * (1 - shift)
            at = pl.ds(pl.multiple_of(at * 8, 8), 8)
            if a < COLS:
                s0[a, q, at] = value
            else:
                kr[q, at] = value

    for q in range(SLABS):
        for t in range(tiles):
            k = kr[q, tile(t)]
            right, left = cut(right_seam, pltpu.roll(k, 127, 1)), cut(left_seam, pltpu.roll(k, 1, 1))
            above = rows_above(kr, (q,), t, tiles, k)
            below = rows_below(kr, (q,), t, k)
            if t == 0 or t == tiles - 2:
                above = cut(above_seam & (upward() == (t > 0)), above)
            if t == 1 or t == tiles - 1:
                below = cut(below_seam & (upward() == (t > 1)), below)
            far, near = next_slab(kr, (), q, tile(t)), last_slab(kr, (), q, tile(t))
            w[0, q, tile(t)] = centre(k, (right, left, above, below, far, near))
            w[1, q, tile(t)] = link(k, right, True)
            w[2, q, tile(t)] = link(k, left, True)
            w[3, q, tile(t)] = link(k, above, True)
            wz[q + 1, tile(t)] = link(k, far, True)
            if q == 0:
                wz[0, tile(t)] = link(k, near, True)
    acc[...] = jnp.zeros_like(acc)
    fields = (s0, s1, s2, s3, None)
    for k in range(1, BASIS + 1):
        src, dst = fields[k - 1], fields[k]

        def slab(q):
            sums = Sums()

            def step(t):
                ws = tile_weights(w, q, wz, q + 1, q, t)
                olds, news = [], []
                for c in range(COLS):
                    v = src[c, q, tile(t)]
                    above = rows_above(src, (c, q), t, tiles, v)
                    below = rows_below(src, (c, q), t, v)
                    far, near = next_slab(src, (c,), q, tile(t)), last_slab(src, (c,), q, tile(t))
                    news.append(apply(v, above, below, far, near, ws))
                    olds.append(v)
                if dst is not None:
                    for c in range(COLS):
                        dst[c, q, tile(t)] = news[c]
                return olds, news

            first, last = step(0), step(tiles - 1)
            olds, news = (
                [jnp.where(half, b, a) for a, b in zip(first[i], last[i])] for i in range(2)
            )
            sums.products(k, olds, news)
            for t in range(1, tiles - 1):
                sums.products(k, *step(t))
            sums.flush(acc.at[q])

        for q in range(SLABS):
            slab(q)

    lane1 = lax.broadcasted_iota(jnp.int32, (1, 128), 1)
    z = lane1 // PITCH * SLABS
    here = (lane1 % PITCH >= DEEP) & (lane1 % PITCH < PITCH - DEEP)
    groups = 128 // PITCH
    total = jnp.where(
        (lane1 >= DEEP) & (lane1 < 128 - DEEP), jnp.sum(acc1[...] + acc2[...] + acc3[...], axis=1), 0.0
    )
    for q in range(SLABS):
        kept = here & (z + q >= DEEP) & (z + q < groups * SLABS - DEEP)
        total = total + jnp.where(kept, jnp.sum(acc[q], axis=1), 0.0)
    total = jnp.concatenate([total, jnp.zeros((128 - total.shape[0], 128), F32)], 0)
    row = lax.dot_general(
        jnp.ones((8, 128), F32),
        total,
        (((1,), (1,)), ((), ())),
        precision=lax.Precision.HIGHEST,
        preferred_element_type=F32,
    )
    out[...] = jnp.broadcast_to(row[0:1][None], out.shape)


def x_strip(strip, side, far_strip, far_rim, face, corner, accs, peers):
    _, slabs, ny, nx = strip.shape
    laid = (slabs, ny + 8, nx)
    return pl.pallas_call(
        x_strip_kernel,
        out_shape=jax.ShapeDtypeStruct((peers, 1, 128), F32),
        in_specs=[VMEM] * 9,
        out_specs=VMEM,
        scratch_shapes=[pltpu.VMEM((COLS,) + laid, F32)] * 4
        + [
            pltpu.VMEM(laid, F32),
            pltpu.VMEM((4,) + laid, F32),
            pltpu.VMEM((slabs + 1,) + laid[1:], F32),
            pltpu.VMEM((slabs, MOMENTS * NPAIRS, 8, nx), F32),
        ],
        compiler_params=params(16),
        name="x_strip",
    )(strip, side, far_strip, far_rim, face, corner, *accs)


def factor(row, triangle, coef):
    lane, sub = lanes(8), sublanes(8)
    blocks = (KRYLOV + 7) // 8
    columns = []
    for b in range(KRYLOV):
        parts = []
        for i in range(blocks):
            a = sub + 8 * i
            low, high = jnp.minimum(a % COLS, b % COLS), jnp.maximum(a % COLS, b % COLS)
            pair = low * COLS - (low * (low - 1)) // 2 + high - low
            index = jnp.where(a < KRYLOV, (a // COLS + b // COLS) * NPAIRS + pair, 127)
            parts.append(permute_lanes(row, index))
        columns.append(parts)
    at = 0
    for k in range(KRYLOV):
        i, j = k // 8, k % 8

        def entry(b):
            return jnp.broadcast_to(columns[b][i][j : j + 1], (8, 128))

        pivot = entry(k)
        inverse = 1.0 / pivot
        root = jnp.sqrt(pivot)
        scale = 1.0 / root
        line = jnp.where(lane == k, root, 0.0)
        if k < COLS:
            coef[at] = scale
            at += 1
        for b in range(k + 1, KRYLOV):
            value = entry(b)
            line = jnp.where(lane == b, value * scale, line)
            if b < COLS:
                coef[at] = value * scale
                at += 1
            value = value * inverse
            for n in range((k + 1) // 8, blocks):
                columns[b][n] = columns[b][n] - columns[k][n] * value
        triangle[k : k + 1, :] = line[0:1, 0:KRYLOV]


def finish_kernel(ncells, parts, block, ortho, triangle, coef):
    step = pl.program_id(0)

    @pl.when(step == 0)
    def _():
        row = jnp.sum(parts[...], axis=0) * (1.0 / ncells)
        factor(jnp.broadcast_to(row, (8, 128)), triangle, coef)

    u = {}
    for i in range(COLS):
        for j in range(i, COLS):
            u[i, j] = coef[len(u)]
    slabs = ortho.shape[1]

    def slab(z, carry):
        for t in range(ortho.shape[2] // 8):
            done = []
            for j in range(COLS):
                value = block[j, step * slabs + z, tile(t)]
                for i in range(j):
                    value = value - u[i, j] * done[i]
                value = value * u[j, j]
                ortho[j, z, tile(t)] = value
                done.append(value)
        return carry

    lax.fori_loop(0, slabs, slab, 0, unroll=2)


def finish(parts, block, ncells):
    cols, nz, ny, nx = block.shape
    steps = 2
    piece = pl.BlockSpec((cols, nz // steps, ny, nx), lambda i: (0, i, 0, 0))
    return pl.pallas_call(
        lambda *refs: finish_kernel(ncells, *refs),
        grid=(steps,),
        out_shape=[
            jax.ShapeDtypeStruct(block.shape, F32),
            jax.ShapeDtypeStruct((KRYLOV, KRYLOV), F32),
        ],
        in_specs=[pl.BlockSpec(parts.shape, lambda i: (0, 0, 0)), VMEM],
        out_specs=[piece, pl.BlockSpec((KRYLOV, KRYLOV), lambda i: (0, 0))],
        scratch_shapes=[pltpu.VMEM((NPAIRS, 8, 128), F32)],
        compiler_params=params(16),
        name="finish",
    )(parts, block)


def shards(block, kappa):
    axes = ("gx", "gy", "gz")
    peers = lax.axis_size(axes)
    ncells = float(kappa.size * peers)
    far = [pltpu.with_memory_space_constraint(value, pltpu.HBM) for value in (block, kappa)]
    first, second = swap(*pack_z(*far), "gz")
    strip, x_face, y_face, y_kept = faces(block, kappa)
    rim = pull(y_face, "gy")
    acc1, edge = inner(block, kappa)
    far_face, far_kept = far_y(first, second, acc1)
    far_rim = pull(far_face, "gy")
    far_strip = far_strips(first, second, far_kept)
    side, x_face, corner = pack_x(x_face, rim, far_strip)
    x_face, corner = pull(x_face, "gx"), pull(corner, "gx", "gy")
    acc2 = outer(block, kappa, edge, first, second, side)
    acc3 = y_strip(y_kept, far_kept, rim, far_rim)
    accs = (acc1, acc2, acc3)
    moments = x_strip(strip, side, far_strip, far_rim, x_face, corner, accs, peers)
    parts = lax.all_to_all(moments, axes, 0, 0, tiled=True)
    return tuple(finish(parts, block, ncells))


def solution(mesh):
    return jax.shard_map(
        shards,
        mesh=mesh,
        in_specs=(P(None, "gz", "gy", "gx"), P("gz", "gy", "gx")),
        out_specs=(P(None, "gz", "gy", "gx"), P()),
        check_vma=False,
    )
```

```python
import jax
import jax.numpy as jnp
import numpy as np
from jax import lax
from jax.experimental import pallas as pl
from jax.experimental.pallas import tpu as pltpu
from jax.sharding import PartitionSpec as P

COLS = 4
BASIS = 4
KRYLOV = 20
MOMENTS = 2 * BASIS + 1
PAIRS = [(c, d) for c in range(COLS) for d in range(c, COLS)]
NPAIRS = len(PAIRS)
DEEP = BASIS
ARRAYS = COLS + 1
PITCH = 4 * DEEP
SLABS = 3

basis_shift = 6.0
basis_scale = 3.0

F32 = jnp.float32
VMEM = pl.BlockSpec(memory_space=pltpu.VMEM)
HBM = pl.BlockSpec(memory_space=pltpu.HBM)


def params(mib):
    return pltpu.CompilerParams(vmem_limit_bytes=mib * 1024 * 1024)


def cost(flops):
    return pl.CostEstimate(flops=flops, bytes_accessed=1 << 20, transcendentals=0)


def lanes(rows):
    return lax.broadcasted_iota(jnp.int32, (rows, 128), 1)


def sublanes(rows):
    return lax.broadcasted_iota(jnp.int32, (rows, 128), 0)


def permute_lanes(value, index):
    return jnp.take_along_axis(value, index, axis=1, mode="promise_in_bounds")


def even_first(axis, first, second):
    return jnp.where(lax.axis_index(axis) % 2 == 0, first, second)


def sides(axis, first, second):
    at = lax.axis_index(axis)
    upper = jnp.where(at == lax.axis_size(axis) - 1, 0.0, even_first(axis, first, second))
    lower = jnp.where(at == 0, 0.0, even_first(axis, second, first))
    return upper, lower


def swap(first, second, axis):
    peers = lax.axis_size(axis)
    other = [(i, (i - 1 if i % 2 == 0 else i + 1) % peers) for i in range(peers)]
    second = lax.ppermute(second, axis, other)
    first = lax.ppermute(first, axis, [(i, i ^ 1) for i in range(peers)])
    return first, second


def upward():
    return lax.axis_index("gz") % 2 == 0


def pull(face, *axes):
    sizes = [lax.axis_size(axis) for axis in axes] + [lax.axis_size("gz")]
    pairs = []
    for at in np.ndindex(*sizes):
        step = -1 if at[-1] % 2 == 0 else 1
        to = [(i + step) % size for i, size in zip(at[:-1], sizes)] + [at[-1]]
        pairs.append(tuple(int(np.ravel_multi_index(place, sizes)) for place in (at, to)))
    return lax.ppermute(face, (*axes, "gz"), pairs)


def at_seam(axis):
    at = lax.axis_index(axis)
    return at == jnp.where(upward(), lax.axis_size(axis) - 1, 0)


def cut(there, value):
    return jnp.where(there, 0.0, value)


def link(one, other, bounded):
    weight = (one + other) * (0.5 / basis_scale)
    if bounded:
        weight = jnp.where(jnp.minimum(one, other) > 0.0, weight, 0.0)
    return weight


def centre(k, others):
    total = 6.0 * k
    for other in others:
        total = total + other
    return total * (0.5 / basis_scale) - basis_shift / basis_scale


def rows_above(ref, index, t, tiles, value):
    if t == tiles - 1:
        return pltpu.roll(value, 7, 0)
    return ref[index + (slice(8 * t + 1, 8 * t + 9),)]


def rows_below(ref, index, t, value):
    if t == 0:
        return pltpu.roll(value, 1, 0)
    return ref[index + (slice(8 * t - 1, 8 * t + 7),)]


def tile(t):
    return slice(8 * t, 8 * t + 8)


class Sums:
    def __init__(self):
        self.held = {}

    def add(self, at, term):
        self.held[at] = self.held[at] + term if at in self.held else term

    def products(self, k, olds, news):
        for p, (c, d) in enumerate(PAIRS):
            if k == 1:
                self.add(p, olds[c] * olds[d])
            self.add((2 * k - 1) * NPAIRS + p, olds[c] * news[d])
            self.add(2 * k * NPAIRS + p, news[c] * news[d])

    def flush(self, acc):
        for at, total in self.held.items():
            acc[at] += total


def apply(v, above, below, far, near, w):
    new = w[0] * v
    new -= w[1] * pltpu.roll(v, 127, 1)
    new -= w[2] * pltpu.roll(v, 1, 1)
    new -= w[3] * above
    new -= w[4] * below
    new -= w[5] * far
    new -= w[6] * near
    return new


def tile_weights(w, q, wz, far, near, t):
    c0, right, left, above = (w[i, q, tile(t)] for i in range(4))
    below = rows_below(w, (3, q), t, above)
    return c0, right, left, above, below, wz[far, tile(t)], wz[near, tile(t)]


def pack_z_kernel(block, kappa, to_first, to_second, sems):
    nz = kappa.shape[0]
    high = nz - DEEP
    even = lax.axis_index("gz") % 2 == 0
    copies = []
    for i, (out, at) in enumerate(
        ((to_second, jnp.where(even, 0, high)), (to_first, jnp.where(even, high, 0)))
    ):
        copies.append(pltpu.make_async_copy(block.at[:, pl.ds(at, DEEP)], out.at[0:COLS], sems.at[2 * i]))
        copies.append(pltpu.make_async_copy(kappa.at[pl.ds(at, DEEP)], out.at[COLS], sems.at[2 * i + 1]))
    for copy in copies:
        copy.start()
    for copy in copies:
        copy.wait()


def pack_z(block, kappa):
    nz, ny, nx = kappa.shape
    face = jax.ShapeDtypeStruct((ARRAYS, DEEP, ny, nx), F32)
    return pl.pallas_call(
        pack_z_kernel,
        out_shape=[face, face],
        in_specs=[HBM, HBM],
        out_specs=[VMEM] * 2,
        scratch_shapes=[pltpu.SemaphoreType.DMA((4,))],
        compiler_params=params(8),
        name="pack_z",
    )(block, kappa)


def inner_kernel(block, kappa, acc, edge, p1, p2, p3, w, wz):
    nz, ny, _ = kappa.shape
    tiles = ny // 8
    half = sublanes(8) < 4
    acc[...] = jnp.zeros_like(acc)

    def weights(z, carry):
        for t in range(tiles):
            k = kappa[z, tile(t)]
            right, left = pltpu.roll(k, 127, 1), pltpu.roll(k, 1, 1)
            above = rows_above(kappa, (z,), t, tiles, k)
            below = rows_below(kappa, (z,), t, k)
            far = kappa[z + 1, tile(t)]
            near = kappa[jnp.maximum(z - 1, 0), tile(t)]
            w[0, z, tile(t)] = centre(k, (right, left, above, below, far, near))
            w[1, z, tile(t)] = link(k, right, False)
            w[2, z, tile(t)] = link(k, left, False)
            w[3, z, tile(t)] = link(k, above, False)
            wz[z, tile(t)] = link(k, far, False)
        return carry

    lax.fori_loop(0, nz - 1, weights, 0, unroll=5)
    fields = (block, p1, p2, p3, None)
    for k in range(1, BASIS + 1):
        src, dst = fields[k - 1], fields[k]

        def slab(z, carry, k=k, src=src, dst=dst):
            sums = Sums()

            def step(t):
                ws = tile_weights(w, z, wz, z, z - 1, t)
                olds, news = [], []
                for c in range(COLS):
                    v = src[c, z, tile(t)]
                    above = rows_above(src, (c, z), t, tiles, v)
                    below = rows_below(src, (c, z), t, v)
                    news.append(apply(v, above, below, src[c, z + 1, tile(t)], src[c, z - 1, tile(t)], ws))
                    olds.append(v)
                if dst is not None:
                    for c in range(COLS):
                        dst[c, z, tile(t)] = news[c]
                return olds, news

            first, last = step(0), step(tiles - 1)
            olds, news = (
                [jnp.where(half, b, a) for a, b in zip(first[i], last[i])] for i in range(2)
            )
            sums.products(k, olds, news)
            for t in range(1, tiles - 1):
                sums.products(k, *step(t))
            sums.flush(acc)
            return carry

        lax.fori_loop(k, nz - k, slab, 0, unroll=(nz - 2 * k + 1) // 2)
        if dst is not None:
            for i in range(2):
                edge[k - 1, 0, i] = dst[:, k + i]
                edge[k - 1, 1, i] = dst[:, nz - 1 - k - i]


def inner(block, kappa):
    nz, ny, nx = kappa.shape
    return pl.pallas_call(
        inner_kernel,
        out_shape=[
            jax.ShapeDtypeStruct((MOMENTS * NPAIRS, 8, nx), F32),
            jax.ShapeDtypeStruct((BASIS - 1, 2, 2, COLS, ny, nx), F32),
        ],
        in_specs=[VMEM] * 2,
        out_specs=[VMEM] * 2,
        scratch_shapes=[pltpu.VMEM(block.shape, F32)] * 3
        + [pltpu.VMEM((4, nz, ny, nx), F32), pltpu.VMEM((nz, ny, nx), F32)],
        compiler_params=params(24),
        cost_estimate=cost(1 << 28),
        name="inner",
    )(block, kappa)


def strip_of(planes):
    lane = lanes(8)
    offset, group = lane % PITCH, lane // PITCH
    index = jnp.where(offset < 8, 120 + offset, offset - 8)
    strip = None
    for g, plane in enumerate(planes):
        if plane is not None:
            value = permute_lanes(plane, index)
            strip = value if strip is None else jnp.where(group == g, value, strip)
    return strip


def pack_halves(one, other):
    value = jnp.where(upward(), pltpu.roll(one, 120, 1), one)
    if other is None:
        return value
    low = lanes(8) % PITCH < 8
    return jnp.where(low, value, jnp.where(upward(), other, pltpu.roll(other, 8, 1)))


HALVES = [(a, q) for a in range(ARRAYS) for q in range(SLABS)]
DUOS = [HALVES[n : n + 2] for n in range(0, len(HALVES), 2)]
FAR = 2 * DEEP


def pack_duo(duo, get):
    return pack_halves(get(*duo[0]), get(*duo[1]) if len(duo) > 1 else None)


def faces_kernel(block, kappa, strip, x_face, y_face, y_kept):
    nz, ny, _ = kappa.shape

    def rows(t, carry):
        at = pl.ds(pl.multiple_of(t * 8, 8), 8)

        def plane(a, z):
            if z < 0 or z >= nz:
                return None
            return block[a, z, at] if a < COLS else kappa[z, at]

        held = {}
        for a, q in HALVES:
            held[a, q] = strip_of([plane(a, z - DEEP) for z in range(q, nz + FAR, SLABS)])
            strip[a, q, at] = held[a, q]
        for n, duo in enumerate(DUOS):
            x_face[n, at] = pack_duo(duo, lambda a, q: held[a, q])
        return carry

    lax.fori_loop(0, ny // 8, rows, 0, unroll=4)

    def slabs(z, carry):
        for a in range(ARRAYS):
            low, high = (block[a, z, at] if a < COLS else kappa[z, at] for at in (slice(0, 8), slice(ny - 8, ny)))
            y_face[a, z] = jnp.where(upward(), low, high)
            y_kept[a, z] = jnp.where(upward(), high, low)
        return carry

    lax.fori_loop(0, nz, slabs, 0, unroll=4)


def faces(block, kappa):
    nz, ny, nx = kappa.shape
    shapes = ((ARRAYS, SLABS, ny, nx), (len(DUOS), ny, nx), (ARRAYS, nz, 8, nx), (ARRAYS, nz, 8, nx))
    return pl.pallas_call(
        faces_kernel,
        out_shape=[jax.ShapeDtypeStruct(shape, F32) for shape in shapes],
        in_specs=[VMEM] * 2,
        out_specs=[VMEM] * 4,
        compiler_params=params(16),
        cost_estimate=cost(1 << 24),
        name="faces",
    )(block, kappa)


def far_y_kernel(f_low, f_high, s_low, s_high, after, face, kept):
    def slabs(i, carry):
        for a in range(ARRAYS):
            low = sides("gz", f_low[a, i], s_low[a, i])
            high = sides("gz", f_high[a, i], s_high[a, i])
            for at, which in ((i, 1), (DEEP + i, 0)):
                face[a, at] = jnp.where(upward(), low[which], high[which])
                kept[a, at] = jnp.where(upward(), high[which], low[which])
        return carry

    lax.fori_loop(0, DEEP, slabs, 0, unroll=2)


def far_y(first, second, after):
    _, _, ny, nx = first.shape
    last = ny // 8 - 1
    whole = lambda shape: pl.BlockSpec(shape, lambda i: (0,) * len(shape))
    edge = lambda at: pl.BlockSpec((ARRAYS, DEEP, 8, nx), lambda i: (0, 0, at, 0))
    shape = (ARRAYS, FAR, 8, nx)
    return pl.pallas_call(
        far_y_kernel,
        grid=(1,),
        out_shape=[jax.ShapeDtypeStruct(shape, F32)] * 2,
        in_specs=[edge(0), edge(last), edge(0), edge(last), pl.BlockSpec(memory_space=pl.ANY)],
        out_specs=[whole(shape)] * 2,
        compiler_params=params(16),
        name="far_y",
    )(first, first, second, second, after)


def far_strips_kernel(first, second, after, strip):
    def rows(t, carry):
        at = pl.ds(pl.multiple_of(t * 8, 8), 8)
        for a in range(ARRAYS):
            uppers, lowers = zip(*[sides("gz", first[a, i, at], second[a, i, at]) for i in range(DEEP)])
            strip[a, at] = strip_of(lowers + uppers)
        return carry

    lax.fori_loop(0, strip.shape[1] // 8, rows, 0, unroll=4)


def far_strips(first, second, after):
    _, _, ny, nx = first.shape
    return pl.pallas_call(
        far_strips_kernel,
        out_shape=jax.ShapeDtypeStruct((ARRAYS, ny, nx), F32),
        in_specs=[VMEM] * 2 + [pl.BlockSpec(memory_space=pl.ANY)],
        out_specs=VMEM,
        compiler_params=params(16),
        cost_estimate=cost(1 << 23),
        name="far_strips",
    )(first, second, after)


def far_pairs():
    return [(n, n + 1 if n + 1 < ARRAYS else None) for n in range(0, ARRAYS, 2)]


def pack_x_kernel(own_face, rim, far_strip, side, face, corner):
    nz = rim.shape[1]
    tiles = far_strip.shape[1] // 8

    def plane(a, z):
        return rim[a, z] if 0 <= z < nz else None

    def far_tile(a, t):
        return None if a is None else far_strip[a, tile(t)]

    for n in range(len(DUOS)):
        for t in range(tiles):
            face[n * tiles + t] = own_face[n, tile(t)]
    at = len(DUOS) * tiles
    for n, (one, other) in enumerate(far_pairs()):
        packed = [pack_halves(far_tile(one, t), far_tile(other, t)) for t in range(tiles)]
        for t in range(tiles):
            face[at + n * tiles + t] = packed[t]
        corner[n] = jnp.where(upward(), packed[0], packed[tiles - 1])
    at += len(far_pairs()) * tiles
    for a, q in HALVES:
        side[a, q] = strip_of([plane(a, z - DEEP) for z in range(q, nz + FAR, SLABS)])
    for n, duo in enumerate(DUOS):
        face[at + n] = pack_duo(duo, lambda a, q: side[a, q])


def pack_x(own_face, rim, far_strip):
    _, ny, nx = far_strip.shape
    count = (len(DUOS) + len(far_pairs())) * ny // 8 + len(DUOS)
    shapes = ((ARRAYS, SLABS, 8, nx), (count, 8, nx), (len(far_pairs()), 8, nx))
    return pl.pallas_call(
        pack_x_kernel,
        out_shape=[jax.ShapeDtypeStruct(shape, F32) for shape in shapes],
        in_specs=[VMEM] * 3,
        out_specs=[VMEM] * 3,
        compiler_params=params(16),
        name="pack_x",
    )(own_face, rim, far_strip)


def outer_kernel(block, kappa, edge, first, second, after, acc, f0, f1, f2, f3, kz, w, wz):
    nz, ny, _ = kappa.shape
    tiles = ny // 8
    half = sublanes(8) < 4
    acc[...] = jnp.zeros_like(acc)

    def far(i, carry):
        for a in range(ARRAYS):
            upper, lower = sides("gz", first[a, i], second[a, i])
            if a < COLS:
                f0[0, a, i] = lower
                f0[1, a, DEEP - 1 - i] = upper
            else:
                kz[0, i] = lower
                kz[1, DEEP - 1 - i] = upper
        return carry

    lax.fori_loop(0, DEEP, far, 0, unroll=4)
    for i in range(2):
        for c in range(COLS):
            f0[0, c, DEEP + i] = block[c, i]
            f0[1, c, DEEP + i] = block[c, nz - 1 - i]
            for k, f in enumerate((f1, f2, f3)):
                for side in range(2):
                    f[side, c, DEEP + i] = edge[k, side, i, c]
    for i in range(DEEP + 1):
        kz[0, DEEP + i] = kappa[i]
        kz[1, DEEP + i] = kappa[nz - 1 - i]

    def weights(at, carry):
        side, e = at // 8, at % 8
        for t in range(tiles):
            k = kz[side, e, tile(t)]
            right, left = pltpu.roll(k, 127, 1), pltpu.roll(k, 1, 1)
            above = rows_above(kz, (side, e), t, tiles, k)
            below = rows_below(kz, (side, e), t, k)
            far = kz[side, e + 1, tile(t)]
            near = kz[side, jnp.maximum(e - 1, 0), tile(t)]
            w[0, at, tile(t)] = centre(k, (right, left, above, below, far, near))
            w[1, at, tile(t)] = link(k, right, False)
            w[2, at, tile(t)] = link(k, left, False)
            w[3, at, tile(t)] = link(k, above, False)
            wz[at, tile(t)] = link(k, far, True)
        return carry

    lax.fori_loop(0, 16, weights, 0, unroll=8)
    fields = (f0, f1, f2, f3, None)
    for k in range(1, BASIS + 1):
        src, dst = fields[k - 1], fields[k]

        def both(side, carry, k=k, src=src, dst=dst):
            for j in range(DEEP):
                own = j >= DEEP - k
                sums = Sums()

                def step(t):
                    at = side * 8 + j + k
                    ws = tile_weights(w, at, wz, at, at - 1, t)
                    olds, news = [], []
                    for c in range(COLS):
                        v = src[side, c, j + 1, tile(t)]
                        above = rows_above(src, (side, c, j + 1), t, tiles, v)
                        below = rows_below(src, (side, c, j + 1), t, v)
                        far, near = src[side, c, j + 2, tile(t)], src[side, c, j, tile(t)]
                        news.append(apply(v, above, below, far, near, ws))
                        olds.append(v)
                    if dst is not None:
                        for c in range(COLS):
                            dst[side, c, j, tile(t)] = news[c]
                    return olds, news

                first, last = step(0), step(tiles - 1)
                if own:
                    olds, news = (
                        [jnp.where(half, b, a) for a, b in zip(first[i], last[i])] for i in range(2)
                    )
                    sums.products(k, olds, news)
                for t in range(1, tiles - 1):
                    pair = step(t)
                    if own:
                        sums.products(k, *pair)
                sums.flush(acc)
            return carry

        lax.fori_loop(0, 2, both, 0)


def outer(block, kappa, edge, first, second, after):
    nz, ny, nx = kappa.shape
    return pl.pallas_call(
        outer_kernel,
        out_shape=jax.ShapeDtypeStruct((MOMENTS * NPAIRS, 8, nx), F32),
        in_specs=[VMEM] * 5 + [pl.BlockSpec(memory_space=pl.ANY)],
        out_specs=VMEM,
        scratch_shapes=[pltpu.VMEM((2, COLS, DEEP + 2, ny, nx), F32)] * 4
        + [
            pltpu.VMEM((2, 2 * DEEP + 1, ny, nx), F32),
            pltpu.VMEM((4, 16, ny, nx), F32),
            pltpu.VMEM((16, ny, nx), F32),
        ],
        compiler_params=params(24),
        cost_estimate=cost(1 << 27),
        name="outer",
    )(block, kappa, edge, first, second, after)


def y_strip_kernel(kept, far_kept, rim, far_rim, acc, g0, g1, g2, g3, kr, w, wz):
    nz = rim.shape[1]
    depth = nz + FAR
    half = sublanes(8) < 4
    seam = [at_seam("gy") & (sublanes(8) == 7), at_seam("gy") & (sublanes(8) == 0)]
    acc[...] = jnp.zeros_like(acc)

    def lay(z, kept, rim, at):
        for a in range(ARRAYS):
            below = jnp.where(upward(), kept[a, at], rim[a, at])
            above = jnp.where(upward(), rim[a, at], kept[a, at])
            for t, part in enumerate((below, above)):
                if a < COLS:
                    g0[a, z, tile(t)] = part
                else:
                    kr[z, tile(t)] = part

    def fill(z, carry):
        lay(z + DEEP, kept, rim, z)
        return carry

    def fill_far(i, carry):
        lay(i, far_kept, far_rim, i)
        lay(nz + DEEP + i, far_kept, far_rim, DEEP + i)
        return carry

    lax.fori_loop(0, nz, fill, 0, unroll=4)
    lax.fori_loop(0, DEEP, fill_far, 0, unroll=2)

    def weights(z, carry):
        for t in range(2):
            k = kr[z, tile(t)]
            right, left = pltpu.roll(k, 127, 1), pltpu.roll(k, 1, 1)
            above = rows_above(kr, (z,), t, 2, k)
            below = rows_below(kr, (z,), t, k)
            above = cut(seam[0], above) if t == 0 else above
            below = cut(seam[1], below) if t == 1 else below
            far = kr[z + 1, tile(t)]
            near = kr[jnp.maximum(z - 1, 0), tile(t)]
            w[0, z, tile(t)] = centre(k, (right, left, above, below, far, near))
            w[1, z, tile(t)] = link(k, right, False)
            w[2, z, tile(t)] = link(k, left, False)
            w[3, z, tile(t)] = link(k, above, True)
            wz[z, tile(t)] = link(k, far, True)
        return carry

    lax.fori_loop(0, depth - 1, weights, 0, unroll=4)
    fields = (g0, g1, g2, g3, None)
    for k in range(1, BASIS + 1):
        src, dst = fields[k - 1], fields[k]

        def slab(z, own, k=k, src=src, dst=dst):
            sums = Sums()
            kept = []
            for t in range(2):
                ws = tile_weights(w, z, wz, z, z - 1, t)
                olds, news = [], []
                for c in range(COLS):
                    v = src[c, z, tile(t)]
                    above = rows_above(src, (c, z), t, 2, v)
                    below = rows_below(src, (c, z), t, v)
                    news.append(apply(v, above, below, src[c, z + 1, tile(t)], src[c, z - 1, tile(t)], ws))
                    olds.append(v)
                if dst is not None:
                    for c in range(COLS):
                        dst[c, z, tile(t)] = news[c]
                kept.append((olds, news))
            if own:
                olds, news = (
                    [jnp.where(half, b, a) for a, b in zip(kept[0][i], kept[1][i])] for i in range(2)
                )
                sums.products(k, olds, news)
                sums.flush(acc)

        def far(i, carry, k=k, slab=slab):
            slab(k + i, False)
            slab(depth - DEEP + i, False)
            return carry

        def own(z, carry, slab=slab):
            slab(z, True)
            return carry

        if k < DEEP:
            lax.fori_loop(0, DEEP - k, far, 0, unroll=True)
        lax.fori_loop(DEEP, depth - DEEP, own, 0, unroll=16)


def y_strip(kept, far_kept, rim, far_rim):
    _, nz, _, nx = rim.shape
    depth = nz + FAR
    return pl.pallas_call(
        y_strip_kernel,
        out_shape=jax.ShapeDtypeStruct((MOMENTS * NPAIRS, 8, nx), F32),
        in_specs=[VMEM] * 4,
        out_specs=VMEM,
        scratch_shapes=[pltpu.VMEM((COLS, depth, 16, nx), F32)] * 4
        + [
            pltpu.VMEM((depth, 16, nx), F32),
            pltpu.VMEM((4, depth, 16, nx), F32),
            pltpu.VMEM((depth, 16, nx), F32),
        ],
        compiler_params=params(16),
        cost_estimate=cost(1 << 30),
        name="y_strip",
    )(kept, far_kept, rim, far_rim)


def x_strip_kernel(strip, side, far_strip, far_rim, face, corner, acc1, acc2, acc3, out, s0, s1, s2, s3, kr, w, wz, acc):
    tiles = strip.shape[2] // 8 + 1
    lane = lanes(8)
    offset = lane % PITCH
    half = sublanes(8) < 4
    right_seam, left_seam = (at_seam("gx") & (offset == at) for at in (7, 8))
    above_seam, below_seam = (at_seam("gy") & (sublanes(8) == at) for at in (7, 0))
    shift = jnp.where(upward(), 0, 1)

    def next_slab(ref, index, q, at):
        if q < SLABS - 1:
            return ref[index + (q + 1, at)]
        return pltpu.roll(ref[index + (0, at)], 128 - PITCH, 1)

    def last_slab(ref, index, q, at):
        if q > 0:
            return ref[index + (q - 1, at)]
        return pltpu.roll(ref[index + (SLABS - 1, at)], PITCH, 1)

    own_side = (offset < 8) == upward()
    depth = 128 // PITCH * SLABS
    far_at = len(DUOS) * (tiles - 1)
    rim_at = far_at + len(far_pairs()) * (tiles - 1)
    far_side = [strip_of([far_rim[a, i] for i in range(FAR)]) for a in range(ARRAYS)]
    for n, (a, q) in enumerate(HALVES):
        z = lane // PITCH * SLABS + q
        far = (z < DEEP) | (z >= depth - DEEP)
        index = jnp.where(z < DEEP, z, jnp.where(far, z - (depth - FAR), 0)) * PITCH
        for t in range(tiles):
            own = strip[a, q, tile(t)] if t < tiles - 1 else side[a, q]
            beyond = face[n // 2 * (tiles - 1) + t] if t < tiles - 1 else face[rim_at + n // 2]
            if n % 2 == 0:
                beyond = jnp.where(upward(), pltpu.roll(beyond, 8, 1), beyond)
            else:
                beyond = jnp.where(upward(), beyond, pltpu.roll(beyond, 120, 1))
            far_own = far_strip[a, tile(t)] if t < tiles - 1 else far_side[a]
            far_beyond = face[far_at + a // 2 * (tiles - 1) + t] if t < tiles - 1 else corner[a // 2]
            far_own = permute_lanes(far_own, index + offset)
            far_beyond = permute_lanes(far_beyond, index + offset % 8 + 8 * (a % 2))
            value = jnp.where(own_side, jnp.where(far, far_own, own), jnp.where(far, far_beyond, beyond))
            at = t + shift if t < tiles - 1 else (tiles - 1) * (1 - shift)
            at = pl.ds(pl.multiple_of(at * 8, 8), 8)
            if a < COLS:
                s0[a, q, at] = value
            else:
                kr[q, at] = value

    for q in range(SLABS):
        for t in range(tiles):
            k = kr[q, tile(t)]
            right, left = cut(right_seam, pltpu.roll(k, 127, 1)), cut(left_seam, pltpu.roll(k, 1, 1))
            above = rows_above(kr, (q,), t, tiles, k)
            below = rows_below(kr, (q,), t, k)
            if t == 0 or t == tiles - 2:
                above = cut(above_seam & (upward() == (t > 0)), above)
            if t == 1 or t == tiles - 1:
                below = cut(below_seam & (upward() == (t > 1)), below)
            far, near = next_slab(kr, (), q, tile(t)), last_slab(kr, (), q, tile(t))
            w[0, q, tile(t)] = centre(k, (right, left, above, below, far, near))
            w[1, q, tile(t)] = link(k, right, True)
            w[2, q, tile(t)] = link(k, left, True)
            w[3, q, tile(t)] = link(k, above, True)
            wz[q + 1, tile(t)] = link(k, far, True)
            if q == 0:
                wz[0, tile(t)] = link(k, near, True)
    acc[...] = jnp.zeros_like(acc)
    fields = (s0, s1, s2, s3, None)
    for k in range(1, BASIS + 1):
        src, dst = fields[k - 1], fields[k]

        def slab(q):
            sums = Sums()

            def step(t):
                ws = tile_weights(w, q, wz, q + 1, q, t)
                olds, news = [], []
                for c in range(COLS):
                    v = src[c, q, tile(t)]
                    above = rows_above(src, (c, q), t, tiles, v)
                    below = rows_below(src, (c, q), t, v)
                    far, near = next_slab(src, (c,), q, tile(t)), last_slab(src, (c,), q, tile(t))
                    news.append(apply(v, above, below, far, near, ws))
                    olds.append(v)
                if dst is not None:
                    for c in range(COLS):
                        dst[c, q, tile(t)] = news[c]
                return olds, news

            first, last = step(0), step(tiles - 1)
            olds, news = (
                [jnp.where(half, b, a) for a, b in zip(first[i], last[i])] for i in range(2)
            )
            sums.products(k, olds, news)
            for t in range(1, tiles - 1):
                sums.products(k, *step(t))
            sums.flush(acc.at[q])

        for q in range(SLABS):
            slab(q)

    lane1 = lax.broadcasted_iota(jnp.int32, (1, 128), 1)
    z = lane1 // PITCH * SLABS
    here = (lane1 % PITCH >= DEEP) & (lane1 % PITCH < PITCH - DEEP)
    groups = 128 // PITCH
    total = jnp.where(
        (lane1 >= DEEP) & (lane1 < 128 - DEEP), jnp.sum(acc1[...] + acc2[...] + acc3[...], axis=1), 0.0
    )
    for q in range(SLABS):
        kept = here & (z + q >= DEEP) & (z + q < groups * SLABS - DEEP)
        total = total + jnp.where(kept, jnp.sum(acc[q], axis=1), 0.0)
    total = jnp.concatenate([total, jnp.zeros((128 - total.shape[0], 128), F32)], 0)
    row = lax.dot_general(
        jnp.ones((8, 128), F32),
        total,
        (((1,), (1,)), ((), ())),
        precision=lax.Precision.HIGHEST,
        preferred_element_type=F32,
    )
    out[...] = jnp.broadcast_to(row[0:1][None], out.shape)


def x_strip(strip, side, far_strip, far_rim, face, corner, accs, peers):
    _, slabs, ny, nx = strip.shape
    laid = (slabs, ny + 8, nx)
    return pl.pallas_call(
        x_strip_kernel,
        out_shape=jax.ShapeDtypeStruct((peers, 1, 128), F32),
        in_specs=[VMEM] * 9,
        out_specs=VMEM,
        scratch_shapes=[pltpu.VMEM((COLS,) + laid, F32)] * 4
        + [
            pltpu.VMEM(laid, F32),
            pltpu.VMEM((4,) + laid, F32),
            pltpu.VMEM((slabs + 1,) + laid[1:], F32),
            pltpu.VMEM((slabs, MOMENTS * NPAIRS, 8, nx), F32),
        ],
        compiler_params=params(16),
        name="x_strip",
    )(strip, side, far_strip, far_rim, face, corner, *accs)


def factor(row, triangle, coef):
    lane, sub = lanes(8), sublanes(8)
    blocks = (KRYLOV + 7) // 8
    columns = []
    for b in range(KRYLOV):
        parts = []
        for i in range(blocks):
            a = sub + 8 * i
            low, high = jnp.minimum(a % COLS, b % COLS), jnp.maximum(a % COLS, b % COLS)
            pair = low * COLS - (low * (low - 1)) // 2 + high - low
            index = jnp.where(a < KRYLOV, (a // COLS + b // COLS) * NPAIRS + pair, 127)
            parts.append(permute_lanes(row, index))
        columns.append(parts)
    at = 0
    for k in range(KRYLOV):
        i, j = k // 8, k % 8

        def entry(b):
            return jnp.broadcast_to(columns[b][i][j : j + 1], (8, 128))

        pivot = entry(k)
        inverse = 1.0 / pivot
        root = jnp.sqrt(pivot)
        scale = 1.0 / root
        line = jnp.where(lane == k, root, 0.0)
        if k < COLS:
            coef[at] = scale
            at += 1
        for b in range(k + 1, KRYLOV):
            value = entry(b)
            line = jnp.where(lane == b, value * scale, line)
            if b < COLS:
                coef[at] = value * scale
                at += 1
            value = value * inverse
            for n in range((k + 1) // 8, blocks):
                columns[b][n] = columns[b][n] - columns[k][n] * value
        triangle[k : k + 1, :] = line[0:1, 0:KRYLOV]


def finish_kernel(ncells, parts, block, ortho, triangle, coef):
    step = pl.program_id(0)

    @pl.when(step == 0)
    def _():
        row = jnp.sum(parts[...], axis=0) * (1.0 / ncells)
        factor(jnp.broadcast_to(row, (8, 128)), triangle, coef)

    u = {}
    for i in range(COLS):
        for j in range(i, COLS):
            u[i, j] = coef[len(u)]
    slabs = ortho.shape[1]

    def slab(z, carry):
        for t in range(ortho.shape[2] // 8):
            done = []
            for j in range(COLS):
                value = block[j, step * slabs + z, tile(t)]
                for i in range(j):
                    value = value - u[i, j] * done[i]
                value = value * u[j, j]
                ortho[j, z, tile(t)] = value
                done.append(value)
        return carry

    lax.fori_loop(0, slabs, slab, 0, unroll=2)


def finish(parts, block, ncells):
    cols, nz, ny, nx = block.shape
    steps = 2
    piece = pl.BlockSpec((cols, nz // steps, ny, nx), lambda i: (0, i, 0, 0))
    return pl.pallas_call(
        lambda *refs: finish_kernel(ncells, *refs),
        grid=(steps,),
        out_shape=[
            jax.ShapeDtypeStruct(block.shape, F32),
            jax.ShapeDtypeStruct((KRYLOV, KRYLOV), F32),
        ],
        in_specs=[pl.BlockSpec(parts.shape, lambda i: (0, 0, 0)), VMEM],
        out_specs=[piece, pl.BlockSpec((KRYLOV, KRYLOV), lambda i: (0, 0))],
        scratch_shapes=[pltpu.VMEM((NPAIRS, 8, 128), F32)],
        compiler_params=params(16),
        name="finish",
    )(parts, block)


def shards(block, kappa):
    axes = ("gx", "gy", "gz")
    peers = lax.axis_size(axes)
    ncells = float(kappa.size * peers)
    far = [pltpu.with_memory_space_constraint(value, pltpu.HBM) for value in (block, kappa)]
    first, second = swap(*pack_z(*far), "gz")
    strip, x_face, y_face, y_kept = faces(block, kappa)
    rim = pull(y_face, "gy")
    acc1, edge = inner(block, kappa)
    far_face, far_kept = far_y(first, second, acc1)
    far_rim = pull(far_face, "gy")
    far_strip = far_strips(first, second, far_kept)
    side, x_face, corner = pack_x(x_face, rim, far_strip)
    x_face, corner = pull(x_face, "gx"), pull(corner, "gx", "gy")
    acc2 = outer(block, kappa, edge, first, second, side)
    acc3 = y_strip(y_kept, far_kept, rim, far_rim)
    accs = (acc1, acc2, acc3)
    moments = x_strip(strip, side, far_strip, far_rim, x_face, corner, accs, peers)
    parts = lax.all_to_all(moments, axes, 0, 0, tiled=True)
    return tuple(finish(parts, block, ncells))


def solution(mesh):
    return jax.shard_map(
        shards,
        mesh=mesh,
        in_specs=(P(None, "gz", "gy", "gx"), P("gz", "gy", "gx")),
        out_specs=(P(None, "gz", "gy", "gx"), P()),
        check_vma=False,
    )
```

```python
import jax
import jax.numpy as jnp
import numpy as np
from jax import lax
from jax.experimental import pallas as pl
from jax.experimental.pallas import tpu as pltpu
from jax.sharding import PartitionSpec as P

COLS = 4
BASIS = 4
KRYLOV = 20
MOMENTS = 2 * BASIS + 1
PAIRS = [(c, d) for c in range(COLS) for d in range(c, COLS)]
NPAIRS = len(PAIRS)
DEEP = BASIS
ARRAYS = COLS + 1
PITCH = 4 * DEEP
SLABS = 3

basis_shift = 6.0
basis_scale = 3.0

F32 = jnp.float32
VMEM = pl.BlockSpec(memory_space=pltpu.VMEM)
HBM = pl.BlockSpec(memory_space=pltpu.HBM)


def params(mib):
    return pltpu.CompilerParams(vmem_limit_bytes=mib * 1024 * 1024)


def cost(flops):
    return pl.CostEstimate(flops=flops, bytes_accessed=1 << 20, transcendentals=0)


def lanes(rows):
    return lax.broadcasted_iota(jnp.int32, (rows, 128), 1)


def sublanes(rows):
    return lax.broadcasted_iota(jnp.int32, (rows, 128), 0)


def permute_lanes(value, index):
    return jnp.take_along_axis(value, index, axis=1, mode="promise_in_bounds")


def even_first(axis, first, second):
    return jnp.where(lax.axis_index(axis) % 2 == 0, first, second)


def sides(axis, first, second):
    at = lax.axis_index(axis)
    upper = jnp.where(at == lax.axis_size(axis) - 1, 0.0, even_first(axis, first, second))
    lower = jnp.where(at == 0, 0.0, even_first(axis, second, first))
    return upper, lower


def swap(first, second, axis):
    peers = lax.axis_size(axis)
    other = [(i, (i - 1 if i % 2 == 0 else i + 1) % peers) for i in range(peers)]
    second = lax.ppermute(second, axis, other)
    first = lax.ppermute(first, axis, [(i, i ^ 1) for i in range(peers)])
    return first, second


def upward():
    return lax.axis_index("gz") % 2 == 0


def pull(face, *axes):
    sizes = [lax.axis_size(axis) for axis in axes] + [lax.axis_size("gz")]
    pairs = []
    for at in np.ndindex(*sizes):
        step = -1 if at[-1] % 2 == 0 else 1
        to = [(i + step) % size for i, size in zip(at[:-1], sizes)] + [at[-1]]
        pairs.append(tuple(int(np.ravel_multi_index(place, sizes)) for place in (at, to)))
    return lax.ppermute(face, (*axes, "gz"), pairs)


def at_seam(axis):
    at = lax.axis_index(axis)
    return at == jnp.where(upward(), lax.axis_size(axis) - 1, 0)


def cut(there, value):
    return jnp.where(there, 0.0, value)


def link(one, other, bounded):
    weight = (one + other) * (0.5 / basis_scale)
    if bounded:
        weight = jnp.where(jnp.minimum(one, other) > 0.0, weight, 0.0)
    return weight


def centre(k, others):
    total = 6.0 * k
    for other in others:
        total = total + other
    return total * (0.5 / basis_scale) - basis_shift / basis_scale


def rows_above(ref, index, t, tiles, value):
    if t == tiles - 1:
        return pltpu.roll(value, 7, 0)
    return ref[index + (slice(8 * t + 1, 8 * t + 9),)]


def rows_below(ref, index, t, value):
    if t == 0:
        return pltpu.roll(value, 1, 0)
    return ref[index + (slice(8 * t - 1, 8 * t + 7),)]


def tile(t):
    return slice(8 * t, 8 * t + 8)


class Sums:
    def __init__(self):
        self.held = {}

    def add(self, at, term):
        self.held[at] = self.held[at] + term if at in self.held else term

    def products(self, k, olds, news):
        for p, (c, d) in enumerate(PAIRS):
            if k == 1:
                self.add(p, olds[c] * olds[d])
            self.add((2 * k - 1) * NPAIRS + p, olds[c] * news[d])
            self.add(2 * k * NPAIRS + p, news[c] * news[d])

    def flush(self, acc):
        for at, total in self.held.items():
            acc[at] += total


def apply(v, above, below, far, near, w):
    new = w[0] * v
    new -= w[1] * pltpu.roll(v, 127, 1)
    new -= w[2] * pltpu.roll(v, 1, 1)
    new -= w[3] * above
    new -= w[4] * below
    new -= w[5] * far
    new -= w[6] * near
    return new


def tile_weights(w, q, wz, far, near, t):
    c0, right, left, above = (w[i, q, tile(t)] for i in range(4))
    below = rows_below(w, (3, q), t, above)
    return c0, right, left, above, below, wz[far, tile(t)], wz[near, tile(t)]


def pack_z_kernel(block, kappa, to_first, to_second, sems):
    nz = kappa.shape[0]
    high = nz - DEEP
    even = lax.axis_index("gz") % 2 == 0
    copies = []
    for i, (out, at) in enumerate(
        ((to_second, jnp.where(even, 0, high)), (to_first, jnp.where(even, high, 0)))
    ):
        copies.append(pltpu.make_async_copy(block.at[:, pl.ds(at, DEEP)], out.at[0:COLS], sems.at[2 * i]))
        copies.append(pltpu.make_async_copy(kappa.at[pl.ds(at, DEEP)], out.at[COLS], sems.at[2 * i + 1]))
    for copy in copies:
        copy.start()
    for copy in copies:
        copy.wait()


def pack_z(block, kappa):
    nz, ny, nx = kappa.shape
    face = jax.ShapeDtypeStruct((ARRAYS, DEEP, ny, nx), F32)
    return pl.pallas_call(
        pack_z_kernel,
        out_shape=[face, face],
        in_specs=[HBM, HBM],
        out_specs=[VMEM] * 2,
        scratch_shapes=[pltpu.SemaphoreType.DMA((4,))],
        compiler_params=params(8),
        name="pack_z",
    )(block, kappa)


def inner_kernel(block, kappa, acc, edge, p1, p2, p3, w, wz):
    nz, ny, _ = kappa.shape
    tiles = ny // 8
    half = sublanes(8) < 4
    acc[...] = jnp.zeros_like(acc)

    def weights(z, carry):
        for t in range(tiles):
            k = kappa[z, tile(t)]
            right, left = pltpu.roll(k, 127, 1), pltpu.roll(k, 1, 1)
            above = rows_above(kappa, (z,), t, tiles, k)
            below = rows_below(kappa, (z,), t, k)
            far = kappa[z + 1, tile(t)]
            near = kappa[jnp.maximum(z - 1, 0), tile(t)]
            w[0, z, tile(t)] = centre(k, (right, left, above, below, far, near))
            w[1, z, tile(t)] = link(k, right, False)
            w[2, z, tile(t)] = link(k, left, False)
            w[3, z, tile(t)] = link(k, above, False)
            wz[z, tile(t)] = link(k, far, False)
        return carry

    lax.fori_loop(0, nz - 1, weights, 0, unroll=5)
    fields = (block, p1, p2, p3, None)
    for k in range(1, BASIS + 1):
        src, dst = fields[k - 1], fields[k]

        def slab(z, carry, k=k, src=src, dst=dst):
            sums = Sums()

            def step(t):
                ws = tile_weights(w, z, wz, z, z - 1, t)
                olds, news = [], []
                for c in range(COLS):
                    v = src[c, z, tile(t)]
                    above = rows_above(src, (c, z), t, tiles, v)
                    below = rows_below(src, (c, z), t, v)
                    news.append(apply(v, above, below, src[c, z + 1, tile(t)], src[c, z - 1, tile(t)], ws))
                    olds.append(v)
                if dst is not None:
                    for c in range(COLS):
                        dst[c, z, tile(t)] = news[c]
                return olds, news

            first, last = step(0), step(tiles - 1)
            olds, news = (
                [jnp.where(half, b, a) for a, b in zip(first[i], last[i])] for i in range(2)
            )
            sums.products(k, olds, news)
            for t in range(1, tiles - 1):
                sums.products(k, *step(t))
            sums.flush(acc)
            return carry

        lax.fori_loop(k, nz - k, slab, 0, unroll=(nz - 2 * k + 1) // 2)
        if dst is not None:
            for i in range(2):
                edge[k - 1, 0, i] = dst[:, k + i]
                edge[k - 1, 1, i] = dst[:, nz - 1 - k - i]


def inner(block, kappa):
    nz, ny, nx = kappa.shape
    return pl.pallas_call(
        inner_kernel,
        out_shape=[
            jax.ShapeDtypeStruct((MOMENTS * NPAIRS, 8, nx), F32),
            jax.ShapeDtypeStruct((BASIS - 1, 2, 2, COLS, ny, nx), F32),
        ],
        in_specs=[VMEM] * 2,
        out_specs=[VMEM] * 2,
        scratch_shapes=[pltpu.VMEM(block.shape, F32)] * 3
        + [pltpu.VMEM((4, nz, ny, nx), F32), pltpu.VMEM((nz, ny, nx), F32)],
        compiler_params=params(24),
        cost_estimate=cost(1 << 28),
        name="inner",
    )(block, kappa)


def strip_of(planes):
    lane = lanes(8)
    offset, group = lane % PITCH, lane // PITCH
    index = jnp.where(offset < 8, 120 + offset, offset - 8)
    strip = None
    for g, plane in enumerate(planes):
        if plane is not None:
            value = permute_lanes(plane, index)
            strip = value if strip is None else jnp.where(group == g, value, strip)
    return strip


def pack_halves(one, other):
    value = jnp.where(upward(), pltpu.roll(one, 120, 1), one)
    if other is None:
        return value
    low = lanes(8) % PITCH < 8
    return jnp.where(low, value, jnp.where(upward(), other, pltpu.roll(other, 8, 1)))


HALVES = [(a, q) for a in range(ARRAYS) for q in range(SLABS)]
DUOS = [HALVES[n : n + 2] for n in range(0, len(HALVES), 2)]
FAR = 2 * DEEP


def pack_duo(duo, get):
    return pack_halves(get(*duo[0]), get(*duo[1]) if len(duo) > 1 else None)


def faces_kernel(block, kappa, strip, x_face, y_face, y_kept):
    nz, ny, _ = kappa.shape

    def rows(t, carry):
        at = pl.ds(pl.multiple_of(t * 8, 8), 8)

        def plane(a, z):
            if z < 0 or z >= nz:
                return None
            return block[a, z, at] if a < COLS else kappa[z, at]

        held = {}
        for a, q in HALVES:
            held[a, q] = strip_of([plane(a, z - DEEP) for z in range(q, nz + FAR, SLABS)])
            strip[a, q, at] = held[a, q]
        for n, duo in enumerate(DUOS):
            x_face[n, at] = pack_duo(duo, lambda a, q: held[a, q])
        return carry

    lax.fori_loop(0, ny // 8, rows, 0, unroll=4)

    def slabs(z, carry):
        for a in range(ARRAYS):
            low, high = (block[a, z, at] if a < COLS else kappa[z, at] for at in (slice(0, 8), slice(ny - 8, ny)))
            y_face[a, z] = jnp.where(upward(), low, high)
            y_kept[a, z] = jnp.where(upward(), high, low)
        return carry

    lax.fori_loop(0, nz, slabs, 0, unroll=4)


def faces(block, kappa):
    nz, ny, nx = kappa.shape
    shapes = ((ARRAYS, SLABS, ny, nx), (len(DUOS), ny, nx), (ARRAYS, nz, 8, nx), (ARRAYS, nz, 8, nx))
    return pl.pallas_call(
        faces_kernel,
        out_shape=[jax.ShapeDtypeStruct(shape, F32) for shape in shapes],
        in_specs=[VMEM] * 2,
        out_specs=[VMEM] * 4,
        compiler_params=params(16),
        cost_estimate=cost(1 << 24),
        name="faces",
    )(block, kappa)


def far_y_kernel(f_low, f_high, s_low, s_high, after, face, kept):
    def slabs(i, carry):
        for a in range(ARRAYS):
            low = sides("gz", f_low[a, i], s_low[a, i])
            high = sides("gz", f_high[a, i], s_high[a, i])
            for at, which in ((i, 1), (DEEP + i, 0)):
                face[a, at] = jnp.where(upward(), low[which], high[which])
                kept[a, at] = jnp.where(upward(), high[which], low[which])
        return carry

    lax.fori_loop(0, DEEP, slabs, 0, unroll=2)


def far_y(first, second, after):
    _, _, ny, nx = first.shape
    last = ny // 8 - 1
    whole = lambda shape: pl.BlockSpec(shape, lambda i: (0,) * len(shape))
    edge = lambda at: pl.BlockSpec((ARRAYS, DEEP, 8, nx), lambda i: (0, 0, at, 0))
    shape = (ARRAYS, FAR, 8, nx)
    return pl.pallas_call(
        far_y_kernel,
        grid=(1,),
        out_shape=[jax.ShapeDtypeStruct(shape, F32)] * 2,
        in_specs=[edge(0), edge(last), edge(0), edge(last), pl.BlockSpec(memory_space=pl.ANY)],
        out_specs=[whole(shape)] * 2,
        compiler_params=params(16),
        name="far_y",
    )(first, first, second, second, after)


def far_strips_kernel(first, second, after, strip):
    def rows(t, carry):
        at = pl.ds(pl.multiple_of(t * 8, 8), 8)
        for a in range(ARRAYS):
            uppers, lowers = zip(*[sides("gz", first[a, i, at], second[a, i, at]) for i in range(DEEP)])
            strip[a, at] = strip_of(lowers + uppers)
        return carry

    lax.fori_loop(0, strip.shape[1] // 8, rows, 0, unroll=4)


def far_strips(first, second, after):
    _, _, ny, nx = first.shape
    return pl.pallas_call(
        far_strips_kernel,
        out_shape=jax.ShapeDtypeStruct((ARRAYS, ny, nx), F32),
        in_specs=[VMEM] * 2 + [pl.BlockSpec(memory_space=pl.ANY)],
        out_specs=VMEM,
        compiler_params=params(16),
        cost_estimate=cost(1 << 23),
        name="far_strips",
    )(first, second, after)


def far_pairs():
    return [(n, n + 1 if n + 1 < ARRAYS else None) for n in range(0, ARRAYS, 2)]


def pack_x_kernel(own_face, rim, far_strip, side, face, corner):
    nz = rim.shape[1]
    tiles = far_strip.shape[1] // 8

    def plane(a, z):
        return rim[a, z] if 0 <= z < nz else None

    def far_tile(a, t):
        return None if a is None else far_strip[a, tile(t)]

    for n in range(len(DUOS)):
        for t in range(tiles):
            face[n * tiles + t] = own_face[n, tile(t)]
    at = len(DUOS) * tiles
    for n, (one, other) in enumerate(far_pairs()):
        packed = [pack_halves(far_tile(one, t), far_tile(other, t)) for t in range(tiles)]
        for t in range(tiles):
            face[at + n * tiles + t] = packed[t]
        corner[n] = jnp.where(upward(), packed[0], packed[tiles - 1])
    at += len(far_pairs()) * tiles
    for a, q in HALVES:
        side[a, q] = strip_of([plane(a, z - DEEP) for z in range(q, nz + FAR, SLABS)])
    for n, duo in enumerate(DUOS):
        face[at + n] = pack_duo(duo, lambda a, q: side[a, q])


def pack_x(own_face, rim, far_strip):
    _, ny, nx = far_strip.shape
    count = (len(DUOS) + len(far_pairs())) * ny // 8 + len(DUOS)
    shapes = ((ARRAYS, SLABS, 8, nx), (count, 8, nx), (len(far_pairs()), 8, nx))
    return pl.pallas_call(
        pack_x_kernel,
        out_shape=[jax.ShapeDtypeStruct(shape, F32) for shape in shapes],
        in_specs=[VMEM] * 3,
        out_specs=[VMEM] * 3,
        compiler_params=params(16),
        name="pack_x",
    )(own_face, rim, far_strip)


def outer_kernel(block, kappa, edge, first, second, start, after, acc, f0, f1, f2, f3, kz, w, wz):
    nz, ny, _ = kappa.shape
    tiles = ny // 8
    half = sublanes(8) < 4
    acc[...] = start[...]

    def far(i, carry):
        for a in range(ARRAYS):
            upper, lower = sides("gz", first[a, i], second[a, i])
            if a < COLS:
                f0[0, a, i] = lower
                f0[1, a, DEEP - 1 - i] = upper
            else:
                kz[0, i] = lower
                kz[1, DEEP - 1 - i] = upper
        return carry

    lax.fori_loop(0, DEEP, far, 0, unroll=4)
    for i in range(2):
        for c in range(COLS):
            f0[0, c, DEEP + i] = block[c, i]
            f0[1, c, DEEP + i] = block[c, nz - 1 - i]
            for k, f in enumerate((f1, f2, f3)):
                for side in range(2):
                    f[side, c, DEEP + i] = edge[k, side, i, c]
    for i in range(DEEP + 1):
        kz[0, DEEP + i] = kappa[i]
        kz[1, DEEP + i] = kappa[nz - 1 - i]

    def weights(at, carry):
        side, e = at // 8, at % 8
        for t in range(tiles):
            k = kz[side, e, tile(t)]
            right, left = pltpu.roll(k, 127, 1), pltpu.roll(k, 1, 1)
            above = rows_above(kz, (side, e), t, tiles, k)
            below = rows_below(kz, (side, e), t, k)
            far = kz[side, e + 1, tile(t)]
            near = kz[side, jnp.maximum(e - 1, 0), tile(t)]
            w[0, at, tile(t)] = centre(k, (right, left, above, below, far, near))
            w[1, at, tile(t)] = link(k, right, False)
            w[2, at, tile(t)] = link(k, left, False)
            w[3, at, tile(t)] = link(k, above, False)
            wz[at, tile(t)] = link(k, far, True)
        return carry

    lax.fori_loop(0, 16, weights, 0, unroll=8)
    fields = (f0, f1, f2, f3, None)
    for k in range(1, BASIS + 1):
        src, dst = fields[k - 1], fields[k]

        def both(side, carry, k=k, src=src, dst=dst):
            for j in range(DEEP):
                own = j >= DEEP - k
                sums = Sums()

                def step(t):
                    at = side * 8 + j + k
                    ws = tile_weights(w, at, wz, at, at - 1, t)
                    olds, news = [], []
                    for c in range(COLS):
                        v = src[side, c, j + 1, tile(t)]
                        above = rows_above(src, (side, c, j + 1), t, tiles, v)
                        below = rows_below(src, (side, c, j + 1), t, v)
                        far, near = src[side, c, j + 2, tile(t)], src[side, c, j, tile(t)]
                        news.append(apply(v, above, below, far, near, ws))
                        olds.append(v)
                    if dst is not None:
                        for c in range(COLS):
                            dst[side, c, j, tile(t)] = news[c]
                    return olds, news

                first, last = step(0), step(tiles - 1)
                if own:
                    olds, news = (
                        [jnp.where(half, b, a) for a, b in zip(first[i], last[i])] for i in range(2)
                    )
                    sums.products(k, olds, news)
                for t in range(1, tiles - 1):
                    pair = step(t)
                    if own:
                        sums.products(k, *pair)
                sums.flush(acc)
            return carry

        lax.fori_loop(0, 2, both, 0)


def outer(block, kappa, edge, first, second, start, after):
    nz, ny, nx = kappa.shape
    return pl.pallas_call(
        outer_kernel,
        out_shape=jax.ShapeDtypeStruct((MOMENTS * NPAIRS, 8, nx), F32),
        in_specs=[VMEM] * 6 + [pl.BlockSpec(memory_space=pl.ANY)],
        out_specs=VMEM,
        scratch_shapes=[pltpu.VMEM((2, COLS, DEEP + 2, ny, nx), F32)] * 4
        + [
            pltpu.VMEM((2, 2 * DEEP + 1, ny, nx), F32),
            pltpu.VMEM((4, 16, ny, nx), F32),
            pltpu.VMEM((16, ny, nx), F32),
        ],
        compiler_params=params(24),
        cost_estimate=cost(1 << 27),
        name="outer",
    )(block, kappa, edge, first, second, start, after)


def y_strip_kernel(kept, far_kept, rim, far_rim, acc, g0, g1, g2, g3, kr, w, wz):
    nz = rim.shape[1]
    depth = nz + FAR
    half = sublanes(8) < 4
    seam = [at_seam("gy") & (sublanes(8) == 7), at_seam("gy") & (sublanes(8) == 0)]
    acc[...] = jnp.zeros_like(acc)

    def lay(z, kept, rim, at):
        for a in range(ARRAYS):
            below = jnp.where(upward(), kept[a, at], rim[a, at])
            above = jnp.where(upward(), rim[a, at], kept[a, at])
            for t, part in enumerate((below, above)):
                if a < COLS:
                    g0[a, z, tile(t)] = part
                else:
                    kr[z, tile(t)] = part

    def fill(z, carry):
        lay(z + DEEP, kept, rim, z)
        return carry

    def fill_far(i, carry):
        lay(i, far_kept, far_rim, i)
        lay(nz + DEEP + i, far_kept, far_rim, DEEP + i)
        return carry

    lax.fori_loop(0, nz, fill, 0, unroll=4)
    lax.fori_loop(0, DEEP, fill_far, 0, unroll=2)

    def weights(z, carry):
        for t in range(2):
            k = kr[z, tile(t)]
            right, left = pltpu.roll(k, 127, 1), pltpu.roll(k, 1, 1)
            above = rows_above(kr, (z,), t, 2, k)
            below = rows_below(kr, (z,), t, k)
            above = cut(seam[0], above) if t == 0 else above
            below = cut(seam[1], below) if t == 1 else below
            far = kr[z + 1, tile(t)]
            near = kr[jnp.maximum(z - 1, 0), tile(t)]
            w[0, z, tile(t)] = centre(k, (right, left, above, below, far, near))
            w[1, z, tile(t)] = link(k, right, False)
            w[2, z, tile(t)] = link(k, left, False)
            w[3, z, tile(t)] = link(k, above, True)
            wz[z, tile(t)] = link(k, far, True)
        return carry

    lax.fori_loop(0, depth - 1, weights, 0, unroll=4)
    fields = (g0, g1, g2, g3, None)
    for k in range(1, BASIS + 1):
        src, dst = fields[k - 1], fields[k]

        def slab(z, own, k=k, src=src, dst=dst):
            sums = Sums()
            kept = []
            for t in range(2):
                ws = tile_weights(w, z, wz, z, z - 1, t)
                olds, news = [], []
                for c in range(COLS):
                    v = src[c, z, tile(t)]
                    above = rows_above(src, (c, z), t, 2, v)
                    below = rows_below(src, (c, z), t, v)
                    news.append(apply(v, above, below, src[c, z + 1, tile(t)], src[c, z - 1, tile(t)], ws))
                    olds.append(v)
                if dst is not None:
                    for c in range(COLS):
                        dst[c, z, tile(t)] = news[c]
                kept.append((olds, news))
            if own:
                olds, news = (
                    [jnp.where(half, b, a) for a, b in zip(kept[0][i], kept[1][i])] for i in range(2)
                )
                sums.products(k, olds, news)
                sums.flush(acc)

        def far(i, carry, k=k, slab=slab):
            slab(k + i, False)
            slab(depth - DEEP + i, False)
            return carry

        def own(z, carry, slab=slab):
            slab(z, True)
            return carry

        if k < DEEP:
            lax.fori_loop(0, DEEP - k, far, 0, unroll=True)
        lax.fori_loop(DEEP, depth - DEEP, own, 0, unroll=16)


def y_strip(kept, far_kept, rim, far_rim):
    _, nz, _, nx = rim.shape
    depth = nz + FAR
    return pl.pallas_call(
        y_strip_kernel,
        out_shape=jax.ShapeDtypeStruct((MOMENTS * NPAIRS, 8, nx), F32),
        in_specs=[VMEM] * 4,
        out_specs=VMEM,
        scratch_shapes=[pltpu.VMEM((COLS, depth, 16, nx), F32)] * 4
        + [
            pltpu.VMEM((depth, 16, nx), F32),
            pltpu.VMEM((4, depth, 16, nx), F32),
            pltpu.VMEM((depth, 16, nx), F32),
        ],
        compiler_params=params(16),
        cost_estimate=cost(1 << 30),
        name="y_strip",
    )(kept, far_kept, rim, far_rim)


def x_strip_kernel(strip, side, far_strip, far_rim, face, corner, acc1, acc2, out, s0, s1, s2, s3, kr, w, wz, acc):
    tiles = strip.shape[2] // 8 + 1
    lane = lanes(8)
    offset = lane % PITCH
    half = sublanes(8) < 4
    right_seam, left_seam = (at_seam("gx") & (offset == at) for at in (7, 8))
    above_seam, below_seam = (at_seam("gy") & (sublanes(8) == at) for at in (7, 0))
    shift = jnp.where(upward(), 0, 1)

    def next_slab(ref, index, q, at):
        if q < SLABS - 1:
            return ref[index + (q + 1, at)]
        return pltpu.roll(ref[index + (0, at)], 128 - PITCH, 1)

    def last_slab(ref, index, q, at):
        if q > 0:
            return ref[index + (q - 1, at)]
        return pltpu.roll(ref[index + (SLABS - 1, at)], PITCH, 1)

    own_side = (offset < 8) == upward()
    depth = 128 // PITCH * SLABS
    far_at = len(DUOS) * (tiles - 1)
    rim_at = far_at + len(far_pairs()) * (tiles - 1)
    far_side = [strip_of([far_rim[a, i] for i in range(FAR)]) for a in range(ARRAYS)]
    for n, (a, q) in enumerate(HALVES):
        z = lane // PITCH * SLABS + q
        far = (z < DEEP) | (z >= depth - DEEP)
        index = jnp.where(z < DEEP, z, jnp.where(far, z - (depth - FAR), 0)) * PITCH
        for t in range(tiles):
            own = strip[a, q, tile(t)] if t < tiles - 1 else side[a, q]
            beyond = face[n // 2 * (tiles - 1) + t] if t < tiles - 1 else face[rim_at + n // 2]
            if n % 2 == 0:
                beyond = jnp.where(upward(), pltpu.roll(beyond, 8, 1), beyond)
            else:
                beyond = jnp.where(upward(), beyond, pltpu.roll(beyond, 120, 1))
            far_own = far_strip[a, tile(t)] if t < tiles - 1 else far_side[a]
            far_beyond = face[far_at + a // 2 * (tiles - 1) + t] if t < tiles - 1 else corner[a // 2]
            far_own = permute_lanes(far_own, index + offset)
            far_beyond = permute_lanes(far_beyond, index + offset % 8 + 8 * (a % 2))
            value = jnp.where(own_side, jnp.where(far, far_own, own), jnp.where(far, far_beyond, beyond))
            at = t + shift if t < tiles - 1 else (tiles - 1) * (1 - shift)
            at = pl.ds(pl.multiple_of(at * 8, 8), 8)
            if a < COLS:
                s0[a, q, at] = value
            else:
                kr[q, at] = value

    for q in range(SLABS):
        for t in range(tiles):
            k = kr[q, tile(t)]
            right, left = cut(right_seam, pltpu.roll(k, 127, 1)), cut(left_seam, pltpu.roll(k, 1, 1))
            above = rows_above(kr, (q,), t, tiles, k)
            below = rows_below(kr, (q,), t, k)
            if t == 0 or t == tiles - 2:
                above = cut(above_seam & (upward() == (t > 0)), above)
            if t == 1 or t == tiles - 1:
                below = cut(below_seam & (upward() == (t > 1)), below)
            far, near = next_slab(kr, (), q, tile(t)), last_slab(kr, (), q, tile(t))
            w[0, q, tile(t)] = centre(k, (right, left, above, below, far, near))
            w[1, q, tile(t)] = link(k, right, True)
            w[2, q, tile(t)] = link(k, left, True)
            w[3, q, tile(t)] = link(k, above, True)
            wz[q + 1, tile(t)] = link(k, far, True)
            if q == 0:
                wz[0, tile(t)] = link(k, near, True)
    acc[...] = jnp.zeros_like(acc)
    fields = (s0, s1, s2, s3, None)
    for k in range(1, BASIS + 1):
        src, dst = fields[k - 1], fields[k]

        def slab(q):
            sums = Sums()

            def step(t):
                ws = tile_weights(w, q, wz, q + 1, q, t)
                olds, news = [], []
                for c in range(COLS):
                    v = src[c, q, tile(t)]
                    above = rows_above(src, (c, q), t, tiles, v)
                    below = rows_below(src, (c, q), t, v)
                    far, near = next_slab(src, (c,), q, tile(t)), last_slab(src, (c,), q, tile(t))
                    news.append(apply(v, above, below, far, near, ws))
                    olds.append(v)
                if dst is not None:
                    for c in range(COLS):
                        dst[c, q, tile(t)] = news[c]
                return olds, news

            first, last = step(0), step(tiles - 1)
            olds, news = (
                [jnp.where(half, b, a) for a, b in zip(first[i], last[i])] for i in range(2)
            )
            sums.products(k, olds, news)
            for t in range(1, tiles - 1):
                sums.products(k, *step(t))
            sums.flush(acc.at[q])

        for q in range(SLABS):
            slab(q)

    lane1 = lax.broadcasted_iota(jnp.int32, (1, 128), 1)
    z = lane1 // PITCH * SLABS
    here = (lane1 % PITCH >= DEEP) & (lane1 % PITCH < PITCH - DEEP)
    groups = 128 // PITCH
    total = jnp.where(
        (lane1 >= DEEP) & (lane1 < 128 - DEEP), jnp.sum(acc1[...] + acc2[...], axis=1), 0.0
    )
    for q in range(SLABS):
        kept = here & (z + q >= DEEP) & (z + q < groups * SLABS - DEEP)
        total = total + jnp.where(kept, jnp.sum(acc[q], axis=1), 0.0)
    total = jnp.concatenate([total, jnp.zeros((128 - total.shape[0], 128), F32)], 0)
    row = lax.dot_general(
        jnp.ones((8, 128), F32),
        total,
        (((1,), (1,)), ((), ())),
        precision=lax.Precision.HIGHEST,
        preferred_element_type=F32,
    )
    out[...] = jnp.broadcast_to(row[0:1][None], out.shape)


def x_strip(strip, side, far_strip, far_rim, face, corner, accs, peers):
    _, slabs, ny, nx = strip.shape
    laid = (slabs, ny + 8, nx)
    return pl.pallas_call(
        x_strip_kernel,
        out_shape=jax.ShapeDtypeStruct((peers, 1, 128), F32),
        in_specs=[VMEM] * 8,
        out_specs=VMEM,
        scratch_shapes=[pltpu.VMEM((COLS,) + laid, F32)] * 4
        + [
            pltpu.VMEM(laid, F32),
            pltpu.VMEM((4,) + laid, F32),
            pltpu.VMEM((slabs + 1,) + laid[1:], F32),
            pltpu.VMEM((slabs, MOMENTS * NPAIRS, 8, nx), F32),
        ],
        compiler_params=params(16),
        name="x_strip",
    )(strip, side, far_strip, far_rim, face, corner, *accs)


def factor(row, triangle, coef):
    lane, sub = lanes(8), sublanes(8)
    blocks = (KRYLOV + 7) // 8
    columns = []
    for b in range(KRYLOV):
        parts = []
        for i in range(blocks):
            a = sub + 8 * i
            low, high = jnp.minimum(a % COLS, b % COLS), jnp.maximum(a % COLS, b % COLS)
            pair = low * COLS - (low * (low - 1)) // 2 + high - low
            index = jnp.where(a < KRYLOV, (a // COLS + b // COLS) * NPAIRS + pair, 127)
            parts.append(permute_lanes(row, index))
        columns.append(parts)
    at = 0
    for k in range(KRYLOV):
        i, j = k // 8, k % 8

        def entry(b):
            return jnp.broadcast_to(columns[b][i][j : j + 1], (8, 128))

        pivot = entry(k)
        inverse = 1.0 / pivot
        root = jnp.sqrt(pivot)
        scale = 1.0 / root
        line = jnp.where(lane == k, root, 0.0)
        if k < COLS:
            coef[at] = scale
            at += 1
        for b in range(k + 1, KRYLOV):
            value = entry(b)
            line = jnp.where(lane == b, value * scale, line)
            if b < COLS:
                coef[at] = value * scale
                at += 1
            value = value * inverse
            for n in range((k + 1) // 8, blocks):
                columns[b][n] = columns[b][n] - columns[k][n] * value
        triangle[k : k + 1, :] = line[0:1, 0:KRYLOV]


def finish_kernel(ncells, parts, block, ortho, triangle, coef):
    step = pl.program_id(0)

    @pl.when(step == 0)
    def _():
        row = jnp.sum(parts[...], axis=0) * (1.0 / ncells)
        factor(jnp.broadcast_to(row, (8, 128)), triangle, coef)

    u = {}
    for i in range(COLS):
        for j in range(i, COLS):
            u[i, j] = coef[len(u)]
    slabs = ortho.shape[1]

    def slab(z, carry):
        for t in range(ortho.shape[2] // 8):
            done = []
            for j in range(COLS):
                value = block[j, step * slabs + z, tile(t)]
                for i in range(j):
                    value = value - u[i, j] * done[i]
                value = value * u[j, j]
                ortho[j, z, tile(t)] = value
                done.append(value)
        return carry

    lax.fori_loop(0, slabs, slab, 0, unroll=2)


def finish(parts, block, ncells):
    cols, nz, ny, nx = block.shape
    steps = 2
    piece = pl.BlockSpec((cols, nz // steps, ny, nx), lambda i: (0, i, 0, 0))
    return pl.pallas_call(
        lambda *refs: finish_kernel(ncells, *refs),
        grid=(steps,),
        out_shape=[
            jax.ShapeDtypeStruct(block.shape, F32),
            jax.ShapeDtypeStruct((KRYLOV, KRYLOV), F32),
        ],
        in_specs=[pl.BlockSpec(parts.shape, lambda i: (0, 0, 0)), VMEM],
        out_specs=[piece, pl.BlockSpec((KRYLOV, KRYLOV), lambda i: (0, 0))],
        scratch_shapes=[pltpu.VMEM((NPAIRS, 8, 128), F32)],
        compiler_params=params(16),
        name="finish",
    )(parts, block)


def shards(block, kappa):
    axes = ("gx", "gy", "gz")
    peers = lax.axis_size(axes)
    ncells = float(kappa.size * peers)
    far = [pltpu.with_memory_space_constraint(value, pltpu.HBM) for value in (block, kappa)]
    first, second = swap(*pack_z(*far), "gz")
    strip, x_face, y_face, y_kept = faces(block, kappa)
    rim = pull(y_face, "gy")
    acc1, edge = inner(block, kappa)
    far_face, far_kept = far_y(first, second, acc1)
    far_rim = pull(far_face, "gy")
    far_strip = far_strips(first, second, far_kept)
    side, x_face, corner = pack_x(x_face, rim, far_strip)
    x_face, corner = pull(x_face, "gx"), pull(corner, "gx", "gy")
    acc2 = outer(block, kappa, edge, first, second, acc1, side)
    acc3 = y_strip(y_kept, far_kept, rim, far_rim)
    accs = (acc2, acc3)
    moments = x_strip(strip, side, far_strip, far_rim, x_face, corner, accs, peers)
    parts = lax.all_to_all(moments, axes, 0, 0, tiled=True)
    return tuple(finish(parts, block, ncells))


def solution(mesh):
    return jax.shard_map(
        shards,
        mesh=mesh,
        in_specs=(P(None, "gz", "gy", "gx"), P("gz", "gy", "gx")),
        out_specs=(P(None, "gz", "gy", "gx"), P()),
        check_vma=False,
    )
```
